32 devices in a mesh: section: 2 (over core), slab: 16 (over z, y, x).
Axes of the slice: x: 2, y: 2, z: 4, core: 2. Of those that a mesh axis runs over, the one named last changes fastest.
Arguments:
- tokens: bfloat16 [2, 96, 180, 768], P(None, 'slab'), may hold values from -6 to 6
- cotangent: bfloat16 [2, 96, 180, 768], P(None, 'slab'), may hold values from -6 to 6
- gain_one: bfloat16 [2, 768], P('section'), may hold values from 0.5 to 1.5
- shift_one: bfloat16 [2, 768], P('section'), may hold values from -2 to 2
- spectral_one: bfloat16 [2, 2, 8, 96, 96], P('section'), may hold values from -0.4375 to 0.4375
- spectral_bias_one: bfloat16 [2, 2, 8, 96], P('section'), may hold values from -2 to 2
- spectral_two: bfloat16 [2, 2, 8, 96, 96], P('section'), may hold values from -0.4375 to 0.4375
- spectral_bias_two: bfloat16 [2, 2, 8, 96], P('section'), may hold values from -2 to 2
- gain_two: bfloat16 [2, 768], P('section'), may hold values from 0.5 to 1.5
- shift_two: bfloat16 [2, 768], P('section'), may hold values from -2 to 2
- dense_in: bfloat16 [2, 768, 3072], P('section'), may hold values from -0.21875 to 0.21875
- dense_in_bias: bfloat16 [2, 3072], P('section'), may hold values from -2 to 2
- dense_out: bfloat16 [2, 3072, 768], P('section'), may hold values from -0.109375 to 0.109375
- dense_out_bias: bfloat16 [2, 768], P('section'), may hold values from -2 to 2
Outputs:
- activations: bfloat16 [2, 2, 96, 180, 768], P('section', None, 'slab')
- input_grads: bfloat16 [2, 2, 96, 180, 768], P('section', None, 'slab')
- grad_gain_one: float32 [2, 768], P('section')
- grad_shift_one: float32 [2, 768], P('section')
- grad_spectral_one: float32 [2, 2, 8, 96, 96], P('section')
- grad_spectral_bias_one: float32 [2, 2, 8, 96], P('section')
- grad_spectral_two: float32 [2, 2, 8, 96, 96], P('section')
- grad_spectral_bias_two: float32 [2, 2, 8, 96], P('section')
- grad_gain_two: float32 [2, 768], P('section')
- grad_shift_two: float32 [2, 768], P('section')
- grad_dense_in: float32 [2, 768, 3072], P('section')
- grad_dense_in_bias: float32 [2, 3072], P('section')
- grad_dense_out: float32 [2, 3072, 768], P('section')
- grad_dense_out_bias: float32 [2, 768], P('section')
The draws below stay inside these ranges and needn't reach their ends.
All inputs are finite; a program needn't handle non-finite values.
Results may differ from the reference program's by a relative error of at most 0.015.
Values may be sent and summed in bfloat16 or wider, within the bound.
No kernel may reach another device: no remote copies, remote signals or barrier semaphores. Data moves between devices by JAX's collectives and lax.ppermute only.
A program may use at most 384 MiB of HBM per device.

```python
import jax
import jax.numpy as jnp
from jax import lax

D = 768
FF = 3072
BLOCKS = 8
LAT = 90
LON = 180
LAYERS = 2
MB = 2
BLOCK = 96
ROWS = 96
FIELDS = 1


def level_of(stream_key, extent, cuts, least, high):
    def one(axis_at, parts):
        heights = jax.random.uniform(jax.random.fold_in(jax.random.fold_in(stream_key, 6), axis_at), (parts,), jnp.float32, least / len(cuts), high / len(cuts))
        return jnp.repeat(jnp.exp(heights), extent[axis_at] // parts).reshape((-1,) + (1,) * (len(extent) - axis_at - 1))

    level = one(*cuts[0])
    for cut in cuts[1:]:
        level = level * one(*cut)
    return level


def scatter_about(rng, dims, width, bound, split=(), held_as=jnp.bfloat16):
    drawn = jax.random.normal(rng, dims, jnp.float32) * width
    if len(split) > 0:
        drawn = level_of(rng, dims, split, -0.22, 0.18) * drawn
    return jnp.clip(drawn, min=-bound, max=bound).astype(held_as)


def setup_inputs(seed: int = 0) -> dict:
    streams_of = jax.random.split(jax.random.key(seed), 15)
    tokens = scatter_about(streams_of[0], (MB, ROWS, LON, D), 1.0, 6.0, ((1, 16),))
    cotangent = scatter_about(streams_of[1], (MB, ROWS, LON, D), 1.0, 6.0, ((1, 16),))
    gain_one = jnp.clip(1.0 + 0.1 * jax.random.normal(streams_of[2], (LAYERS, D), jnp.float32), 0.5, 1.5).astype(jnp.bfloat16)
    shift_one = scatter_about(streams_of[3], (LAYERS, D), 0.3, 2.0, ((0, 2),))
    spectral_one = scatter_about(streams_of[4], (LAYERS, 2, BLOCKS, BLOCK, BLOCK), (2 * BLOCK) ** -0.5, 0.4375, ((0, 2),))
    spectral_bias_one = scatter_about(streams_of[5], (LAYERS, 2, BLOCKS, BLOCK), 0.3, 2.0, ((0, 2),))
    spectral_two = scatter_about(streams_of[6], (LAYERS, 2, BLOCKS, BLOCK, BLOCK), (2 * BLOCK) ** -0.5, 0.4375, ((0, 2),))
    spectral_bias_two = scatter_about(streams_of[7], (LAYERS, 2, BLOCKS, BLOCK), 0.3, 2.0, ((0, 2),))
    gain_two = jnp.clip(1.0 + 0.1 * jax.random.normal(streams_of[8], (LAYERS, D), jnp.float32), 0.5, 1.5).astype(jnp.bfloat16)
    shift_two = scatter_about(streams_of[9], (LAYERS, D), 0.3, 2.0, ((0, 2),))
    dense_in = scatter_about(streams_of[10], (LAYERS, D, FF), D ** -0.5, 0.21875, ((0, 2),))
    dense_in_bias = scatter_about(streams_of[11], (LAYERS, FF), 0.3, 2.0, ((0, 2),))
    dense_out = scatter_about(streams_of[12], (LAYERS, FF, D), FF ** -0.5, 0.109375, ((0, 2),))
    dense_out_bias = scatter_about(streams_of[13], (LAYERS, D), 0.3, 2.0, ((0, 2),))
    return dict(tokens=tokens, cotangent=cotangent, gain_one=gain_one, shift_one=shift_one, spectral_one=spectral_one, spectral_bias_one=spectral_bias_one, spectral_two=spectral_two, spectral_bias_two=spectral_bias_two, gain_two=gain_two, shift_two=shift_two, dense_in=dense_in, dense_in_bias=dense_in_bias, dense_out=dense_out, dense_out_bias=dense_out_bias)


EPSILON = 1e-05
SHRINK = 0.01
SOFTNESS = 0.1
HIGHEST = lax.Precision.HIGHEST

@jax.custom_vjp
def low(v):
    return lax.optimization_barrier(v.astype(jnp.bfloat16)).astype(jnp.float32)

@jax.custom_vjp
def low_back(v):
    return v

def low_keep(v):
    return (low(v), None)

def low_pass(kept, grad):
    return (grad,)

def back_keep(v):
    return (v, None)

def back_low(kept, grad):
    return (low(grad),)
low.defvjp(low_keep, low_pass)
low_back.defvjp(back_keep, back_low)

def layer_norm(values, gain, shift):
    center = values - lax.optimization_barrier(jnp.mean(values, axis=-1, keepdims=True))
    spread = lax.optimization_barrier(jnp.mean(center * center, axis=-1, keepdims=True))
    return center * lax.rsqrt(spread + EPSILON) * gain + shift

def smooth_gelu(values):
    return jax.nn.gelu(values, approximate=False)

def mix_blocks(real_part, imag_part, weight, bias):
    real_real = jnp.einsum('...bi,bij->...bj', real_part, weight[0], precision=HIGHEST)
    imag_imag = jnp.einsum('...bi,bij->...bj', imag_part, weight[1], precision=HIGHEST)
    real_imag = jnp.einsum('...bi,bij->...bj', real_part, weight[1], precision=HIGHEST)
    imag_real = jnp.einsum('...bi,bij->...bj', imag_part, weight[0], precision=HIGHEST)
    return (real_real - imag_imag + bias[0], real_imag + imag_real + bias[1])

def afno_layer(values, params):
    gain_one, shift_one, spectral_one, spectral_bias_one, spectral_two, spectral_bias_two, gain_two, shift_two, dense_in, dense_in_bias, dense_out, dense_out_bias = params
    normed = layer_norm(values, gain_one, shift_one)
    spectrum = jnp.fft.rfft(normed, axis=2, norm='ortho')
    sent_real = low(low_back(jnp.real(spectrum)))
    sent_imag = low(low_back(jnp.imag(spectrum)))
    modes = jnp.fft.fft(lax.complex(sent_real, sent_imag), axis=1, norm='ortho')
    blocked = modes.shape[:-1] + (BLOCKS, BLOCK)
    mode_real = low(jnp.real(modes)).reshape(blocked)
    mode_imag = low(jnp.imag(modes)).reshape(blocked)
    first_real, first_imag = mix_blocks(mode_real, mode_imag, spectral_one, spectral_bias_one)
    first_real = low_back(first_real)
    first_imag = low_back(first_imag)
    active_real = low(smooth_gelu(first_real))
    active_imag = low(smooth_gelu(first_imag))
    second_real, second_imag = mix_blocks(active_real, active_imag, spectral_two, spectral_bias_two)
    second_real = low_back(second_real)
    second_imag = low_back(second_imag)
    shrunk_real = (second_real - SHRINK * jnp.tanh(second_real / SOFTNESS)).reshape(modes.shape)
    shrunk_imag = (second_imag - SHRINK * jnp.tanh(second_imag / SOFTNESS)).reshape(modes.shape)
    restored = jnp.fft.ifft(lax.complex(shrunk_real, shrunk_imag), axis=1, norm='ortho')
    back_real = low(low_back(jnp.real(restored)))
    back_imag = low(low_back(jnp.imag(restored)))
    filtered = jnp.fft.irfft(lax.complex(back_real, back_imag), n=LON, axis=2, norm='ortho')
    mixed = filtered + normed + values
    second_norm = low(layer_norm(mixed, gain_two, shift_two))
    hidden = low_back(jnp.einsum('...d,df->...f', second_norm, dense_in, precision=HIGHEST) + dense_in_bias)
    activated = low(smooth_gelu(hidden))
    output = jnp.einsum('...f,fd->...d', activated, dense_out, precision=HIGHEST) + dense_out_bias + mixed
    return low(low_back(output))

def reference(tokens, cotangent, gain_one, shift_one, spectral_one, spectral_bias_one, spectral_two, spectral_bias_two, gain_two, shift_two, dense_in, dense_in_bias, dense_out, dense_out_bias):
    weights = (gain_one, shift_one, spectral_one, spectral_bias_one, spectral_two, spectral_bias_two, gain_two, shift_two, dense_in, dense_in_bias, dense_out, dense_out_bias)
    live = FIELDS * LAT

    def as_fields(array):
        return array[:, :live].astype(jnp.float32).reshape(MB * FIELDS, LAT, LON, D)

    def as_rows(array):
        shaped = array.reshape(MB, live, LON, D)
        return jnp.pad(shaped, ((0, 0), (0, ROWS - live), (0, 0), (0, 0)))
    first_params = tuple((item[0].astype(jnp.float32) for item in weights))
    second_params = tuple((item[1].astype(jnp.float32) for item in weights))
    first_out, first_pull = jax.vjp(afno_layer, as_fields(tokens), first_params)
    second_out, second_pull = jax.vjp(afno_layer, first_out, second_params)
    middle_grad, second_grads = second_pull(as_fields(cotangent))
    entry_grad, first_grads = first_pull(middle_grad)
    activations = jnp.stack([as_rows(first_out), as_rows(second_out)]).astype(jnp.bfloat16)
    input_grads = jnp.stack([as_rows(entry_grad), as_rows(middle_grad)]).astype(jnp.bfloat16)
    grads = tuple((jnp.stack([earlier, later]) for earlier, later in zip(first_grads, second_grads)))
    return (activations, input_grads, grads[0], grads[1], grads[2], grads[3], grads[4], grads[5], grads[6], grads[7], grads[8], grads[9], grads[10], grads[11])
```

```python
import math

import jax
import jax.numpy as jnp
from jax import lax
from jax.sharding import Mesh, PartitionSpec as P

BLOCKS = 8
LAT = 90
EPSILON = 1e-05
SHRINK = 0.01
SOFTNESS = 0.1
HIGHEST = lax.Precision.HIGHEST
ROWS_AXES = ("section", "lane")
ALL = ("section", "half", "lane")
SLAB = ("half", "lane")
F32 = jnp.float32
BF16 = jnp.bfloat16


def layer_norm(values, gain, shift):
    center = values - jnp.mean(values, axis=-1, keepdims=True)
    spread = jnp.mean(center * center, axis=-1, keepdims=True)
    return center * lax.rsqrt(spread + EPSILON) * gain + shift


def smooth_gelu(values):
    return jax.nn.gelu(values, approximate=False)


def longitude_tables(longitudes, padded):
    column = jnp.arange(longitudes, dtype=jnp.int32)[:, None]
    frequency = jnp.arange(padded, dtype=jnp.int32)[None, :]
    angle = (column * frequency % longitudes).astype(F32) * (2.0 * math.pi / longitudes)
    usable = (frequency <= longitudes // 2).astype(F32) / math.sqrt(longitudes)
    forward = jnp.stack([jnp.cos(angle) * usable, -jnp.sin(angle) * usable], axis=-1)
    doubled = jnp.where((frequency == 0) | (frequency == longitudes // 2), 1.0, 2.0).astype(F32)
    inverse = jnp.transpose(forward * doubled[:, :, None], (1, 2, 0))
    return (forward, inverse)


def latitude_table(latitudes):
    frequency = jnp.arange(latitudes, dtype=jnp.int32)[:, None]
    position = jnp.arange(latitudes, dtype=jnp.int32)[None, :]
    angle = (frequency * position % latitudes).astype(F32) * (2.0 * math.pi / latitudes)
    cosine = jnp.cos(angle) / math.sqrt(latitudes)
    sine = jnp.sin(angle) / math.sqrt(latitudes)
    return jnp.stack([jnp.stack([cosine, sine], axis=-1), jnp.stack([-sine, cosine], axis=-1)], axis=1)


def latitude_forward(rows_first, layout):
    live = layout["live"]
    used = rows_first[:live].reshape((live // LAT, LAT) + rows_first.shape[1:])
    return jnp.einsum("kdrc,frmce->fkmde", layout["latitude"], used, precision=HIGHEST)


def latitude_inverse(spectral, layout):
    back = jnp.einsum("kdrc,fkmde->frmce", layout["latitude"], spectral, precision=HIGHEST)
    back = back.reshape((-1,) + back.shape[2:])
    return jnp.pad(back, ((0, layout["rows"] - back.shape[0]), (0, 0), (0, 0), (0, 0)))


def block_matrix(weight):
    upper = jnp.stack([weight[0], weight[1]], axis=2)
    lower = jnp.stack([-weight[1], weight[0]], axis=2)
    return jnp.stack([upper, lower], axis=1)


def mix_forward(inputs, matrix, bias):
    product = jnp.einsum("xmcbi,bcidj->xmdbj", inputs, matrix, preferred_element_type=F32)
    return product + bias.astype(F32)


def mix_backward(inputs, grad_output, matrix):
    grad_input = jnp.einsum("xmdbj,bcidj->xmcbi", grad_output, matrix, preferred_element_type=F32)
    outer = jnp.einsum("xmcbi,xmdbj->bcidj", inputs, grad_output, preferred_element_type=F32)
    grad_weight = jnp.stack(
        [outer[:, 0, :, 0] + outer[:, 1, :, 1], outer[:, 0, :, 1] - outer[:, 1, :, 0]]
    )
    grad_bias = jnp.sum(grad_output.astype(F32), axis=(0, 1))
    return (grad_input, grad_weight, grad_bias)


def to_modes(spectrum, layout):
    rows, modes, _, width = spectrum.shape
    lanes, per = layout["lanes"], layout["per"]
    parts = spectrum.astype(BF16).reshape(rows, lanes, per, 2, 2, width // 2)
    parts = jnp.transpose(parts, (4, 1, 0, 2, 3, 5)).reshape(2 * lanes, rows * per, width)
    moved = lax.all_to_all(parts, ROWS_AXES, 0, 0, tiled=True)
    return moved.reshape(2 * lanes * rows, per, 2, width // 2)


def to_rows(modes, layout):
    total, per, _, half_width = modes.shape
    lanes = layout["lanes"]
    rows = total // (2 * lanes)
    parts = modes.astype(BF16).reshape(2 * lanes, rows * per, 2 * half_width)
    moved = lax.all_to_all(parts, ROWS_AXES, 0, 0, tiled=True)
    moved = moved.reshape(2, lanes, rows, per, 2, half_width)
    return jnp.transpose(moved, (2, 1, 3, 4, 0, 5)).reshape(rows, lanes * per, 2, 2 * half_width)


def layer_forward(values, weights, layout):
    normed = layer_norm(values, weights[0].astype(F32), weights[1].astype(F32))
    spectrum = jnp.einsum("rnd,nkc->rkcd", normed, layout["forward"], precision=HIGHEST)
    received = to_modes(spectrum, layout)
    mode_low = latitude_forward(received.astype(F32), layout).astype(BF16).reshape(layout["view"])
    first = mix_forward(mode_low, weights[2], weights[3])
    active = smooth_gelu(first).astype(BF16)
    second = mix_forward(active, weights[4], weights[5])
    shrunk = (second - SHRINK * jnp.tanh(second / SOFTNESS)) * layout["modes"]
    back = to_rows(latitude_inverse(shrunk.reshape(layout["spectral"]), layout), layout)
    filtered = jnp.einsum("rkcd,kcn->rnd", back.astype(F32), layout["inverse"], precision=HIGHEST)
    mixed = (filtered + normed + values).reshape(-1, values.shape[-1])
    second_norm = layer_norm(mixed, weights[6].astype(F32), weights[7].astype(F32)).astype(BF16)
    hidden = jnp.dot(second_norm, weights[8], preferred_element_type=F32) + weights[9].astype(F32)
    activated = smooth_gelu(hidden).astype(BF16)
    output = jnp.dot(activated, weights[10], preferred_element_type=F32)
    output = (output + weights[11].astype(F32) + mixed).reshape(values.shape)
    output = (output * layout["live_rows"]).astype(BF16)
    return output, (values, mode_low, first, active, second, mixed, second_norm, hidden, activated)


def layer_backward(saved, grad_out, weights, layout):
    values, mode_low, first, active, second, mixed, second_norm, hidden, activated = saved
    width = values.shape[-1]
    grad_flat = grad_out.reshape(-1, width)
    gelu_pull = jax.vjp(smooth_gelu, hidden)[1]
    grad_activated = jnp.einsum("td,fd->tf", grad_flat, weights[10], preferred_element_type=F32)
    grad_hidden = gelu_pull(grad_activated)[0].astype(BF16)
    grad_second_norm = jnp.einsum("tf,df->td", grad_hidden, weights[8], preferred_element_type=F32)
    norm_pull = jax.vjp(layer_norm, mixed, weights[6].astype(F32), weights[7].astype(F32))[1]
    grad_mixed, grad_gain_two, grad_shift_two = norm_pull(grad_second_norm)
    grad_mixed = (grad_mixed + grad_flat.astype(F32)).reshape(values.shape)
    grad_returned = jnp.einsum("rnd,kcn->rkcd", grad_mixed, layout["inverse"], precision=HIGHEST)
    grad_modes = to_modes(grad_returned, layout)
    grad_dense_out = jnp.einsum("tf,td->fd", activated, grad_flat, preferred_element_type=F32)
    grad_dense_out_bias = jnp.sum(grad_flat.astype(F32), axis=0)
    grad_dense_in = jnp.einsum("td,tf->df", second_norm, grad_hidden, preferred_element_type=F32)
    grad_dense_in_bias = jnp.sum(grad_hidden.astype(F32), axis=0)
    grad_shrunk = latitude_forward(grad_modes.astype(F32), layout).reshape(layout["view"])
    grad_shrunk = grad_shrunk * layout["modes"]
    slope = jnp.tanh(second / SOFTNESS)
    grad_second = (grad_shrunk * (1.0 - SHRINK / SOFTNESS * (1.0 - slope * slope))).astype(BF16)
    grad_active, grad_two, grad_bias_two = mix_backward(active, grad_second, weights[4])
    grad_first = jax.vjp(smooth_gelu, first)[1](grad_active)[0].astype(BF16)
    grad_mode, grad_one, grad_bias_one = mix_backward(mode_low, grad_first, weights[2])
    back = to_rows(latitude_inverse(grad_mode.reshape(layout["spectral"]), layout), layout)
    front_pull = jax.vjp(layer_norm, values, weights[0].astype(F32), weights[1].astype(F32))[1]
    grad_normed = jnp.einsum("rkcd,nkc->rnd", back.astype(F32), layout["forward"], precision=HIGHEST)
    grad_values, grad_gain_one, grad_shift_one = front_pull(grad_normed + grad_mixed)
    grad_values = grad_values + grad_mixed
    small = (grad_gain_one, grad_shift_one, grad_gain_two, grad_shift_two, grad_dense_in_bias, grad_dense_out_bias)
    return grad_values.astype(BF16), small, (grad_one, grad_two), (grad_bias_one, grad_bias_two), (grad_dense_in, grad_dense_out)


def both_layers(item, core):
    other = lax.ppermute(item, "section", [(0, 1), (1, 0)])
    return (jnp.where(core == 0, item, other), jnp.where(core == 0, other, item))


def fetch(pair, core, half):
    own = lax.dynamic_index_in_dim(pair, half, 0, keepdims=False)
    give = lax.dynamic_index_in_dim(pair, 1 - half, 0, keepdims=False)
    got = lax.ppermute(give, ("section", "half"), [(0, 1), (3, 2)])
    return jnp.where(core == half, own, got)


def deliver(layer_zero, layer_one, core):
    parts = []
    for micro in range(2):
        first = lax.ppermute(layer_zero, ("section", "half"), [(micro, 0), (2 + micro, 1)])
        second = lax.ppermute(layer_one, ("section", "half"), [(micro, 2), (2 + micro, 3)])
        parts.append(jnp.where(core == 0, first, second))
    return jnp.stack(parts)[None]


def shards(tokens, cotangent, *params):
    core = lax.axis_index("section")
    half = lax.axis_index("half")
    lane = lax.axis_index("lane")
    lanes = lax.axis_size("lane")
    micro_count, local_rows, longitudes, width = tokens.shape
    total_rows = local_rows * lanes * 2
    fields = total_rows // LAT
    live = fields * LAT
    mode_count = longitudes // 2 + 1
    per = (mode_count + lanes - 1) // lanes
    forward_table, inverse_table = longitude_tables(longitudes, per * lanes)
    mode_ids = lane * per + jnp.arange(per, dtype=jnp.int32)
    row_ids = (core * lanes + lane) * local_rows + jnp.arange(local_rows, dtype=jnp.int32)
    row_mask = row_ids < live
    blocks = BLOCKS // 2
    layout = {
        "forward": forward_table,
        "inverse": inverse_table,
        "latitude": latitude_table(LAT),
        "live": live,
        "rows": total_rows,
        "lanes": lanes,
        "per": per,
        "modes": (mode_ids < mode_count).astype(F32).reshape(1, per, 1, 1, 1),
        "live_rows": row_mask.astype(F32).reshape(local_rows, 1, 1),
        "view": (fields * LAT, per, 2, blocks, width // BLOCKS),
        "spectral": (fields, LAT, per, 2, width // 2),
    }
    values = fetch(tokens, core, half)
    grad_out = fetch(cotangent, core, half)
    grad_out = jnp.where(row_mask.reshape(local_rows, 1, 1), grad_out, jnp.zeros_like(grad_out))
    pairs = [both_layers(item[0], core) for item in params]
    layers = []
    for level in range(2):
        w = [pair[level] for pair in pairs]
        for at in (2, 4):
            part = lax.dynamic_slice_in_dim(w[at], core * blocks, blocks, 1)
            w[at] = block_matrix(part)
        for at in (3, 5):
            w[at] = lax.dynamic_slice_in_dim(w[at], core * blocks, blocks, 1)
        layers.append(w)
    out_one, saved_one = layer_forward(values.astype(F32), layers[0], layout)
    out_two, saved_two = layer_forward(out_one.astype(F32), layers[1], layout)
    grad_two, small_two, spec_two, bias_two, dense_two = layer_backward(saved_two, grad_out, layers[1], layout)
    grad_one, small_one, spec_one, bias_one, dense_one = layer_backward(saved_one, grad_two, layers[0], layout)
    outputs = deliver(out_one, out_two, core)
    input_grads = deliver(grad_one, grad_two, core)

    def spread_bias(item):
        full = jnp.zeros((2, BLOCKS, width // BLOCKS), F32)
        return lax.dynamic_update_slice_in_dim(full, item, core * blocks, 1)

    small = [a.reshape(-1) for a in small_one] + [spread_bias(b).reshape(-1) for b in bias_one]
    small = small + [a.reshape(-1) for a in small_two] + [spread_bias(b).reshape(-1) for b in bias_two]
    sizes = [a.shape[0] for a in small]
    merged = lax.psum(jnp.concatenate(small), ALL)
    ends = [sum(sizes[: i + 1]) for i in range(len(sizes))]
    pieces = [merged[e - s : e] for e, s in zip(ends, sizes)]
    pieces = [jnp.where(core == 0, a, b)[None] for a, b in zip(pieces[:8], pieces[8:])]
    spec = lax.psum(jnp.stack([jnp.stack(spec_one), jnp.stack(spec_two)]), SLAB)
    given = lax.ppermute(jnp.where(core == 0, spec[1], spec[0]), "section", [(0, 1), (1, 0)])
    kept = jnp.where(core == 0, spec[0], spec[1])
    spec = jnp.where(core == 0, jnp.concatenate([kept, given], 2), jnp.concatenate([given, kept], 2))
    dense = []
    for at in range(2):
        a = lax.psum(dense_one[at].astype(BF16), ALL)
        b = lax.psum(dense_two[at].astype(BF16), ALL)
        dense.append(jnp.where(core == 0, a, b).astype(F32)[None])
    shape = (1, 2, BLOCKS, width // BLOCKS)
    return (
        outputs, input_grads, pieces[0], pieces[1], spec[0][None], pieces[6].reshape(shape),
        spec[1][None], pieces[7].reshape(shape), pieces[2], pieces[3], dense[0], pieces[4], dense[1], pieces[5],
    )


def solution(mesh):
    devices = mesh.devices
    slabs = devices.shape[1]
    wide = Mesh(devices.reshape(2, 2, slabs // 2), ALL)
    rows = P(None, ("half", "lane"))
    own = P("section")
    return jax.shard_map(
        shards,
        mesh=wide,
        in_specs=(rows, rows) + (own,) * 12,
        out_specs=(P("section", None, ("half", "lane")),) * 2 + (own,) * 12,
        check_vma=False,
    )
```

```python
import functools
import math

import jax
import jax.numpy as jnp
import numpy as np
from jax import lax
from jax.experimental import pallas as pl
from jax.experimental.pallas import tpu as pltpu
from jax.sharding import Mesh, PartitionSpec as P

BLOCKS = 8
LAT = 90
EPSILON = 1e-05
SHRINK = 0.01
SOFTNESS = 0.1
ROWS_AXES = ("section", "lane")
ALL = ("section", "half", "lane")
SLAB = ("half", "lane")
F32 = jnp.float32
BF16 = jnp.bfloat16
VMEM_BYTES = 56 * 1024 * 1024


def split_table(table):
    high = np.asarray(table, np.float32).astype(jnp.bfloat16)
    low = (np.asarray(table, np.float64) - high.astype(np.float64)).astype(jnp.bfloat16)
    return np.concatenate([high, low], 0)


def longitude_tables(longitudes, padded):
    column = np.arange(longitudes)[:, None]
    frequency = np.arange(padded)[None, :]
    angle = (column * frequency % longitudes) * (2.0 * math.pi / longitudes)
    usable = (frequency <= longitudes // 2) / math.sqrt(longitudes)
    forward = np.concatenate([np.cos(angle) * usable, -np.sin(angle) * usable], 1)
    doubled = np.where((frequency == 0) | (frequency == longitudes // 2), 1.0, 2.0)
    inverse = forward * np.concatenate([doubled, doubled], 1)
    return (forward, inverse)


def latitude_table(rows, fields):
    index = np.arange(LAT)
    angle = (index[:, None] * index[None, :] % LAT) * (2.0 * math.pi / LAT)
    parts = []
    for wave in (np.cos(angle), np.sin(angle)):
        whole = np.zeros((rows, rows))
        for field in range(fields):
            span = slice(field * LAT, (field + 1) * LAT)
            whole[span, span] = wave / math.sqrt(LAT)
        parts.append(whole)
    return np.concatenate(parts, 0)


def dot(left, right):
    return jnp.dot(left, right, preferred_element_type=F32)


def dot_transposed(left, right):
    return lax.dot_general(left, right, (((1,), (1,)), ((), ())), preferred_element_type=F32)


def table_times_low(table_ref, low):
    count = table_ref.shape[0] // 2
    return dot(table_ref[:count, :], low) + dot(table_ref[count:, :], low)


def table_times(table_ref, value):
    count = table_ref.shape[0] // 2
    high = value.astype(BF16)
    rest = (value - high.astype(F32)).astype(BF16)
    return dot(table_ref[:count, :], high) + dot(table_ref[:count, :], rest) + dot(table_ref[count:, :], high)


def gelu_pair(value):
    size = jnp.abs(value) * math.sqrt(0.5)
    inverse = 1.0 / (1.0 + 0.3275911 * size)
    wave = jnp.exp(-0.5 * value * value)
    series = inverse * (0.254829592 + inverse * (-0.284496736 + inverse * (1.421413741 + inverse * (-1.453152027 + inverse * 1.061405429))))
    tail = 0.5 * series * wave
    share = jnp.where(value > 0, 1.0 - tail, tail)
    return value * share, share + value * wave * (1.0 / math.sqrt(2.0 * math.pi))


def centered(value):
    center = value - jnp.mean(value, axis=-1, keepdims=True)
    inverse = lax.rsqrt(jnp.mean(center * center, axis=-1, keepdims=True) + EPSILON)
    return center * inverse, inverse


def norm_back(grad, gain, unit, inverse):
    scaled = grad * gain
    return (scaled - jnp.mean(scaled, axis=-1, keepdims=True) - unit * jnp.mean(scaled * unit, axis=-1, keepdims=True)) * inverse


def scatter_modes(sent, spectrum, row, rows, lanes, per):
    width = spectrum.shape[1]
    half = width // 2
    modes = lanes * per
    for part in range(2):
        for lane in range(lanes):
            base = ((part * lanes + lane) * rows + row) * per
            for wave in range(2):
                piece = spectrum[wave * modes + lane * per : wave * modes + (lane + 1) * per, part * half : (part + 1) * half]
                sent[base : base + per, wave * half : (wave + 1) * half] = piece


def gather_modes(spectrum, back, row, rows, lanes, per):
    width = spectrum.shape[1]
    half = width // 2
    modes = lanes * per
    for part in range(2):
        for lane in range(lanes):
            base = ((part * lanes + lane) * rows + row) * per
            for wave in range(2):
                piece = back[base : base + per, wave * half : (wave + 1) * half]
                spectrum[wave * modes + lane * per : wave * modes + (lane + 1) * per, part * half : (part + 1) * half] = piece


def front_kernel(x_ref, gain_ref, shift_ref, table_ref, sent_ref, x32, sent32, *, rows, lanes, per):
    x32[...] = x_ref[...].astype(F32)
    longs = x_ref.shape[0] // rows
    for row in range(rows):
        unit, _ = centered(x32[row * longs : (row + 1) * longs, :])
        spectrum = table_times(table_ref, unit * gain_ref[...] + shift_ref[...])
        scatter_modes(sent32, spectrum, row, rows, lanes, per)
    sent_ref[...] = sent32[...].astype(BF16)


def middle_kernel(back_ref, x_ref, gain_ref, shift_ref, gain_two_ref, shift_two_ref, table_ref, mixed_ref, norm_ref, x32, back32, spectrum, norm32, *, rows, lanes, per):
    x32[...] = x_ref[...].astype(F32)
    back32[...] = back_ref[...].astype(F32)
    longs = x_ref.shape[0] // rows
    for row in range(rows):
        span = slice(row * longs, (row + 1) * longs)
        gather_modes(spectrum, back32, row, rows, lanes, per)
        value = x32[span, :]
        unit, _ = centered(value)
        mixed = table_times_low(table_ref, spectrum[...].astype(BF16)) + (unit * gain_ref[...] + shift_ref[...]) + value
        mixed_ref[span, :] = mixed
        unit, _ = centered(mixed)
        norm32[span, :] = unit * gain_two_ref[...] + shift_two_ref[...]
    norm_ref[...] = norm32[...].astype(BF16)


def latitude_forward(table_ref, value, count):
    half = value.shape[1] // 2
    both = table_times_low(table_ref, value)
    cosine, sine = both[:count, :], both[count:, :]
    return cosine[:, :half] + sine[:, half:], cosine[:, half:] - sine[:, :half]


def latitude_inverse(table_ref, value, count):
    half = value.shape[1] // 2
    both = table_times(table_ref, value)
    cosine, sine = both[:count, :], both[count:, :]
    return cosine[:, :half] - sine[:, half:], cosine[:, half:] + sine[:, :half]


def strided_fill(apart, got_ref):
    total, width = got_ref.shape
    for tile in range(width // 128):
        apart[tile * total : (tile + 1) * total, :] = got_ref[:, tile * 128 : (tile + 1) * 128].astype(F32)


def strided_take(apart, mode, per, total, width):
    spans = [pl.ds(tile * total + mode, total // per, stride=per) for tile in range(width // 128)]
    return jnp.concatenate([apart[span, :] for span in spans], 1).astype(BF16)


def strided_put(apart, mode, per, total, first, value):
    for tile in range(value.shape[1] // 128):
        span = pl.ds((first + tile) * total + mode, total // per, stride=per)
        apart[span, :] = value[:, tile * 128 : (tile + 1) * 128]


def strided_send(sent_ref, apart):
    total, width = sent_ref.shape
    for tile in range(width // 128):
        sent_ref[:, tile * 128 : (tile + 1) * 128] = apart[tile * total : (tile + 1) * total, :].astype(BF16)


def chunk_of(total):
    return total // 3 if total % 48 == 0 else total


def spectral_kernel(got_ref, table_ref, one_ref, bias_one_ref, two_ref, bias_two_ref, sent_ref, low_ref, active_ref, slope_ref, factor_ref, got32, shrunk, *, per):
    total, width = got_ref.shape
    count, half = total // per, width // 2
    strided_fill(got32, got_ref)
    for mode in range(per):
        real, imag = latitude_forward(table_ref, strided_take(got32, mode, per, total, width), count)
        span = slice(mode * count, (mode + 1) * count)
        low_ref[span, :half] = real.astype(BF16)
        low_ref[span, half:] = imag.astype(BF16)
    chunk = chunk_of(total)

    @pl.loop(0, total // chunk)
    def _(step):
        span = pl.ds(pl.multiple_of(step * chunk, chunk), chunk)
        first = dot(low_ref[span, :], one_ref[...]) + bias_one_ref[...]
        active, slope = gelu_pair(first)
        active = active.astype(BF16)
        active_ref[span, :] = active
        slope_ref[span, :] = slope.astype(BF16)
        second = dot(active, two_ref[...]) + bias_two_ref[...]
        bend = jnp.tanh(second * (1.0 / SOFTNESS))
        shrunk[span, :] = second - SHRINK * bend
        factor_ref[span, :] = (1.0 - SHRINK / SOFTNESS * (1.0 - bend * bend)).astype(BF16)

    for mode in range(per):
        real, imag = latitude_inverse(table_ref, shrunk[mode * count : (mode + 1) * count, :], count)
        strided_put(got32, mode, per, total, 0, real)
        strided_put(got32, mode, per, total, half // 128, imag)
    strided_send(sent_ref, got32)


def spectral_back_kernel(got_ref, table_ref, one_ref, two_ref, slope_ref, factor_ref, sent_ref, second_ref, first_ref, got32, grad, *, per):
    total, width = got_ref.shape
    count, half = total // per, width // 2
    strided_fill(got32, got_ref)
    for mode in range(per):
        real, imag = latitude_forward(table_ref, strided_take(got32, mode, per, total, width), count)
        span = slice(mode * count, (mode + 1) * count)
        second_ref[span, :half] = (real * factor_ref[span, :half].astype(F32)).astype(BF16)
        second_ref[span, half:] = (imag * factor_ref[span, half:].astype(F32)).astype(BF16)
    chunk = chunk_of(total)

    @pl.loop(0, total // chunk)
    def _(step):
        span = pl.ds(pl.multiple_of(step * chunk, chunk), chunk)
        grad_active = dot_transposed(second_ref[span, :], two_ref[...])
        first = (grad_active * slope_ref[span, :].astype(F32)).astype(BF16)
        first_ref[span, :] = first
        grad[span, :] = dot_transposed(first, one_ref[...])

    for mode in range(per):
        real, imag = latitude_inverse(table_ref, grad[mode * count : (mode + 1) * count, :], count)
        strided_put(got32, mode, per, total, 0, real)
        strided_put(got32, mode, per, total, half // 128, imag)
    strided_send(sent_ref, got32)


def dense_kernel(live_ref, norm_ref, in_ref, in_bias_ref, out_ref, out_bias_ref, mixed_ref, result_ref, active_ref, slope_ref, total):
    step = pl.program_id(0)
    hidden = dot(norm_ref[...], in_ref[...]) + in_bias_ref[...]
    active, slope = gelu_pair(hidden)
    active = active.astype(BF16)
    active_ref[...] = active
    slope_ref[...] = slope.astype(BF16)
    part = dot(active, out_ref[...])

    @pl.when(step == 0)
    def _():
        total[...] = part + mixed_ref[...] + out_bias_ref[...]

    @pl.when(step > 0)
    def _():
        total[...] += part

    @pl.when(step == pl.num_programs(0) - 1)
    def _():
        index = lax.broadcasted_iota(jnp.int32, total.shape, 0)
        result_ref[...] = jnp.where(index < live_ref[0], total[...], 0.0).astype(BF16)


def dense_back_kernel(grad_ref, out_ref, slope_ref, in_ref, hidden_ref, bias_ref, norm_ref):
    step = pl.program_id(0)
    grad_active = dot_transposed(grad_ref[...], out_ref[...])
    hidden = (grad_active * slope_ref[...].astype(F32)).astype(BF16)
    hidden_ref[...] = hidden
    bias_ref[...] = jnp.sum(hidden.astype(F32), axis=0, keepdims=True)
    part = dot_transposed(hidden, in_ref[...])

    @pl.when(step == 0)
    def _():
        norm_ref[...] = part

    @pl.when(step > 0)
    def _():
        norm_ref[...] += part


def middle_back_kernel(norm_ref, mixed_ref, grad_ref, gain_two_ref, table_ref, sent_ref, grad_mixed_ref, small_ref, grad32, sent32, *, rows, lanes, per):
    grad32[...] = grad_ref[...].astype(F32)
    longs = mixed_ref.shape[0] // rows
    gain_grad = shift_grad = bias_grad = 0.0
    for row in range(rows):
        span = slice(row * longs, (row + 1) * longs)
        unit, inverse = centered(mixed_ref[span, :])
        grad_norm = norm_ref[span, :]
        grad_out = grad32[span, :]
        grad_mixed = norm_back(grad_norm, gain_two_ref[...], unit, inverse) + grad_out
        gain_grad += jnp.sum(grad_norm * unit, axis=0, keepdims=True)
        shift_grad += jnp.sum(grad_norm, axis=0, keepdims=True)
        bias_grad += jnp.sum(grad_out, axis=0, keepdims=True)
        grad_mixed_ref[span, :] = grad_mixed
        scatter_modes(sent32, table_times(table_ref, grad_mixed), row, rows, lanes, per)
    small_ref[0:1, :] = gain_grad
    small_ref[1:2, :] = shift_grad
    small_ref[2:3, :] = bias_grad
    sent_ref[...] = sent32[...].astype(BF16)


def front_back_kernel(back_ref, grad_mixed_ref, x_ref, gain_ref, table_ref, grad_ref, small_ref, x32, back32, spectrum, *, rows, lanes, per):
    x32[...] = x_ref[...].astype(F32)
    back32[...] = back_ref[...].astype(F32)
    longs = x_ref.shape[0] // rows
    gain_grad = shift_grad = 0.0
    for row in range(rows):
        span = slice(row * longs, (row + 1) * longs)
        gather_modes(spectrum, back32, row, rows, lanes, per)
        grad_mixed = grad_mixed_ref[span, :]
        grad_normed = table_times_low(table_ref, spectrum[...].astype(BF16)) + grad_mixed
        unit, inverse = centered(x32[span, :])
        gain_grad += jnp.sum(grad_normed * unit, axis=0, keepdims=True)
        shift_grad += jnp.sum(grad_normed, axis=0, keepdims=True)
        x32[span, :] = norm_back(grad_normed, gain_ref[...], unit, inverse) + grad_mixed
    small_ref[0:1, :] = gain_grad
    small_ref[1:2, :] = shift_grad
    grad_ref[...] = x32[...].astype(BF16)


def call(body, outs, scratch, *args, flops=0, **named):
    bytes_moved = sum(a.size * a.dtype.itemsize for a in args) + sum(math.prod(s) * np.dtype(d).itemsize for s, d in outs)
    return pl.pallas_call(
        functools.partial(body, **named),
        out_shape=[jax.ShapeDtypeStruct(s, d) for s, d in outs],
        in_specs=[pl.BlockSpec(memory_space=pltpu.VMEM)] * len(args),
        out_specs=[pl.BlockSpec(memory_space=pltpu.VMEM)] * len(outs),
        scratch_shapes=[pltpu.VMEM(s, F32) for s in scratch],
        compiler_params=pltpu.CompilerParams(vmem_limit_bytes=VMEM_BYTES),
        cost_estimate=pl.CostEstimate(flops=flops, bytes_accessed=bytes_moved, transcendentals=0),
    )(*args)


def front(x, gain, shift, lay):
    tokens, width = x.shape
    moved = (lay["modes"], width)
    return call(front_kernel, [(moved, BF16)], [(tokens, width), moved], x, gain, shift, lay["to_modes"], flops=lay["cost"], **lay["sizes"])[0]


def middle(back, x, gain, shift, gain_two, shift_two, lay):
    tokens, width = x.shape
    scratch = [(tokens, width), (lay["modes"], width), (lay["waves"], width), (tokens, width)]
    outs = [((tokens, width), F32), ((tokens, width), BF16)]
    return call(middle_kernel, outs, scratch, back, x, gain, shift, gain_two, shift_two, lay["from_modes"], flops=lay["cost"], **lay["sizes"])


def apart(shape):
    return (shape[0] * shape[1] // 128, 128)


def spectral(got, w, lay):
    shape = got.shape
    return call(spectral_kernel, [(shape, BF16)] * 5, [apart(shape), shape], got, lay["latitude"], w[2], w[3], w[4], w[5], flops=4 * lay["cost"], per=lay["sizes"]["per"])


def spectral_back(got, w, slope, factor, lay):
    shape = got.shape
    return call(spectral_back_kernel, [(shape, BF16)] * 3, [apart(shape), shape], got, lay["latitude"], w[2], w[4], slope, factor, flops=4 * lay["cost"], per=lay["sizes"]["per"])


def dense(norm, mixed, w, live):
    tokens, width = norm.shape
    hidden = w[8].shape[1]
    tile = 512
    whole = lambda shape: pl.BlockSpec(shape, lambda j: (0, 0))
    across = lambda count: pl.BlockSpec((count, tile), lambda j: (0, j))
    return pl.pallas_call(
        dense_kernel,
        grid=(hidden // tile,),
        out_shape=[
            jax.ShapeDtypeStruct((tokens, width), BF16),
            jax.ShapeDtypeStruct((tokens, hidden), BF16),
            jax.ShapeDtypeStruct((tokens, hidden), BF16),
        ],
        in_specs=[
            pl.BlockSpec(memory_space=pltpu.SMEM),
            whole((tokens, width)),
            across(width),
            across(1),
            pl.BlockSpec((tile, width), lambda j: (j, 0)),
            whole((1, width)),
            whole((tokens, width)),
        ],
        out_specs=[whole((tokens, width)), across(tokens), across(tokens)],
        scratch_shapes=[pltpu.VMEM((tokens, width), F32)],
        compiler_params=pltpu.CompilerParams(vmem_limit_bytes=VMEM_BYTES, dimension_semantics=("arbitrary",)),
        cost_estimate=pl.CostEstimate(flops=4 * tokens * width * hidden, bytes_accessed=30 << 20, transcendentals=tokens * hidden),
    )(live, norm, w[8], w[9], w[10], w[11], mixed)


def dense_back(grad, w, slope):
    tokens, width = grad.shape
    hidden = w[8].shape[1]
    tile = 512
    whole = lambda shape: pl.BlockSpec(shape, lambda j: (0, 0))
    across = lambda count: pl.BlockSpec((count, tile), lambda j: (0, j))
    return pl.pallas_call(
        dense_back_kernel,
        grid=(hidden // tile,),
        out_shape=[
            jax.ShapeDtypeStruct((tokens, hidden), BF16),
            jax.ShapeDtypeStruct((1, hidden), F32),
            jax.ShapeDtypeStruct((tokens, width), F32),
        ],
        in_specs=[whole((tokens, width)), pl.BlockSpec((tile, width), lambda j: (j, 0)), across(tokens), across(width)],
        out_specs=[across(tokens), across(1), whole((tokens, width))],
        compiler_params=pltpu.CompilerParams(vmem_limit_bytes=VMEM_BYTES, dimension_semantics=("arbitrary",)),
        cost_estimate=pl.CostEstimate(flops=4 * tokens * width * hidden, bytes_accessed=30 << 20, transcendentals=0),
    )(grad, w[10], slope, w[8])


def middle_back(grad_norm, mixed, grad, gain_two, lay):
    tokens, width = mixed.shape
    moved = (lay["modes"], width)
    outs = [(moved, BF16), ((tokens, width), F32), ((3, width), F32)]
    return call(middle_back_kernel, outs, [(tokens, width), moved], grad_norm, mixed, grad, gain_two, lay["to_modes_grad"], flops=lay["cost"], **lay["sizes"])


def front_back(back, grad_mixed, x, gain, lay):
    tokens, width = x.shape
    scratch = [(tokens, width), (lay["modes"], width), (lay["waves"], width)]
    return call(front_back_kernel, [((tokens, width), BF16), ((2, width), F32)], scratch, back, grad_mixed, x, gain, lay["from_modes_grad"], flops=lay["cost"], **lay["sizes"])


def exchange(item):
    count = lax.axis_size("lane") * 2
    pieces = item.reshape(count, item.shape[0] // count, item.shape[1])
    return lax.all_to_all(pieces, ROWS_AXES, 0, 0, tiled=True).reshape(item.shape)


def swap(item, axis, bit):
    return lax.ppermute(item, axis, [(i, i ^ bit) for i in range(lax.axis_size(axis))])


def shed(item, axis, bit):
    set_bit = (lax.axis_index(axis) & bit) > 0
    count = item.shape[0] // 2
    lower, upper = item[:count], item[count:]
    got = swap(jnp.where(set_bit, lower, upper), axis, bit)
    return (jnp.where(set_bit, upper, lower).astype(F32) + got.astype(F32)).astype(BF16)


def double(item, axis, bit):
    set_bit = (lax.axis_index(axis) & bit) > 0
    got = swap(item, axis, bit)
    return jnp.concatenate([jnp.where(set_bit, got, item), jnp.where(set_bit, item, got)], 0)


def lane_bits(turn):
    bits = [1 << i for i in range(lax.axis_size("lane").bit_length() - 1)]
    return [("lane", b) for b in bits[-turn:] + bits[:-turn]] if turn else [("lane", b) for b in bits]


def add_up(item, turn):
    route = [("section", 1)] + lane_bits(turn) + [("half", 1)]
    for axis, bit in route:
        item = shed(item, axis, bit)
    for axis, bit in route[:0:-1]:
        item = double(item, axis, bit)
    return item


def add_small(item):
    slabs = lax.axis_size("lane") * lax.axis_size("half")
    size = item.shape[0]
    each = -(-size // (slabs * 1024)) * 1024
    pieces = jnp.pad(item, (0, slabs * each - size)).astype(BF16).reshape(slabs, each // 128, 128)
    got = lax.all_to_all(pieces, SLAB, 0, 0, tiled=True)
    total = jnp.sum(got.astype(F32), axis=0).astype(BF16)
    spread = jnp.broadcast_to(total[None], pieces.shape)
    return lax.all_to_all(spread, SLAB, 0, 0, tiled=True).reshape(-1)[:size].astype(F32)


def both_layers(item, core):
    other = lax.ppermute(item, "section", [(0, 1), (1, 0)])
    return (jnp.where(core == 0, item, other), jnp.where(core == 0, other, item))


def fetch(pair, core, half):
    own = lax.dynamic_index_in_dim(pair, half, 0, keepdims=False)
    give = lax.dynamic_index_in_dim(pair, 1 - half, 0, keepdims=False)
    got = lax.ppermute(give, ("section", "half"), [(0, 1), (3, 2)])
    got = jnp.where(core == half, own, got)
    return got.reshape(-1, got.shape[-1])


def deliver(layer_zero, layer_one, core, shape):
    parts = []
    for micro in range(2):
        first = lax.ppermute(layer_zero, ("section", "half"), [(micro, 0), (2 + micro, 1)])
        second = lax.ppermute(layer_one, ("section", "half"), [(micro, 2), (2 + micro, 3)])
        parts.append(jnp.where(core == 0, first, second).reshape(shape))
    return jnp.stack(parts)[None]


def block_diagonal(weight):
    _, blocks, size, _ = weight.shape
    same = jnp.eye(blocks, dtype=weight.dtype)
    real, imag = (jnp.einsum("bij,bc->bicj", w, same).reshape(blocks * size, blocks * size) for w in (weight[0], weight[1]))
    return jnp.concatenate([jnp.concatenate([real, imag], 1), jnp.concatenate([-imag, real], 1)], 0)


def block_grads(left, right):
    width = left.shape[1]
    blocks = BLOCKS // 2
    size = width // 2 // blocks
    outer = lax.dot_general(left, right, (((0,), (0,)), ((), ())), preferred_element_type=F32)

    def pick(i, j, b):
        top, side = (i * blocks + b) * size, (j * blocks + b) * size
        return outer[top : top + size, side : side + size]

    real = [pick(0, 0, b) + pick(1, 1, b) for b in range(blocks)]
    imag = [pick(0, 1, b) - pick(1, 0, b) for b in range(blocks)]
    return jnp.stack(real + imag).reshape(2, blocks, size, size)


def layer_forward(x, w, live, lay):
    got = exchange(front(x, w[0], w[1], lay))
    sent, low, active, slope, factor = spectral(got, w, lay)
    mixed, norm = middle(exchange(sent), x, w[0], w[1], w[6], w[7], lay)
    result, activated, bend = dense(norm, mixed, w, live)
    return result, (x, low, active, slope, factor, mixed, norm, activated, bend)


def layer_backward(saved, grad, w, lay):
    x, low, active, slope, factor, mixed, norm, activated, bend = saved
    grad_hidden, grad_in_bias, grad_norm = dense_back(grad, w, bend)
    sent, grad_mixed, small_two = middle_back(grad_norm, mixed, grad, w[6], lay)
    got = exchange(sent)
    across = (((0,), (0,)), ((), ()))
    grad_in = lax.dot_general(norm, grad_hidden, across, preferred_element_type=F32).astype(BF16)
    grad_out = lax.dot_general(activated, grad, across, preferred_element_type=F32).astype(BF16)
    dense_grads = (add_up(grad_in, 0), add_up(grad_out, 1))
    sent, grad_second, grad_first = spectral_back(got, w, slope, factor, lay)
    got = exchange(sent)
    grad_one, grad_two = block_grads(low, grad_first), block_grads(active, grad_second)
    bias_one = jnp.sum(grad_first.astype(F32), axis=0)
    bias_two = jnp.sum(grad_second.astype(F32), axis=0)
    grad_x, small_one = front_back(got, grad_mixed, x, w[0], lay)
    late = add_small(small_one.reshape(-1))
    early = (grad_one, grad_two, bias_one, bias_two, small_two, grad_in_bias)
    shapes = [a.shape for a in early]
    merged = add_small(jnp.concatenate([a.reshape(-1) for a in early]))
    pieces = []
    for shape in shapes:
        size = math.prod(shape)
        pieces.append(merged[:size].reshape(shape))
        merged = merged[size:]
    return grad_x, dense_grads, (*pieces, late.reshape(small_one.shape))


def shards(tokens, cotangent, *params):
    core = lax.axis_index("section")
    half = lax.axis_index("half")
    lane = lax.axis_index("lane")
    lanes = lax.axis_size("lane")
    _, rows, longitudes, width = tokens.shape
    total_rows = rows * lanes * 2
    fields = total_rows // LAT
    live = fields * LAT
    per = -(-(longitudes // 2 + 1) // lanes)
    forward_table, inverse_table = longitude_tables(longitudes, per * lanes)
    lay = {
        "to_modes": jnp.asarray(split_table(forward_table.T)),
        "from_modes": jnp.asarray(split_table(inverse_table)),
        "to_modes_grad": jnp.asarray(split_table(inverse_table.T)),
        "from_modes_grad": jnp.asarray(split_table(forward_table)),
        "latitude": jnp.asarray(split_table(latitude_table(total_rows, fields))),
        "modes": 2 * lanes * rows * per,
        "waves": 2 * lanes * per,
        "cost": 1 << 30,
        "sizes": {"rows": rows, "lanes": lanes, "per": per},
    }
    first_row = (core * lanes + lane) * rows
    live_tokens = (jnp.clip(live - first_row, 0, rows) * longitudes).astype(jnp.int32)
    blocks = BLOCKS // 2
    x = fetch(tokens, core, half)
    grad = fetch(cotangent, core, half)
    grad = jnp.where(jnp.arange(grad.shape[0], dtype=jnp.int32)[:, None] < live_tokens, grad, jnp.zeros_like(grad))
    pairs = [both_layers(item[0], core) for item in params]
    layers = []
    for level in range(2):
        w = [pair[level] for pair in pairs]
        for at in (2, 4):
            w[at] = block_diagonal(lax.dynamic_slice_in_dim(w[at], core * blocks, blocks, 1))
        for at in (3, 5):
            w[at] = lax.dynamic_slice_in_dim(w[at], core * blocks, blocks, 1).astype(F32).reshape(1, -1)
        for at in (0, 1, 6, 7, 9, 11):
            w[at] = w[at].astype(F32).reshape(1, -1)
        layers.append(w)
    live_arg = live_tokens.reshape(1)
    out_one, saved_one = layer_forward(x, layers[0], live_arg, lay)
    out_two, saved_two = layer_forward(out_one, layers[1], live_arg, lay)
    grad_two, dense_two, rest_two = layer_backward(saved_two, grad, layers[1], lay)
    grad_one, dense_one, rest_one = layer_backward(saved_one, grad_two, layers[0], lay)
    shape = tokens.shape[1:]
    outputs = deliver(out_one, out_two, core, shape)
    input_grads = deliver(grad_one, grad_two, core, shape)
    dense_outs = []
    for first, second in zip(dense_one, dense_two):
        got_first = lax.ppermute(first, "section", [(1, 0)])
        got_second = lax.ppermute(second, "section", [(0, 1)])
        upper = jnp.where(core == 0, first, got_second)
        lower = jnp.where(core == 0, got_first, second)
        dense_outs.append(jnp.concatenate([upper, lower], 0).astype(F32)[None])
    size = width // BLOCKS
    rest = []
    for first, second in zip(rest_one, rest_two):
        other = lax.ppermute(jnp.where(core == 0, second, first), "section", [(0, 1), (1, 0)])
        rest.append((jnp.where(core == 0, first, second), other))

    def joined(pair, axis):
        own, other = pair
        return jnp.where(core == 0, jnp.concatenate([own, other], axis), jnp.concatenate([other, own], axis))

    spectral_one, spectral_two = (joined(rest[i], 1)[None] for i in (0, 1))
    biases = []
    for i in (2, 3):
        biases.append(joined([a.reshape(2, blocks, size) for a in rest[i]], 1)[None])
    small_two, in_bias, small_one = (a + b for a, b in rest[4:])
    return (
        outputs, input_grads, small_one[0:1], small_one[1:2], spectral_one, biases[0], spectral_two, biases[1],
        small_two[0:1], small_two[1:2], dense_outs[0], in_bias, dense_outs[1], small_two[2:3],
    )


def solution(mesh):
    devices = mesh.devices
    slabs = devices.shape[1]
    wide = Mesh(devices.reshape(2, 2, slabs // 2), ALL)
    rows = P(None, ("half", "lane"))
    own = P("section")
    return jax.shard_map(
        shards,
        mesh=wide,
        in_specs=(rows, rows) + (own,) * 12,
        out_specs=(P("section", None, ("half", "lane")),) * 2 + (own,) * 12,
        check_vma=False,
    )
```

```python
import functools
import math

import jax
import jax.numpy as jnp
import numpy as np
from jax import lax
from jax.experimental import pallas as pl
from jax.experimental.pallas import tpu as pltpu
from jax.sharding import Mesh, PartitionSpec as P

BLOCKS = 8
LAT = 90
EPSILON = 1e-05
SHRINK = 0.01
SOFTNESS = 0.1
ROWS_AXES = ("section", "lane")
ALL = ("section", "half", "lane")
SLAB = ("half", "lane")
F32 = jnp.float32
BF16 = jnp.bfloat16
VMEM_BYTES = 56 * 1024 * 1024
GAIN_ONE, SHIFT_ONE, GAIN_TWO, SHIFT_TWO, OUT_BIAS, IN_BIAS, BIAS_ONE, BIAS_TWO = 0, 1, 2, 3, 4, 5, 9, 10
G_GAIN_TWO, G_SHIFT_TWO, G_OUT_BIAS, G_IN_BIAS, G_BIAS_ONE, G_BIAS_TWO, G_GAIN_ONE, G_SHIFT_ONE, G_ROWS = 0, 1, 2, 3, 7, 8, 9, 10, 16


def split_table(table):
    high = np.asarray(table, np.float32).astype(jnp.bfloat16)
    low = (np.asarray(table, np.float64) - high.astype(np.float64)).astype(jnp.bfloat16)
    return np.concatenate([high, low], 0)


def longitude_tables(longitudes, padded):
    column = np.arange(longitudes)[:, None]
    frequency = np.arange(padded)[None, :]
    angle = (column * frequency % longitudes) * (2.0 * math.pi / longitudes)
    usable = (frequency <= longitudes // 2) / math.sqrt(longitudes)
    forward = np.concatenate([np.cos(angle) * usable, -np.sin(angle) * usable], 1)
    doubled = np.where((frequency == 0) | (frequency == longitudes // 2), 1.0, 2.0)
    inverse = forward * np.concatenate([doubled, doubled], 1)
    return (forward, inverse)


def latitude_table(rows, fields):
    index = np.arange(LAT)
    angle = (index[:, None] * index[None, :] % LAT) * (2.0 * math.pi / LAT)
    parts = []
    for wave in (np.cos(angle), np.sin(angle)):
        whole = np.zeros((rows, rows))
        for field in range(fields):
            span = slice(field * LAT, (field + 1) * LAT)
            whole[span, span] = wave / math.sqrt(LAT)
        parts.append(whole)
    return np.concatenate(parts, 0)


def dot(left, right):
    return jnp.dot(left, right, preferred_element_type=F32)


def dot_transposed(left, right):
    return lax.dot_general(left, right, (((1,), (1,)), ((), ())), preferred_element_type=F32)


def table_times_low(table_ref, low):
    count = table_ref.shape[0] // 2
    return dot(table_ref[:count, :], low) + dot(table_ref[count:, :], low)


def table_times(table_ref, value):
    count = table_ref.shape[0] // 2
    high = value.astype(BF16)
    rest = (value - high.astype(F32)).astype(BF16)
    return dot(table_ref[:count, :], high) + dot(table_ref[:count, :], rest) + dot(table_ref[count:, :], high)


def gelu_pair(value):
    size = jnp.abs(value) * math.sqrt(0.5)
    inverse = 1.0 / (1.0 + 0.3275911 * size)
    wave = jnp.exp(-0.5 * value * value)
    series = inverse * (0.254829592 + inverse * (-0.284496736 + inverse * (1.421413741 + inverse * (-1.453152027 + inverse * 1.061405429))))
    tail = 0.5 * series * wave
    share = jnp.where(value > 0, 1.0 - tail, tail)
    return value * share, share + value * wave * (1.0 / math.sqrt(2.0 * math.pi))


def row_of(vec_ref, at):
    return vec_ref[at : at + 1, :]


def centered(value):
    center = value - jnp.mean(value, axis=-1, keepdims=True)
    inverse = lax.rsqrt(jnp.mean(center * center, axis=-1, keepdims=True) + EPSILON)
    return center * inverse, inverse


def norm_back(grad, gain, unit, inverse):
    scaled = grad * gain
    return (scaled - jnp.mean(scaled, axis=-1, keepdims=True) - unit * jnp.mean(scaled * unit, axis=-1, keepdims=True)) * inverse


def scatter_modes(sent, spectrum, row, rows, lanes, per):
    width = spectrum.shape[1]
    half = width // 2
    modes = lanes * per
    for part in range(2):
        for lane in range(lanes):
            base = ((part * lanes + lane) * rows + row) * per
            for wave in range(2):
                piece = spectrum[wave * modes + lane * per : wave * modes + (lane + 1) * per, part * half : (part + 1) * half]
                sent[base : base + per, wave * half : (wave + 1) * half] = piece


def gather_modes(spectrum, back, row, rows, lanes, per):
    width = spectrum.shape[1]
    half = width // 2
    modes = lanes * per
    for part in range(2):
        for lane in range(lanes):
            base = ((part * lanes + lane) * rows + row) * per
            for wave in range(2):
                piece = back[base : base + per, wave * half : (wave + 1) * half]
                spectrum[wave * modes + lane * per : wave * modes + (lane + 1) * per, part * half : (part + 1) * half] = piece


def front_kernel(x_ref, vec_ref, table_ref, sent_ref, sent32, *, rows, lanes, per):
    for row in range(rows):
        unit, _ = centered(x_ref[row].astype(F32))
        spectrum = table_times(table_ref, unit * row_of(vec_ref, GAIN_ONE) + row_of(vec_ref, SHIFT_ONE))
        scatter_modes(sent32, spectrum, row, rows, lanes, per)
    sent_ref[...] = sent32[...].astype(BF16)


def middle_kernel(back_ref, x_ref, vec_ref, table_ref, mixed_ref, norm_ref, back32, spectrum, norm32, *, rows, lanes, per):
    back32[...] = back_ref[...].astype(F32)
    longs = x_ref.shape[1]
    for row in range(rows):
        span = slice(row * longs, (row + 1) * longs)
        gather_modes(spectrum, back32, row, rows, lanes, per)
        value = x_ref[row].astype(F32)
        unit, _ = centered(value)
        mixed = table_times_low(table_ref, spectrum[...].astype(BF16)) + (unit * row_of(vec_ref, GAIN_ONE) + row_of(vec_ref, SHIFT_ONE)) + value
        mixed_ref[span, :] = mixed
        unit, _ = centered(mixed)
        norm32[span, :] = unit * row_of(vec_ref, GAIN_TWO) + row_of(vec_ref, SHIFT_TWO)
    norm_ref[...] = norm32[...].astype(BF16)


def latitude_forward(table_ref, value, count):
    half = value.shape[1] // 2
    both = table_times_low(table_ref, value)
    cosine, sine = both[:count, :], both[count:, :]
    return cosine[:, :half] + sine[:, half:], cosine[:, half:] - sine[:, :half]


def latitude_inverse(table_ref, value, count):
    half = value.shape[1] // 2
    both = table_times(table_ref, value)
    cosine, sine = both[:count, :], both[count:, :]
    return cosine[:, :half] - sine[:, half:], cosine[:, half:] + sine[:, :half]


def strided_fill(apart, got_ref):
    total, width = got_ref.shape
    for tile in range(width // 128):
        apart[tile * total : (tile + 1) * total, :] = got_ref[:, tile * 128 : (tile + 1) * 128].astype(F32)


def strided_take(apart, mode, per, total, width):
    spans = [pl.ds(tile * total + mode, total // per, stride=per) for tile in range(width // 128)]
    return jnp.concatenate([apart[span, :] for span in spans], 1).astype(BF16)


def strided_put(apart, mode, per, total, first, value):
    for tile in range(value.shape[1] // 128):
        span = pl.ds((first + tile) * total + mode, total // per, stride=per)
        apart[span, :] = value[:, tile * 128 : (tile + 1) * 128]


def strided_send(sent_ref, apart):
    total, width = sent_ref.shape
    for tile in range(width // 128):
        sent_ref[:, tile * 128 : (tile + 1) * 128] = apart[tile * total : (tile + 1) * total, :].astype(BF16)


def chunk_of(total):
    return total // 3 if total % 48 == 0 else total


def spectral_kernel(got_ref, table_ref, one_ref, two_ref, vec_ref, sent_ref, low_ref, active_ref, slope_ref, factor_ref, got32, shrunk, *, per):
    total, width = got_ref.shape
    count, half = total // per, width // 2
    strided_fill(got32, got_ref)
    for mode in range(per):
        real, imag = latitude_forward(table_ref, strided_take(got32, mode, per, total, width), count)
        span = slice(mode * count, (mode + 1) * count)
        low_ref[span, :half] = real.astype(BF16)
        low_ref[span, half:] = imag.astype(BF16)
    chunk = chunk_of(total)

    @pl.loop(0, total // chunk)
    def _(step):
        span = pl.ds(pl.multiple_of(step * chunk, chunk), chunk)
        first = dot(low_ref[span, :], one_ref[...]) + row_of(vec_ref, BIAS_ONE)
        active, slope = gelu_pair(first)
        active = active.astype(BF16)
        active_ref[span, :] = active
        slope_ref[span, :] = slope.astype(BF16)
        second = dot(active, two_ref[...]) + row_of(vec_ref, BIAS_TWO)
        bend = jnp.tanh(second * (1.0 / SOFTNESS))
        shrunk[span, :] = second - SHRINK * bend
        factor_ref[span, :] = (1.0 - SHRINK / SOFTNESS * (1.0 - bend * bend)).astype(BF16)

    for mode in range(per):
        real, imag = latitude_inverse(table_ref, shrunk[mode * count : (mode + 1) * count, :], count)
        strided_put(got32, mode, per, total, 0, real)
        strided_put(got32, mode, per, total, half // 128, imag)
    strided_send(sent_ref, got32)


def spectral_back_kernel(got_ref, table_ref, one_ref, two_ref, slope_ref, factor_ref, sent_ref, second_ref, first_ref, got32, grad, *, per):
    total, width = got_ref.shape
    count, half = total // per, width // 2
    strided_fill(got32, got_ref)
    for mode in range(per):
        real, imag = latitude_forward(table_ref, strided_take(got32, mode, per, total, width), count)
        span = slice(mode * count, (mode + 1) * count)
        second_ref[span, :half] = (real * factor_ref[span, :half].astype(F32)).astype(BF16)
        second_ref[span, half:] = (imag * factor_ref[span, half:].astype(F32)).astype(BF16)
    chunk = chunk_of(total)

    @pl.loop(0, total // chunk)
    def _(step):
        span = pl.ds(pl.multiple_of(step * chunk, chunk), chunk)
        grad_active = dot_transposed(second_ref[span, :], two_ref[...])
        first = (grad_active * slope_ref[span, :].astype(F32)).astype(BF16)
        first_ref[span, :] = first
        grad[span, :] = dot_transposed(first, one_ref[...])

    for mode in range(per):
        real, imag = latitude_inverse(table_ref, grad[mode * count : (mode + 1) * count, :], count)
        strided_put(got32, mode, per, total, 0, real)
        strided_put(got32, mode, per, total, half // 128, imag)
    strided_send(sent_ref, got32)


def choose(place_ref, level, own_ref, other_ref, chosen):
    @pl.when(place_ref[0] == level)
    def _():
        chosen[...] = own_ref[...]

    @pl.when(place_ref[0] != level)
    def _():
        chosen[...] = other_ref[...]


def dense_kernel(place_ref, norm_ref, in_ref, in_other_ref, out_ref, out_other_ref, vec_ref, mixed_ref, result_ref, active_ref, slope_ref, total, in_kept, out_kept, *, level):
    step = pl.program_id(0)
    choose(place_ref, level, in_ref, in_other_ref, in_kept)
    choose(place_ref, level, out_ref, out_other_ref, out_kept)
    hidden = dot(norm_ref[...], in_kept[...]) + vec_ref[pl.ds(IN_BIAS + step, 1), :]
    active, slope = gelu_pair(hidden)
    active = active.astype(BF16)
    active_ref[...] = active
    slope_ref[...] = slope.astype(BF16)
    part = dot(active, out_kept[...])

    @pl.when(step == 0)
    def _():
        total[...] = part + mixed_ref[...] + row_of(vec_ref, OUT_BIAS)

    @pl.when(step > 0)
    def _():
        total[...] += part

    @pl.when(step == pl.num_programs(0) - 1)
    def _():
        rows, longs, _ = result_ref.shape
        for row in range(rows):
            value = total[row * longs : (row + 1) * longs, :]
            result_ref[row] = jnp.where(row < place_ref[1], value, 0.0).astype(BF16)


def dense_back_kernel(place_ref, grad_ref, out_ref, out_other_ref, slope_ref, in_ref, in_other_ref, hidden_ref, bias_ref, norm_ref, in_kept, out_kept, *, level):
    step = pl.program_id(0)
    choose(place_ref, level, in_ref, in_other_ref, in_kept)
    choose(place_ref, level, out_ref, out_other_ref, out_kept)
    grad_active = dot_transposed(grad_ref[...], out_kept[...])
    hidden = (grad_active * slope_ref[...].astype(F32)).astype(BF16)
    hidden_ref[...] = hidden
    bias_ref[pl.ds(step, 1), :] = jnp.sum(hidden.astype(F32), axis=0, keepdims=True)
    part = dot_transposed(hidden, in_kept[...])

    @pl.when(step == 0)
    def _():
        norm_ref[...] = part

    @pl.when(step > 0)
    def _():
        norm_ref[...] += part


def middle_back_kernel(norm_ref, mixed_ref, grad_ref, vec_ref, table_ref, sent_ref, grad_mixed_ref, small_ref, grad32, sent32, *, rows, lanes, per):
    grad32[...] = grad_ref[...].astype(F32)
    longs = mixed_ref.shape[0] // rows
    gain_grad = shift_grad = bias_grad = 0.0
    for row in range(rows):
        span = slice(row * longs, (row + 1) * longs)
        unit, inverse = centered(mixed_ref[span, :])
        grad_norm = norm_ref[span, :]
        grad_out = grad32[span, :]
        grad_mixed = norm_back(grad_norm, row_of(vec_ref, GAIN_TWO), unit, inverse) + grad_out
        gain_grad += jnp.sum(grad_norm * unit, axis=0, keepdims=True)
        shift_grad += jnp.sum(grad_norm, axis=0, keepdims=True)
        bias_grad += jnp.sum(grad_out, axis=0, keepdims=True)
        grad_mixed_ref[span, :] = grad_mixed
        scatter_modes(sent32, table_times(table_ref, grad_mixed), row, rows, lanes, per)
    small_ref[0:1, :] = gain_grad
    small_ref[1:2, :] = shift_grad
    small_ref[2:3, :] = bias_grad
    sent_ref[...] = sent32[...].astype(BF16)


def front_back_kernel(back_ref, grad_mixed_ref, x_ref, vec_ref, table_ref, known_ref, grad_ref, flat_ref, small_ref, back32, spectrum, flat32, *, rows, lanes, per):
    back32[...] = back_ref[...].astype(F32)
    longs = x_ref.shape[1]
    gain_grad = shift_grad = 0.0
    for row in range(rows):
        span = slice(row * longs, (row + 1) * longs)
        gather_modes(spectrum, back32, row, rows, lanes, per)
        grad_mixed = grad_mixed_ref[span, :]
        grad_normed = table_times_low(table_ref, spectrum[...].astype(BF16)) + grad_mixed
        unit, inverse = centered(x_ref[row].astype(F32))
        gain_grad += jnp.sum(grad_normed * unit, axis=0, keepdims=True)
        shift_grad += jnp.sum(grad_normed, axis=0, keepdims=True)
        grad = norm_back(grad_normed, row_of(vec_ref, GAIN_ONE), unit, inverse) + grad_mixed
        flat32[span, :] = grad
        grad_ref[row] = grad.astype(BF16)
    known = known_ref[...]
    index = lax.broadcasted_iota(jnp.int32, known.shape, 0)
    known = jnp.where(index == G_GAIN_ONE, gain_grad, jnp.where(index == G_SHIFT_ONE, shift_grad, known))
    for tile in range(known.shape[1] // 128):
        small_ref[tile * G_ROWS : (tile + 1) * G_ROWS, :] = known[:, tile * 128 : (tile + 1) * 128].astype(BF16)
    flat_ref[...] = flat32[...].astype(BF16)


def spectral_grad_kernel(low_ref, first_ref, active_ref, second_ref, small_ref, in_bias_ref, blocks_ref, known_ref, outer, *, blocks):
    half = outer.shape[0] // 2
    size = half // blocks
    blocks_ref[...] = jnp.zeros_like(blocks_ref)
    for which, (left, right) in enumerate(((low_ref, first_ref), (active_ref, second_ref))):
        outer[...] = lax.dot_general(left[...], right[...], (((0,), (0,)), ((), ())), preferred_element_type=F32)
        for block in range(blocks):
            up, down = slice(block * size, (block + 1) * size), slice(half + block * size, half + (block + 1) * size)
            at = (which * 2 * blocks + block) * size
            blocks_ref[at : at + size, :size] = (outer[up, up] + outer[down, down]).astype(BF16)
            at += blocks * size
            blocks_ref[at : at + size, :size] = (outer[up, down] - outer[down, up]).astype(BF16)
    known_ref[...] = jnp.zeros_like(known_ref)
    known_ref[G_GAIN_TWO : G_OUT_BIAS + 1, :] = small_ref[...]
    known_ref[G_IN_BIAS : G_IN_BIAS + 4, :] = in_bias_ref[...]
    known_ref[G_BIAS_ONE : G_BIAS_ONE + 1, :] = jnp.sum(first_ref[...].astype(F32), axis=0, keepdims=True)
    known_ref[G_BIAS_TWO : G_BIAS_TWO + 1, :] = jnp.sum(second_ref[...].astype(F32), axis=0, keepdims=True)


def matrices_kernel(place_ref, own_one_ref, own_two_ref, other_one_ref, other_two_ref, one_a_ref, two_a_ref, one_b_ref, two_b_ref, whole, *, blocks):
    core = place_ref[0]
    size = own_one_ref.shape[-1]
    half = blocks * size

    def build(source, target):
        whole[...] = jnp.zeros_like(whole)
        for block in range(blocks):
            real = source[0, core * blocks + block].astype(F32)
            imag = source[1, core * blocks + block].astype(F32)
            up, down = slice(block * size, (block + 1) * size), slice(half + block * size, half + (block + 1) * size)
            whole[up, up] = real
            whole[up, down] = imag
            whole[down, up] = -imag
            whole[down, down] = real
        target[...] = whole[...].astype(BF16)

    for level, targets in enumerate(((one_a_ref, two_a_ref), (one_b_ref, two_b_ref))):

        @pl.when(core == level)
        def _(targets=targets):
            build(own_one_ref, targets[0])
            build(own_two_ref, targets[1])

        @pl.when(core != level)
        def _(targets=targets):
            build(other_one_ref, targets[0])
            build(other_two_ref, targets[1])


def first_shed_kernel(place_ref, in_ref, in_got_ref, out_ref, out_got_ref, *targets):
    step = pl.program_id(0)
    for core, (mine, got) in enumerate(((out_ref, out_got_ref), (in_ref, in_got_ref))):

        @pl.when(place_ref[0] == core)
        def _(mine=mine, got=got):
            total = (mine[...].astype(F32) + got[...].astype(F32)).astype(BF16)
            for route in range(len(targets) // 2):
                keeps = (step // 2) % 2 == place_ref[2 + route]

                @pl.when((step // 4 == route) & keeps)
                def _(route=route, total=total):
                    targets[2 * route + 1][...] = total

                @pl.when((step // 4 == route) & jnp.logical_not(keeps))
                def _(route=route, total=total):
                    targets[2 * route][...] = total


def shed_kernel(bits_ref, *refs):
    count = len(refs) // 4
    kept, got, sends, keeps = (refs[i * count : (i + 1) * count] for i in range(4))
    for at in range(count):
        half = sends[at].shape[0]
        for target, bit in ((keeps[at], bits_ref[at]), (sends[at], 1 - bits_ref[at])):
            span = pl.ds(pl.multiple_of(bit * half, half), half)
            target[...] = (kept[at][span, :].astype(F32) + got[at][span, :].astype(F32)).astype(BF16)


def stack_kernel(*refs):
    *sources, target = refs
    count = len(sources) // 2
    rows = sources[0].shape[0]
    for at in range(count):
        target[at * rows : (at + 1) * rows, :] = (sources[at][...].astype(F32) + sources[count + at][...].astype(F32)).astype(BF16)


def add_kernel(place_ref, one_ref, one_got_ref, two_ref, two_got_ref, mine_ref, give_ref):
    for core, (first, second) in enumerate(((mine_ref, give_ref), (give_ref, mine_ref))):

        @pl.when(place_ref[0] == core)
        def _(first=first, second=second):
            first[...] = (one_ref[...].astype(F32) + one_got_ref[...].astype(F32)).astype(BF16)
            second[...] = (two_ref[...].astype(F32) + two_got_ref[...].astype(F32)).astype(BF16)


def pack_kernel(place_ref, mine_ref, got_ref, *targets):
    for core, (first, second) in enumerate(((mine_ref, got_ref), (got_ref, mine_ref))):

        @pl.when(place_ref[0] == core)
        def _(first=first, second=second):
            for at, target in enumerate(targets):
                rows = target.shape[1]
                target[0] = first[at * rows : (at + 1) * rows, :]
                target[1] = second[at * rows : (at + 1) * rows, :]


def double_kernel(bits_ref, *refs):
    count = len(refs) // 3
    own, got, targets = (refs[i * count : (i + 1) * count] for i in range(3))
    for at in range(count):
        rows = own[at].shape[1]
        for source, bit in ((own[at], bits_ref[at]), (got[at], 1 - bits_ref[at])):
            targets[at][:, pl.ds(pl.multiple_of(bit * rows, rows), rows), :] = source[...]


def finish_kernel(place_ref, *refs, routes):
    sources, (in_grad_ref, out_grad_ref) = refs[:routes], refs[-2:]
    part, step = pl.program_id(0), pl.program_id(1)
    rows = out_grad_ref.shape[0]
    per_half = sources[0].shape[1] // rows
    span = pl.ds(pl.multiple_of((step % per_half) * rows, rows), rows)
    for route in range(routes):
        for which, target in enumerate((out_grad_ref, in_grad_ref)):

            @pl.when((step // per_half == route) & (part == which))
            def _(target=target, source=sources[route]):
                target[...] = source[0, span, :].astype(F32)


def small_sum_kernel(got_ref, spread_ref):
    total = jnp.sum(got_ref[...].astype(F32), axis=0).astype(BF16)
    for at in range(spread_ref.shape[0]):
        spread_ref[at] = total


def small_finish_kernel(place_ref, own_ref, other_ref, one_ref, two_ref, bias_one_ref, bias_two_ref, gain_one_ref, shift_one_ref, gain_two_ref, shift_two_ref, in_bias_ref, out_bias_ref, vec, vec_other, *, blocks):
    core = place_ref[0]
    size = one_ref.shape[-1]
    matrix_rows = 4 * blocks * size
    tiles = vec.shape[1] // 128
    for which, target in enumerate((one_ref, two_ref)):
        for wave in range(2):
            for block in range(blocks):
                at = core * matrix_rows + ((which * 2 + wave) * blocks + block) * size
                span = pl.ds(pl.multiple_of(at, 32), size)
                target[wave, core * blocks + block] = own_ref[span, :].astype(F32)[:, :size]
                target[wave, (1 - core) * blocks + block] = other_ref[span, :].astype(F32)[:, :size]
    for source, target in ((own_ref, vec), (other_ref, vec_other)):
        for tile in range(tiles):
            at = 2 * matrix_rows + (core * tiles + tile) * G_ROWS
            target[:, tile * 128 : (tile + 1) * 128] = source[pl.ds(pl.multiple_of(at, G_ROWS), G_ROWS), :].astype(F32)
    half = vec.shape[1] // 2
    for row, target in ((G_BIAS_ONE, bias_one_ref), (G_BIAS_TWO, bias_two_ref)):
        for wave in range(2):
            for source, place in ((vec, core), (vec_other, 1 - core)):
                target[wave : wave + 1, pl.ds(pl.multiple_of(place * half, 128), half)] = source[row : row + 1, wave * half : (wave + 1) * half]
    total = vec[...] + vec_other[...]
    for row, target in ((G_GAIN_ONE, gain_one_ref), (G_SHIFT_ONE, shift_one_ref), (G_GAIN_TWO, gain_two_ref), (G_SHIFT_TWO, shift_two_ref), (G_OUT_BIAS, out_bias_ref)):
        target[...] = total[row : row + 1, :]
    in_bias_ref[...] = total[G_IN_BIAS : G_IN_BIAS + 4, :]


def call(body, outs, scratch, *args, flops=0, scalars=0, **named):
    bytes_moved = sum(a.size * a.dtype.itemsize for a in args) + sum(math.prod(s) * np.dtype(d).itemsize for s, d in outs)
    return pl.pallas_call(
        functools.partial(body, **named),
        out_shape=[jax.ShapeDtypeStruct(s, d) for s, d in outs],
        in_specs=[pl.BlockSpec(memory_space=pltpu.SMEM if i < scalars else pltpu.VMEM) for i in range(len(args))],
        out_specs=[pl.BlockSpec(memory_space=pltpu.VMEM)] * len(outs),
        scratch_shapes=[pltpu.VMEM(s, F32) for s in scratch],
        compiler_params=pltpu.CompilerParams(vmem_limit_bytes=VMEM_BYTES),
        cost_estimate=pl.CostEstimate(flops=flops, bytes_accessed=bytes_moved if flops else bytes_moved // 8, transcendentals=0),
    )(*args)


def front(x, vec, lay):
    moved = (lay["modes"], x.shape[2])
    return call(front_kernel, [(moved, BF16)], [moved], x, vec, lay["to_modes"], flops=lay["cost"], **lay["sizes"])[0]


def middle(back, x, vec, lay):
    tokens, width = x.shape[0] * x.shape[1], x.shape[2]
    scratch = [(lay["modes"], width), (lay["waves"], width), (tokens, width)]
    outs = [((tokens, width), F32), ((tokens, width), BF16)]
    return call(middle_kernel, outs, scratch, back, x, vec, lay["from_modes"], flops=lay["cost"], **lay["sizes"])


def apart(shape):
    return (shape[0] * shape[1] // 128, 128)


def spectral(got, one, two, vec, lay):
    shape = got.shape
    return call(spectral_kernel, [(shape, BF16)] * 5, [apart(shape), shape], got, lay["latitude"], one, two, vec, flops=4 * lay["cost"], per=lay["sizes"]["per"])


def spectral_back(got, one, two, slope, factor, lay):
    shape = got.shape
    return call(spectral_back_kernel, [(shape, BF16)] * 3, [apart(shape), shape], got, lay["latitude"], one, two, slope, factor, flops=4 * lay["cost"], per=lay["sizes"]["per"])


def spectral_grads(low, first, active, second, small, in_bias):
    width = low.shape[1]
    blocks = BLOCKS // 2
    outs = [((4 * width // 2, 128), BF16), ((G_ROWS, width), F32)]
    return call(spectral_grad_kernel, outs, [(width, width)], low, first, active, second, small, in_bias, flops=4 * low.shape[0] * width * width, blocks=blocks)


def matrices(place, own, other):
    _, blocks, size, _ = own[0].shape
    shape = (blocks * size, blocks * size)
    return call(matrices_kernel, [(shape, BF16)] * 4, [shape], place, *own, *other, scalars=1, blocks=blocks // 2)


def dense_specs(tokens, width, tile, level):
    whole = lambda shape: pl.BlockSpec(shape, lambda j, c: (0,) * len(shape))
    across = lambda count: pl.BlockSpec((count, tile), lambda j, c: (0, j))
    pick = lambda own: (lambda j, c: jnp.where((c[0] == level) == own, j, 0))
    wide = [pl.BlockSpec((width, tile), lambda j, c, own=own: (0, pick(own)(j, c))) for own in (True, False)]
    tall = [pl.BlockSpec((tile, width), lambda j, c, own=own: (pick(own)(j, c), 0)) for own in (True, False)]
    return whole, across, wide, tall


def dense(place, norm, mixed, pairs, vec, shape, level):
    tokens, width = norm.shape
    hidden = pairs[0][0].shape[1]
    tile = width
    whole, across, wide, tall = dense_specs(tokens, width, tile, level)
    return pl.pallas_call(
        functools.partial(dense_kernel, level=level),
        grid_spec=pltpu.PrefetchScalarGridSpec(
            num_scalar_prefetch=1,
            grid=(hidden // tile,),
            in_specs=[whole((tokens, width)), *wide, *tall, whole(vec.shape), whole((tokens, width))],
            out_specs=[whole(shape), across(tokens), across(tokens)],
            scratch_shapes=[pltpu.VMEM((tokens, width), F32), pltpu.VMEM((width, tile), BF16), pltpu.VMEM((tile, width), BF16)],
        ),
        out_shape=[
            jax.ShapeDtypeStruct(shape, BF16),
            jax.ShapeDtypeStruct((tokens, hidden), BF16),
            jax.ShapeDtypeStruct((tokens, hidden), BF16),
        ],
        compiler_params=pltpu.CompilerParams(vmem_limit_bytes=VMEM_BYTES),
        cost_estimate=pl.CostEstimate(flops=4 * tokens * width * hidden, bytes_accessed=30 << 20, transcendentals=tokens * hidden),
    )(place, norm, *pairs[0], *pairs[1], vec, mixed)


def dense_back(place, grad, pairs, slope, level):
    tokens, width = grad.shape
    hidden = pairs[0][0].shape[1]
    tile = width
    whole, across, wide, tall = dense_specs(tokens, width, tile, level)
    return pl.pallas_call(
        functools.partial(dense_back_kernel, level=level),
        grid_spec=pltpu.PrefetchScalarGridSpec(
            num_scalar_prefetch=1,
            grid=(hidden // tile,),
            in_specs=[whole((tokens, width)), *tall, across(tokens), *wide],
            out_specs=[across(tokens), whole((hidden // tile, tile)), whole((tokens, width))],
            scratch_shapes=[pltpu.VMEM((width, tile), BF16), pltpu.VMEM((tile, width), BF16)],
        ),
        out_shape=[
            jax.ShapeDtypeStruct((tokens, hidden), BF16),
            jax.ShapeDtypeStruct((hidden // tile, tile), F32),
            jax.ShapeDtypeStruct((tokens, width), F32),
        ],
        compiler_params=pltpu.CompilerParams(vmem_limit_bytes=VMEM_BYTES),
        cost_estimate=pl.CostEstimate(flops=4 * tokens * width * hidden, bytes_accessed=30 << 20, transcendentals=0),
    )(place, grad, *pairs[1], slope, *pairs[0])


def middle_back(grad_norm, mixed, grad, vec, lay):
    tokens, width = mixed.shape
    moved = (lay["modes"], width)
    outs = [(moved, BF16), ((tokens, width), F32), ((3, width), F32)]
    return call(middle_back_kernel, outs, [(tokens, width), moved], grad_norm, mixed, grad, vec, lay["to_modes_grad"], flops=lay["cost"], **lay["sizes"])


def front_back(back, grad_mixed, x, vec, known, lay):
    tokens, width = grad_mixed.shape
    scratch = [(lay["modes"], width), (lay["waves"], width), (tokens, width)]
    outs = [(x.shape, BF16), ((tokens, width), BF16), ((G_ROWS * width // 128, 128), BF16)]
    return call(front_back_kernel, outs, scratch, back, grad_mixed, x, vec, lay["from_modes_grad"], known, flops=lay["cost"], **lay["sizes"])


def first_shed(place, grad_in, grad_in_got, grad_out, grad_out_got):
    width, hidden = grad_in.shape
    rows = hidden // ROUTES // 4
    tall = width // rows
    wide = pl.BlockSpec((rows, width), lambda j, c: (jnp.where(c[0] == 1, j % tall, 0), jnp.where(c[0] == 1, j // tall, 0)))
    high = pl.BlockSpec((rows, width), lambda j, c: (jnp.where(c[0] == 0, j, 0), 0))

    def target(route, keep):
        def index(j, c):
            step = jnp.clip(j - 4 * route, 0, 3)
            upper = (c[2 + route] == 1) == keep
            return (jnp.where(upper, jnp.maximum(step - 2, 0), jnp.minimum(step, 1)), 0)

        return pl.BlockSpec((rows, width), index)

    outs = pl.pallas_call(
        first_shed_kernel,
        grid_spec=pltpu.PrefetchScalarGridSpec(
            num_scalar_prefetch=1,
            grid=(4 * ROUTES,),
            in_specs=[wide, wide, high, high],
            out_specs=[target(route, keep) for route in range(ROUTES) for keep in (False, True)],
        ),
        out_shape=[jax.ShapeDtypeStruct((2 * rows, width), BF16)] * (2 * ROUTES),
        compiler_params=pltpu.CompilerParams(vmem_limit_bytes=VMEM_BYTES),
        cost_estimate=pl.CostEstimate(flops=0, bytes_accessed=width * hidden, transcendentals=0),
    )(place, grad_in, grad_in_got, grad_out, grad_out_got)
    return outs[::2], outs[1::2]


def shed(bits, kept, got):
    rows, width = kept[0].shape
    outs = call(shed_kernel, [((rows // 2, width), BF16)] * (2 * len(kept)), [], bits, *kept, *got, scalars=1)
    return outs[: len(kept)], outs[len(kept) :]


def double(bits, own, got):
    _, rows, width = own[0].shape
    return call(double_kernel, [((2, 2 * rows, width), BF16)] * len(own), [], bits, *own, *got, scalars=1)


def finish(place, pieces, shape, other_side, kept=()):
    width, hidden = shape
    half = pieces[0].shape[1]
    rows = hidden // ROUTES // 4
    tall = width // rows
    per_half = half // rows
    steps = ROUTES * per_half

    def block(j, c):
        route = j // per_half
        side = sum(jnp.where(route == r, c[2 + r], 0) for r in range(ROUTES))
        side = 1 - side if other_side else side
        return (2 * route + side) * per_half + j % per_half

    def wide(p, j, c):
        at = block(jnp.where(p == 1, j, 0), c)
        return at % tall, at // tall

    piece = pl.BlockSpec((1, half, width), lambda p, j, c: (p, 0, 0))
    inputs = [piece] * ROUTES + [pl.BlockSpec(memory_space=pl.ANY)] * len(kept)
    return pl.pallas_call(
        functools.partial(finish_kernel, routes=ROUTES),
        grid_spec=pltpu.PrefetchScalarGridSpec(
            num_scalar_prefetch=1,
            grid=(2, steps),
            in_specs=inputs,
            out_specs=[
                pl.BlockSpec((rows, width), wide),
                pl.BlockSpec((rows, width), lambda p, j, c: (block(jnp.where(p == 0, j, steps - 1), c), 0)),
            ],
        ),
        out_shape=[jax.ShapeDtypeStruct((width, hidden), F32), jax.ShapeDtypeStruct((hidden, width), F32)],
        input_output_aliases={1 + ROUTES + i: i for i in range(len(kept))},
        compiler_params=pltpu.CompilerParams(vmem_limit_bytes=VMEM_BYTES),
        cost_estimate=pl.CostEstimate(flops=0, bytes_accessed=6 * width * hidden, transcendentals=0),
    )(place, *pieces, *kept)


def deliver(core, layer_zero, layer_one):
    return jnp.stack([jnp.where(core == 0, a, b) for a, b in zip(layer_zero, layer_one)])[None]


def after(item, *earlier):
    return lax.optimization_barrier((item, *earlier))[0]


def exchange(item):
    count = lax.axis_size("lane") * 2
    pieces = item.reshape(count, item.shape[0] // count, item.shape[1])
    return lax.all_to_all(pieces, ROWS_AXES, 0, 0, tiled=True).reshape(item.shape)


ROUTES = 3


def routes_of():
    bits = [1 << i for i in range(lax.axis_size("lane").bit_length() - 1)]
    turns = [route * len(bits) // ROUTES for route in range(ROUTES)]
    return [bits[turn:] + bits[:turn] for turn in turns]


def swap(item, bit):
    return lax.ppermute(item, "lane", [(i, i ^ bit) for i in range(lax.axis_size("lane"))])


def swap_all(items, at):
    return [swap(item, route[at]) for item, route in zip(items, routes_of())]


def stack(kept, got):
    rows, width = kept[0].shape
    return call(stack_kernel, [((ROUTES * rows, width), BF16)], [], *kept, *got)[0]


def across_halves(item):
    return lax.ppermute(item, "half", [(0, 1), (1, 0)])


def pack(place, one, one_got, two, two_got):
    rows, width = one.shape
    mine, give = call(add_kernel, [(one.shape, BF16)] * 2, [], place, one, one_got, two, two_got, scalars=1)
    got = lax.ppermute(give, "section", [(0, 1), (1, 0)])
    return mine, call(pack_kernel, [((2, rows // ROUTES, width), BF16)] * ROUTES, [], place, mine, got, scalars=1)


def small_sums(parts, core):
    slabs = lax.axis_size("lane") * lax.axis_size("half")
    count = sum(a.shape[0] for a in parts)
    each = -(-count // (slabs * 8)) * 8
    parts = [*parts, jnp.zeros((slabs * each - count, 128), BF16)]
    pieces = jnp.concatenate(parts, 0).reshape(slabs, each, 128)
    got = lax.all_to_all(pieces, SLAB, 0, 0, tiled=True)
    spread = call(small_sum_kernel, [(got.shape, BF16)], [], got)[0]
    total = lax.all_to_all(spread, SLAB, 0, 0, tiled=True).reshape(slabs * each, 128)
    return total, lax.ppermute(total, "section", [(0, 1), (1, 0)])


def fetch(pair, core, half):
    first = lax.ppermute(pair[1], ("section", "half"), [(0, 1)])
    second = lax.ppermute(pair[0], ("section", "half"), [(3, 2)])
    own = jnp.where(half == 0, pair[0], pair[1])
    return jnp.where(core == half, own, jnp.where(core == 0, first, second))


def send_out(item, level):
    return [lax.ppermute(item, ("section", "half"), [(micro, 2 * level), (2 + micro, 2 * level + 1)]) for micro in range(2)]


ACROSS = (((0,), (0,)), ((), ()))


def exchanged(items):
    return [(item, lax.ppermute(item, "section", [(0, 1), (1, 0)])) for item in items]


def shards(tokens, cotangent, *params):
    core = lax.axis_index("section")
    half = lax.axis_index("half")
    lane = lax.axis_index("lane")
    lanes = lax.axis_size("lane")
    _, rows, longitudes, width = tokens.shape
    total_rows = rows * lanes * 2
    fields = total_rows // LAT
    live = fields * LAT
    per = -(-(longitudes // 2 + 1) // lanes)
    forward_table, inverse_table = longitude_tables(longitudes, per * lanes)
    lay = {
        "to_modes": jnp.asarray(split_table(forward_table.T)),
        "from_modes": jnp.asarray(split_table(inverse_table)),
        "to_modes_grad": jnp.asarray(split_table(inverse_table.T)),
        "from_modes_grad": jnp.asarray(split_table(forward_table)),
        "latitude": jnp.asarray(split_table(latitude_table(total_rows, fields))),
        "modes": 2 * lanes * rows * per,
        "waves": 2 * lanes * per,
        "cost": 1 << 30,
        "sizes": {"rows": rows, "lanes": lanes, "per": per},
    }
    first_row = (core * lanes + lane) * rows
    live_rows = jnp.clip(live - first_row, 0, rows).astype(jnp.int32)
    blocks = BLOCKS // 2
    size = width // BLOCKS
    routes = routes_of()
    levels = len(routes[0])
    bits = [jnp.stack([((lane & route[at]) > 0).astype(jnp.int32) for route in routes]) for at in range(levels)]
    place = jnp.concatenate([jnp.stack([core.astype(jnp.int32), live_rows]), bits[0]])
    params = [item[0] for item in params]
    gain_one, shift_one, spectral_one, bias_one, spectral_two, bias_two, gain_two, shift_two, dense_in, in_bias, dense_out, out_bias = params
    x = fetch(tokens, core, half)
    vectors = [gain_one, shift_one, gain_two, shift_two, out_bias, in_bias, bias_one, bias_two]
    vectors = jnp.concatenate([a.reshape(-1, width) for a in vectors], 0)
    vectors, other = exchanged([vectors])[0]
    vectors = jnp.stack([jnp.where(core == 0, vectors, other), jnp.where(core == 0, other, vectors)]).astype(F32)
    mine = lax.dynamic_slice_in_dim(vectors[:, BIAS_ONE:], core * (width // 2), width // 2, 2).reshape(2, 2, width)
    vectors = jnp.concatenate([vectors[:, :BIAS_ONE], mine], 1)
    vec_one, vec_two = vectors[0], vectors[1]
    spectra = exchanged([spectral_one, spectral_two])
    one_a, two_a, one_b, two_b = matrices(place, [a for a, _ in spectra], [b for _, b in spectra])
    shape = x.shape

    got = exchange(front(x, vec_one, lay))
    dense_in, dense_out = after((dense_in, dense_out), got)
    pairs = exchanged([dense_in, dense_out])
    sent, low_one, active_one, slope_one, factor_one = spectral(got, one_a, two_a, vec_one, lay)
    got = exchange(sent)
    grad = fetch(after(cotangent, got), core, half)
    mixed_one, norm_one = middle(got, x, vec_one, lay)
    out_one, activated_one, bend_one = dense(place, norm_one, mixed_one, pairs, vec_one, shape, 0)
    grad = jnp.where(jnp.arange(rows, dtype=jnp.int32)[:, None, None] < live_rows, grad, jnp.zeros_like(grad))
    got = exchange(front(after(out_one, grad), vec_two, lay))
    grad = grad.reshape(-1, width)
    sent, low_two, active_two, slope_two, factor_two = spectral(got, one_b, two_b, vec_two, lay)
    got = exchange(sent)
    delivered_one = send_out(after(out_one, got), 0)
    mixed_two, norm_two = middle(got, out_one, vec_two, lay)
    out_two, activated_two, bend_two = dense(place, norm_two, mixed_two, pairs, vec_two, shape, 1)
    grad_hidden, in_bias_two, grad_norm = dense_back(place, after(grad, *delivered_one), pairs, bend_two, 1)
    sent, grad_mixed, small_two = middle_back(grad_norm, mixed_two, grad, vec_two, lay)
    got = exchange(sent)
    delivered_two = send_out(out_two, 1)
    norm_two, activated_two = after((norm_two, activated_two), sent)
    sums_two = (
        lax.dot_general(norm_two, grad_hidden, ACROSS, preferred_element_type=F32).astype(BF16),
        lax.dot_general(activated_two, grad, ACROSS, preferred_element_type=F32).astype(BF16),
    )
    from_two = (lax.ppermute(sums_two[0], "section", [(0, 1)]), lax.ppermute(sums_two[1], "section", [(1, 0)]))
    sent, grad_second, grad_first = spectral_back(after(got, *delivered_two, *sums_two), one_b, two_b, slope_two, factor_two, lay)
    got = exchange(sent)
    blocks_two, known = spectral_grads(low_two, grad_first, active_two, grad_second, small_two, in_bias_two)
    sums_two, from_two = after((sums_two, from_two), sent)
    sends_two, keeps_two = first_shed(place, sums_two[0], from_two[0], sums_two[1], from_two[1])
    gots_two = swap_all(sends_two, 0)
    activations = deliver(core, delivered_one, delivered_two)
    grad_x_two, grad, small_two = front_back(after(got, activations, *sends_two), grad_mixed, out_one, vec_two, known, lay)
    grads_two = send_out(grad_x_two, 1)
    grad_hidden, in_bias_one, grad_norm = dense_back(place, grad, pairs, bend_one, 0)
    sends_two, keeps_two = shed(bits[1], keeps_two, after(gots_two, grad_norm))
    gots_two = swap_all(sends_two, 1)
    sent, grad_mixed, small_one = middle_back(after(grad_norm, *sends_two), mixed_one, grad, vec_one, lay)
    got = exchange(sent)
    norm_one, activated_one = after((norm_one, activated_one), sent)
    norm_one = after(norm_one, *grads_two)
    grad_out = lax.dot_general(activated_one, grad, ACROSS, preferred_element_type=F32).astype(BF16)
    grad_out_got = lax.ppermute(grad_out, "section", [(1, 0)])
    grad_in = lax.dot_general(norm_one, grad_hidden, ACROSS, preferred_element_type=F32).astype(BF16)
    grad_in_got = lax.ppermute(grad_in, "section", [(0, 1)])
    for at in range(2, levels):
        sends_two, keeps_two = shed(bits[at], keeps_two, gots_two)
        gots_two = swap_all(sends_two, at)
    got = after(got, grad_in, grad_out, *sends_two)
    sent, grad_second, grad_first = spectral_back(got, one_a, two_a, slope_one, factor_one, lay)
    stacked_two = stack(keeps_two, after(gots_two, sent))
    halved_two = across_halves(stacked_two)
    grad_in, grad_in_got, grad_out, grad_out_got = after((grad_in, grad_in_got, grad_out, grad_out_got), sent)
    sends, keeps = first_shed(place, grad_in, grad_in_got, grad_out, grad_out_got)
    gots = swap_all(sends, 0)
    got = exchange(sent)
    blocks_one, known = spectral_grads(low_one, grad_first, active_one, grad_second, small_one, in_bias_one)
    grad_x_one, _, small_one = front_back(after(got, *sends), grad_mixed, x, vec_one, known, lay)
    gots = after(gots, grad_x_one)
    for at in range(1, levels):
        sends, keeps = shed(bits[at], keeps, gots)
        gots = swap_all(sends, at)
    stacked = stack(keeps, gots)
    mine, own = pack(place, stacked, across_halves(stacked), stacked_two, after(halved_two, stacked))
    grads_one = send_out(after(grad_x_one, mine), 0)
    for at in reversed(range(levels)):
        gots = swap_all(own, at)
        if at > 0:
            own = double(bits[at], own, gots)
    total, other = small_sums(after([blocks_one, blocks_two, small_one, small_two], mine), core)
    row = ((1, width), F32)
    outs = [((2, BLOCKS, size, size), F32)] * 2 + [((2, width), F32)] * 2 + [row] * 4 + [((4, width), F32), row]
    one, two, bias_one, bias_two, gain_one, shift_one, gain_two, shift_two, in_bias, out_bias = call(
        small_finish_kernel, outs, [(G_ROWS, width)] * 2, place, total, other, scalars=1, blocks=blocks
    )
    dense_grads = finish(place, own, dense_in.shape, False)
    grad_in, grad_out = finish(place, gots, dense_in.shape, True, dense_grads)
    return (
        activations, deliver(core, grads_one, grads_two),
        gain_one, shift_one, one[None], bias_one.reshape(1, 2, BLOCKS, size), two[None], bias_two.reshape(1, 2, BLOCKS, size),
        gain_two, shift_two, grad_in[None], in_bias.reshape(1, -1), grad_out[None], out_bias,
    )


def solution(mesh):
    devices = mesh.devices
    slabs = devices.shape[1]
    wide = Mesh(devices.reshape(2, 2, slabs // 2), ALL)
    rows = P(None, ("half", "lane"))
    own = P("section")
    return jax.shard_map(
        shards,
        mesh=wide,
        in_specs=(rows, rows) + (own,) * 12,
        out_specs=(P("section", None, ("half", "lane")),) * 2 + (own,) * 12,
        check_vma=False,
    )
```

```python
import functools
import math

import jax
import jax.numpy as jnp
import numpy as np
from jax import lax
from jax.experimental import pallas as pl
from jax.experimental.pallas import tpu as pltpu
from jax.sharding import Mesh, PartitionSpec as P

BLOCKS = 8
LAT = 90
EPSILON = 1e-05
SHRINK = 0.01
SOFTNESS = 0.1
ROWS_AXES = ("section", "lane")
ALL = ("section", "half", "lane")
SLAB = ("half", "lane")
F32 = jnp.float32
BF16 = jnp.bfloat16
VMEM_BYTES = 56 * 1024 * 1024
GAIN_ONE, SHIFT_ONE, GAIN_TWO, SHIFT_TWO, OUT_BIAS, IN_BIAS, BIAS_ONE, BIAS_TWO = 0, 1, 2, 3, 4, 5, 9, 10
G_GAIN_TWO, G_SHIFT_TWO, G_OUT_BIAS, G_IN_BIAS, G_BIAS_ONE, G_BIAS_TWO, G_GAIN_ONE, G_SHIFT_ONE, G_ROWS = 0, 1, 2, 3, 7, 8, 9, 10, 16


def split_table(table):
    high = np.asarray(table, np.float32).astype(jnp.bfloat16)
    low = (np.asarray(table, np.float64) - high.astype(np.float64)).astype(jnp.bfloat16)
    return np.concatenate([high, low], 0)


def longitude_tables(longitudes, padded):
    column = np.arange(longitudes)[:, None]
    frequency = np.arange(padded)[None, :]
    angle = (column * frequency % longitudes) * (2.0 * math.pi / longitudes)
    usable = (frequency <= longitudes // 2) / math.sqrt(longitudes)
    forward = np.concatenate([np.cos(angle) * usable, -np.sin(angle) * usable], 1)
    doubled = np.where((frequency == 0) | (frequency == longitudes // 2), 1.0, 2.0)
    inverse = forward * np.concatenate([doubled, doubled], 1)
    return (forward, inverse)


def latitude_table(rows, fields):
    index = np.arange(LAT)
    angle = (index[:, None] * index[None, :] % LAT) * (2.0 * math.pi / LAT)
    parts = []
    for wave in (np.cos(angle), np.sin(angle)):
        whole = np.zeros((rows, rows))
        for field in range(fields):
            span = slice(field * LAT, (field + 1) * LAT)
            whole[span, span] = wave / math.sqrt(LAT)
        parts.append(whole)
    return np.concatenate(parts, 0)


def dot(left, right):
    return jnp.dot(left, right, preferred_element_type=F32)


def dot_transposed(left, right):
    return lax.dot_general(left, right, (((1,), (1,)), ((), ())), preferred_element_type=F32)


def table_times_low(table_ref, low):
    count = table_ref.shape[0] // 2
    return dot(table_ref[:count, :], low) + dot(table_ref[count:, :], low)


def table_times(table_ref, value):
    count = table_ref.shape[0] // 2
    high = value.astype(BF16)
    rest = (value - high.astype(F32)).astype(BF16)
    return dot(table_ref[:count, :], high) + dot(table_ref[:count, :], rest) + dot(table_ref[count:, :], high)


def gelu_pair(value):
    size = jnp.abs(value) * math.sqrt(0.5)
    inverse = 1.0 / (1.0 + 0.3275911 * size)
    wave = jnp.exp(-0.5 * value * value)
    series = inverse * (0.254829592 + inverse * (-0.284496736 + inverse * (1.421413741 + inverse * (-1.453152027 + inverse * 1.061405429))))
    tail = 0.5 * series * wave
    share = jnp.where(value > 0, 1.0 - tail, tail)
    return value * share, share + value * wave * (1.0 / math.sqrt(2.0 * math.pi))


def row_of(vec_ref, at):
    return vec_ref[at : at + 1, :]


def centered(value):
    center = value - jnp.mean(value, axis=-1, keepdims=True)
    inverse = lax.rsqrt(jnp.mean(center * center, axis=-1, keepdims=True) + EPSILON)
    return center * inverse, inverse


def norm_back(grad, gain, unit, inverse):
    scaled = grad * gain
    return (scaled - jnp.mean(scaled, axis=-1, keepdims=True) - unit * jnp.mean(scaled * unit, axis=-1, keepdims=True)) * inverse


def scatter_modes(sent, spectrum, row, rows, lanes, per):
    width = spectrum.shape[1]
    half = width // 2
    modes = lanes * per
    for part in range(2):
        for lane in range(lanes):
            base = ((part * lanes + lane) * rows + row) * per
            for wave in range(2):
                piece = spectrum[wave * modes + lane * per : wave * modes + (lane + 1) * per, part * half : (part + 1) * half]
                sent[base : base + per, wave * half : (wave + 1) * half] = piece


def gather_modes(spectrum, back, row, rows, lanes, per):
    width = spectrum.shape[1]
    half = width // 2
    modes = lanes * per
    for part in range(2):
        for lane in range(lanes):
            base = ((part * lanes + lane) * rows + row) * per
            for wave in range(2):
                piece = back[base : base + per, wave * half : (wave + 1) * half]
                spectrum[wave * modes + lane * per : wave * modes + (lane + 1) * per, part * half : (part + 1) * half] = piece


def front_kernel(x_ref, vec_ref, table_ref, sent_ref, sent32, *, rows, lanes, per):
    for row in range(rows):
        unit, _ = centered(x_ref[row].astype(F32))
        spectrum = table_times(table_ref, unit * row_of(vec_ref, GAIN_ONE) + row_of(vec_ref, SHIFT_ONE))
        scatter_modes(sent32, spectrum, row, rows, lanes, per)
    sent_ref[...] = sent32[...].astype(BF16)


def middle_kernel(back_ref, x_ref, vec_ref, table_ref, mixed_ref, norm_ref, back32, spectrum, norm32, *, rows, lanes, per):
    back32[...] = back_ref[...].astype(F32)
    longs = x_ref.shape[1]
    for row in range(rows):
        span = slice(row * longs, (row + 1) * longs)
        gather_modes(spectrum, back32, row, rows, lanes, per)
        value = x_ref[row].astype(F32)
        unit, _ = centered(value)
        mixed = table_times_low(table_ref, spectrum[...].astype(BF16)) + (unit * row_of(vec_ref, GAIN_ONE) + row_of(vec_ref, SHIFT_ONE)) + value
        mixed_ref[span, :] = mixed
        unit, _ = centered(mixed)
        norm32[span, :] = unit * row_of(vec_ref, GAIN_TWO) + row_of(vec_ref, SHIFT_TWO)
    norm_ref[...] = norm32[...].astype(BF16)


def latitude_forward(table_ref, value, count):
    half = value.shape[1] // 2
    both = table_times_low(table_ref, value)
    cosine, sine = both[:count, :], both[count:, :]
    return cosine[:, :half] + sine[:, half:], cosine[:, half:] - sine[:, :half]


def latitude_inverse(table_ref, value, count):
    half = value.shape[1] // 2
    both = table_times(table_ref, value)
    cosine, sine = both[:count, :], both[count:, :]
    return cosine[:, :half] - sine[:, half:], cosine[:, half:] + sine[:, :half]


def strided_fill(apart, got_ref):
    total, width = got_ref.shape
    for tile in range(width // 128):
        apart[tile * total : (tile + 1) * total, :] = got_ref[:, tile * 128 : (tile + 1) * 128].astype(F32)


def strided_take(apart, mode, per, total, width):
    spans = [pl.ds(tile * total + mode, total // per, stride=per) for tile in range(width // 128)]
    return jnp.concatenate([apart[span, :] for span in spans], 1).astype(BF16)


def strided_put(apart, mode, per, total, first, value):
    for tile in range(value.shape[1] // 128):
        span = pl.ds((first + tile) * total + mode, total // per, stride=per)
        apart[span, :] = value[:, tile * 128 : (tile + 1) * 128]


def strided_send(sent_ref, apart):
    total, width = sent_ref.shape
    for tile in range(width // 128):
        sent_ref[:, tile * 128 : (tile + 1) * 128] = apart[tile * total : (tile + 1) * total, :].astype(BF16)


def chunk_of(total):
    return total // 3 if total % 48 == 0 else total


def spectral_kernel(got_ref, table_ref, one_ref, two_ref, vec_ref, sent_ref, low_ref, active_ref, slope_ref, factor_ref, got32, shrunk, *, per):
    total, width = got_ref.shape
    count, half = total // per, width // 2
    strided_fill(got32, got_ref)
    for mode in range(per):
        real, imag = latitude_forward(table_ref, strided_take(got32, mode, per, total, width), count)
        span = slice(mode * count, (mode + 1) * count)
        low_ref[span, :half] = real.astype(BF16)
        low_ref[span, half:] = imag.astype(BF16)
    chunk = chunk_of(total)

    @pl.loop(0, total // chunk)
    def _(step):
        span = pl.ds(pl.multiple_of(step * chunk, chunk), chunk)
        first = dot(low_ref[span, :], one_ref[...]) + row_of(vec_ref, BIAS_ONE)
        active, slope = gelu_pair(first)
        active = active.astype(BF16)
        active_ref[span, :] = active
        slope_ref[span, :] = slope.astype(BF16)
        second = dot(active, two_ref[...]) + row_of(vec_ref, BIAS_TWO)
        bend = jnp.tanh(second * (1.0 / SOFTNESS))
        shrunk[span, :] = second - SHRINK * bend
        factor_ref[span, :] = (1.0 - SHRINK / SOFTNESS * (1.0 - bend * bend)).astype(BF16)

    for mode in range(per):
        real, imag = latitude_inverse(table_ref, shrunk[mode * count : (mode + 1) * count, :], count)
        strided_put(got32, mode, per, total, 0, real)
        strided_put(got32, mode, per, total, half // 128, imag)
    strided_send(sent_ref, got32)


def spectral_back_kernel(got_ref, table_ref, one_ref, two_ref, slope_ref, factor_ref, sent_ref, second_ref, first_ref, got32, grad, *, per):
    total, width = got_ref.shape
    count, half = total // per, width // 2
    strided_fill(got32, got_ref)
    for mode in range(per):
        real, imag = latitude_forward(table_ref, strided_take(got32, mode, per, total, width), count)
        span = slice(mode * count, (mode + 1) * count)
        second_ref[span, :half] = (real * factor_ref[span, :half].astype(F32)).astype(BF16)
        second_ref[span, half:] = (imag * factor_ref[span, half:].astype(F32)).astype(BF16)
    chunk = chunk_of(total)

    @pl.loop(0, total // chunk)
    def _(step):
        span = pl.ds(pl.multiple_of(step * chunk, chunk), chunk)
        grad_active = dot_transposed(second_ref[span, :], two_ref[...])
        first = (grad_active * slope_ref[span, :].astype(F32)).astype(BF16)
        first_ref[span, :] = first
        grad[span, :] = dot_transposed(first, one_ref[...])

    for mode in range(per):
        real, imag = latitude_inverse(table_ref, grad[mode * count : (mode + 1) * count, :], count)
        strided_put(got32, mode, per, total, 0, real)
        strided_put(got32, mode, per, total, half // 128, imag)
    strided_send(sent_ref, got32)


def choose(place_ref, level, own_ref, other_ref, chosen):
    @pl.when(place_ref[0] == level)
    def _():
        chosen[...] = own_ref[...]

    @pl.when(place_ref[0] != level)
    def _():
        chosen[...] = other_ref[...]


def dense_kernel(place_ref, norm_ref, in_ref, in_other_ref, out_ref, out_other_ref, vec_ref, mixed_ref, result_ref, active_ref, slope_ref, total, in_kept, out_kept, *, level):
    step = pl.program_id(0)
    choose(place_ref, level, in_ref, in_other_ref, in_kept)
    choose(place_ref, level, out_ref, out_other_ref, out_kept)
    hidden = dot(norm_ref[...], in_kept[...]) + vec_ref[pl.ds(IN_BIAS + step, 1), :]
    active, slope = gelu_pair(hidden)
    active = active.astype(BF16)
    active_ref[...] = active
    slope_ref[...] = slope.astype(BF16)
    part = dot(active, out_kept[...])

    @pl.when(step == 0)
    def _():
        total[...] = part + mixed_ref[...] + row_of(vec_ref, OUT_BIAS)

    @pl.when(step > 0)
    def _():
        total[...] += part

    @pl.when(step == pl.num_programs(0) - 1)
    def _():
        rows, longs, _ = result_ref.shape
        for row in range(rows):
            value = total[row * longs : (row + 1) * longs, :]
            result_ref[row] = jnp.where(row < place_ref[1], value, 0.0).astype(BF16)


def dense_back_kernel(place_ref, grad_ref, out_ref, out_other_ref, slope_ref, in_ref, in_other_ref, hidden_ref, bias_ref, norm_ref, in_kept, out_kept, *, level):
    step = pl.program_id(0)
    choose(place_ref, level, in_ref, in_other_ref, in_kept)
    choose(place_ref, level, out_ref, out_other_ref, out_kept)
    grad_active = dot_transposed(grad_ref[...], out_kept[...])
    hidden = (grad_active * slope_ref[...].astype(F32)).astype(BF16)
    hidden_ref[...] = hidden
    bias_ref[pl.ds(step, 1), :] = jnp.sum(hidden.astype(F32), axis=0, keepdims=True)
    part = dot_transposed(hidden, in_kept[...])

    @pl.when(step == 0)
    def _():
        norm_ref[...] = part

    @pl.when(step > 0)
    def _():
        norm_ref[...] += part


def middle_back_kernel(norm_ref, mixed_ref, grad_ref, vec_ref, table_ref, sent_ref, grad_mixed_ref, small_ref, grad32, sent32, *, rows, lanes, per):
    grad32[...] = grad_ref[...].astype(F32)
    longs = mixed_ref.shape[0] // rows
    gain_grad = shift_grad = bias_grad = 0.0
    for row in range(rows):
        span = slice(row * longs, (row + 1) * longs)
        unit, inverse = centered(mixed_ref[span, :])
        grad_norm = norm_ref[span, :]
        grad_out = grad32[span, :]
        grad_mixed = norm_back(grad_norm, row_of(vec_ref, GAIN_TWO), unit, inverse) + grad_out
        gain_grad += jnp.sum(grad_norm * unit, axis=0, keepdims=True)
        shift_grad += jnp.sum(grad_norm, axis=0, keepdims=True)
        bias_grad += jnp.sum(grad_out, axis=0, keepdims=True)
        grad_mixed_ref[span, :] = grad_mixed
        scatter_modes(sent32, table_times(table_ref, grad_mixed), row, rows, lanes, per)
    small_ref[0:1, :] = gain_grad
    small_ref[1:2, :] = shift_grad
    small_ref[2:3, :] = bias_grad
    sent_ref[...] = sent32[...].astype(BF16)


def front_back_kernel(back_ref, grad_mixed_ref, x_ref, vec_ref, table_ref, known_ref, grad_ref, flat_ref, small_ref, back32, spectrum, flat32, *, rows, lanes, per):
    back32[...] = back_ref[...].astype(F32)
    longs = x_ref.shape[1]
    gain_grad = shift_grad = 0.0
    for row in range(rows):
        span = slice(row * longs, (row + 1) * longs)
        gather_modes(spectrum, back32, row, rows, lanes, per)
        grad_mixed = grad_mixed_ref[span, :]
        grad_normed = table_times_low(table_ref, spectrum[...].astype(BF16)) + grad_mixed
        unit, inverse = centered(x_ref[row].astype(F32))
        gain_grad += jnp.sum(grad_normed * unit, axis=0, keepdims=True)
        shift_grad += jnp.sum(grad_normed, axis=0, keepdims=True)
        grad = norm_back(grad_normed, row_of(vec_ref, GAIN_ONE), unit, inverse) + grad_mixed
        flat32[span, :] = grad
        grad_ref[row] = grad.astype(BF16)
    known = known_ref[...]
    index = lax.broadcasted_iota(jnp.int32, known.shape, 0)
    known = jnp.where(index == G_GAIN_ONE, gain_grad, jnp.where(index == G_SHIFT_ONE, shift_grad, known))
    for tile in range(known.shape[1] // 128):
        small_ref[tile * G_ROWS : (tile + 1) * G_ROWS, :] = known[:, tile * 128 : (tile + 1) * 128].astype(BF16)
    flat_ref[...] = flat32[...].astype(BF16)


def spectral_grad_kernel(low_ref, first_ref, active_ref, second_ref, small_ref, in_bias_ref, blocks_ref, known_ref, outer, *, blocks):
    half = outer.shape[0] // 2
    size = half // blocks
    blocks_ref[...] = jnp.zeros_like(blocks_ref)
    for which, (left, right) in enumerate(((low_ref, first_ref), (active_ref, second_ref))):
        outer[...] = lax.dot_general(left[...], right[...], (((0,), (0,)), ((), ())), preferred_element_type=F32)
        for block in range(blocks):
            up, down = slice(block * size, (block + 1) * size), slice(half + block * size, half + (block + 1) * size)
            at = (which * 2 * blocks + block) * size
            blocks_ref[at : at + size, :size] = (outer[up, up] + outer[down, down]).astype(BF16)
            at += blocks * size
            blocks_ref[at : at + size, :size] = (outer[up, down] - outer[down, up]).astype(BF16)
    known_ref[...] = jnp.zeros_like(known_ref)
    known_ref[G_GAIN_TWO : G_OUT_BIAS + 1, :] = small_ref[...]
    known_ref[G_IN_BIAS : G_IN_BIAS + 4, :] = in_bias_ref[...]
    known_ref[G_BIAS_ONE : G_BIAS_ONE + 1, :] = jnp.sum(first_ref[...].astype(F32), axis=0, keepdims=True)
    known_ref[G_BIAS_TWO : G_BIAS_TWO + 1, :] = jnp.sum(second_ref[...].astype(F32), axis=0, keepdims=True)


def matrices_kernel(place_ref, own_one_ref, own_two_ref, other_one_ref, other_two_ref, one_a_ref, two_a_ref, one_b_ref, two_b_ref, whole, *, blocks):
    core = place_ref[0]
    size = own_one_ref.shape[-1]
    half = blocks * size

    def build(source, target):
        whole[...] = jnp.zeros_like(whole)
        for block in range(blocks):
            real = source[0, core * blocks + block].astype(F32)
            imag = source[1, core * blocks + block].astype(F32)
            up, down = slice(block * size, (block + 1) * size), slice(half + block * size, half + (block + 1) * size)
            whole[up, up] = real
            whole[up, down] = imag
            whole[down, up] = -imag
            whole[down, down] = real
        target[...] = whole[...].astype(BF16)

    for level, targets in enumerate(((one_a_ref, two_a_ref), (one_b_ref, two_b_ref))):

        @pl.when(core == level)
        def _(targets=targets):
            build(own_one_ref, targets[0])
            build(own_two_ref, targets[1])

        @pl.when(core != level)
        def _(targets=targets):
            build(other_one_ref, targets[0])
            build(other_two_ref, targets[1])


def first_shed_kernel(place_ref, in_ref, in_got_ref, out_ref, out_got_ref, *targets):
    step = pl.program_id(0)
    for core, (mine, got) in enumerate(((out_ref, out_got_ref), (in_ref, in_got_ref))):

        @pl.when(place_ref[0] == core)
        def _(mine=mine, got=got):
            total = (mine[...].astype(F32) + got[...].astype(F32)).astype(BF16)
            for route in range(len(targets) // 2):
                keeps = (step // 2) % 2 == place_ref[2 + route]

                @pl.when((step // 4 == route) & keeps)
                def _(route=route, total=total):
                    targets[2 * route + 1][...] = total

                @pl.when((step // 4 == route) & jnp.logical_not(keeps))
                def _(route=route, total=total):
                    targets[2 * route][...] = total


def shed_kernel(bits_ref, *refs):
    count = len(refs) // 4
    kept, got, sends, keeps = (refs[i * count : (i + 1) * count] for i in range(4))
    for at in range(count):
        half = sends[at].shape[0]
        for target, bit in ((keeps[at], bits_ref[at]), (sends[at], 1 - bits_ref[at])):
            span = pl.ds(pl.multiple_of(bit * half, half), half)
            target[...] = (kept[at][span, :].astype(F32) + got[at][span, :].astype(F32)).astype(BF16)


def stack_kernel(*refs):
    *sources, target = refs
    count = len(sources) // 2
    rows = sources[0].shape[0]
    for at in range(count):
        target[at * rows : (at + 1) * rows, :] = (sources[at][...].astype(F32) + sources[count + at][...].astype(F32)).astype(BF16)


def add_kernel(place_ref, one_ref, one_got_ref, two_ref, two_got_ref, mine_ref, give_ref):
    for core, (first, second) in enumerate(((mine_ref, give_ref), (give_ref, mine_ref))):

        @pl.when(place_ref[0] == core)
        def _(first=first, second=second):
            first[...] = (one_ref[...].astype(F32) + one_got_ref[...].astype(F32)).astype(BF16)
            second[...] = (two_ref[...].astype(F32) + two_got_ref[...].astype(F32)).astype(BF16)


def pack_kernel(place_ref, mine_ref, got_ref, *targets):
    for core, (first, second) in enumerate(((mine_ref, got_ref), (got_ref, mine_ref))):

        @pl.when(place_ref[0] == core)
        def _(first=first, second=second):
            for at, target in enumerate(targets):
                rows = target.shape[1]
                target[0] = first[at * rows : (at + 1) * rows, :]
                target[1] = second[at * rows : (at + 1) * rows, :]


def double_kernel(bits_ref, *refs):
    count = len(refs) // 3
    own, got, targets = (refs[i * count : (i + 1) * count] for i in range(3))
    for at in range(count):
        rows = own[at].shape[1]
        for source, bit in ((own[at], bits_ref[at]), (got[at], 1 - bits_ref[at])):
            targets[at][:, pl.ds(pl.multiple_of(bit * rows, rows), rows), :] = source[...]


def finish_kernel(place_ref, *refs, routes):
    sources, (in_grad_ref, out_grad_ref) = refs[:routes], refs[-2:]
    part, step = pl.program_id(0), pl.program_id(1)
    rows = out_grad_ref.shape[0]
    per_half = sources[0].shape[1] // rows
    span = pl.ds(pl.multiple_of((step % per_half) * rows, rows), rows)
    for route in range(routes):
        for which, target in enumerate((out_grad_ref, in_grad_ref)):

            @pl.when((step // per_half == route) & (part == which))
            def _(target=target, source=sources[route]):
                target[...] = source[0, span, :].astype(F32)


def small_sum_kernel(got_ref, spread_ref):
    total = jnp.sum(got_ref[...].astype(F32), axis=0).astype(BF16)
    for at in range(spread_ref.shape[0]):
        spread_ref[at] = total


def small_finish_kernel(place_ref, own_ref, other_ref, one_ref, two_ref, bias_one_ref, bias_two_ref, gain_one_ref, shift_one_ref, gain_two_ref, shift_two_ref, in_bias_ref, out_bias_ref, vec, vec_other, *, blocks):
    core = place_ref[0]
    size = one_ref.shape[-1]
    matrix_rows = 4 * blocks * size
    tiles = vec.shape[1] // 128
    for which, target in enumerate((one_ref, two_ref)):
        for wave in range(2):
            for block in range(blocks):
                at = core * matrix_rows + ((which * 2 + wave) * blocks + block) * size
                span = pl.ds(pl.multiple_of(at, 32), size)
                target[wave, core * blocks + block] = own_ref[span, :].astype(F32)[:, :size]
                target[wave, (1 - core) * blocks + block] = other_ref[span, :].astype(F32)[:, :size]
    for source, target in ((own_ref, vec), (other_ref, vec_other)):
        for tile in range(tiles):
            at = 2 * matrix_rows + (core * tiles + tile) * G_ROWS
            target[:, tile * 128 : (tile + 1) * 128] = source[pl.ds(pl.multiple_of(at, G_ROWS), G_ROWS), :].astype(F32)
    half = vec.shape[1] // 2
    for row, target in ((G_BIAS_ONE, bias_one_ref), (G_BIAS_TWO, bias_two_ref)):
        for wave in range(2):
            for source, place in ((vec, core), (vec_other, 1 - core)):
                target[wave : wave + 1, pl.ds(pl.multiple_of(place * half, 128), half)] = source[row : row + 1, wave * half : (wave + 1) * half]
    total = vec[...] + vec_other[...]
    for row, target in ((G_GAIN_ONE, gain_one_ref), (G_SHIFT_ONE, shift_one_ref), (G_GAIN_TWO, gain_two_ref), (G_SHIFT_TWO, shift_two_ref), (G_OUT_BIAS, out_bias_ref)):
        target[...] = total[row : row + 1, :]
    in_bias_ref[...] = total[G_IN_BIAS : G_IN_BIAS + 4, :]


def call(body, outs, scratch, *args, flops=0, scalars=0, **named):
    bytes_moved = sum(a.size * a.dtype.itemsize for a in args) + sum(math.prod(s) * np.dtype(d).itemsize for s, d in outs)
    return pl.pallas_call(
        functools.partial(body, **named),
        out_shape=[jax.ShapeDtypeStruct(s, d) for s, d in outs],
        in_specs=[pl.BlockSpec(memory_space=pltpu.SMEM if i < scalars else pltpu.VMEM) for i in range(len(args))],
        out_specs=[pl.BlockSpec(memory_space=pltpu.VMEM)] * len(outs),
        scratch_shapes=[pltpu.VMEM(s, F32) for s in scratch],
        compiler_params=pltpu.CompilerParams(vmem_limit_bytes=VMEM_BYTES),
        cost_estimate=pl.CostEstimate(flops=flops, bytes_accessed=bytes_moved if flops else bytes_moved // 8, transcendentals=0),
    )(*args)


def front(x, vec, lay):
    moved = (lay["modes"], x.shape[2])
    return call(front_kernel, [(moved, BF16)], [moved], x, vec, lay["to_modes"], flops=lay["cost"], **lay["sizes"])[0]


def middle(back, x, vec, lay):
    tokens, width = x.shape[0] * x.shape[1], x.shape[2]
    scratch = [(lay["modes"], width), (lay["waves"], width), (tokens, width)]
    outs = [((tokens, width), F32), ((tokens, width), BF16)]
    return call(middle_kernel, outs, scratch, back, x, vec, lay["from_modes"], flops=lay["cost"], **lay["sizes"])


def apart(shape):
    return (shape[0] * shape[1] // 128, 128)


def spectral(got, one, two, vec, lay):
    shape = got.shape
    return call(spectral_kernel, [(shape, BF16)] * 5, [apart(shape), shape], got, lay["latitude"], one, two, vec, flops=4 * lay["cost"], per=lay["sizes"]["per"])


def spectral_back(got, one, two, slope, factor, lay):
    shape = got.shape
    return call(spectral_back_kernel, [(shape, BF16)] * 3, [apart(shape), shape], got, lay["latitude"], one, two, slope, factor, flops=4 * lay["cost"], per=lay["sizes"]["per"])


def spectral_grads(low, first, active, second, small, in_bias):
    width = low.shape[1]
    blocks = BLOCKS // 2
    outs = [((4 * width // 2, 128), BF16), ((G_ROWS, width), F32)]
    return call(spectral_grad_kernel, outs, [(width, width)], low, first, active, second, small, in_bias, flops=4 * low.shape[0] * width * width, blocks=blocks)


def matrices(place, own, other):
    _, blocks, size, _ = own[0].shape
    shape = (blocks * size, blocks * size)
    return call(matrices_kernel, [(shape, BF16)] * 4, [shape], place, *own, *other, scalars=1, blocks=blocks // 2)


def dense_specs(tokens, width, tile, level):
    whole = lambda shape: pl.BlockSpec(shape, lambda j, c: (0,) * len(shape))
    across = lambda count: pl.BlockSpec((count, tile), lambda j, c: (0, j))
    pick = lambda own: (lambda j, c: jnp.where((c[0] == level) == own, j, 0))
    wide = [pl.BlockSpec((width, tile), lambda j, c, own=own: (0, pick(own)(j, c))) for own in (True, False)]
    tall = [pl.BlockSpec((tile, width), lambda j, c, own=own: (pick(own)(j, c), 0)) for own in (True, False)]
    return whole, across, wide, tall


def dense(place, norm, mixed, pairs, vec, shape, level):
    tokens, width = norm.shape
    hidden = pairs[0][0].shape[1]
    tile = width
    whole, across, wide, tall = dense_specs(tokens, width, tile, level)
    return pl.pallas_call(
        functools.partial(dense_kernel, level=level),
        grid_spec=pltpu.PrefetchScalarGridSpec(
            num_scalar_prefetch=1,
            grid=(hidden // tile,),
            in_specs=[whole((tokens, width)), *wide, *tall, whole(vec.shape), whole((tokens, width))],
            out_specs=[whole(shape), across(tokens), across(tokens)],
            scratch_shapes=[pltpu.VMEM((tokens, width), F32), pltpu.VMEM((width, tile), BF16), pltpu.VMEM((tile, width), BF16)],
        ),
        out_shape=[
            jax.ShapeDtypeStruct(shape, BF16),
            jax.ShapeDtypeStruct((tokens, hidden), BF16),
            jax.ShapeDtypeStruct((tokens, hidden), BF16),
        ],
        compiler_params=pltpu.CompilerParams(vmem_limit_bytes=VMEM_BYTES),
        cost_estimate=pl.CostEstimate(flops=4 * tokens * width * hidden, bytes_accessed=30 << 20, transcendentals=tokens * hidden),
    )(place, norm, *pairs[0], *pairs[1], vec, mixed)


def dense_back(place, grad, pairs, slope, level):
    tokens, width = grad.shape
    hidden = pairs[0][0].shape[1]
    tile = width
    whole, across, wide, tall = dense_specs(tokens, width, tile, level)
    return pl.pallas_call(
        functools.partial(dense_back_kernel, level=level),
        grid_spec=pltpu.PrefetchScalarGridSpec(
            num_scalar_prefetch=1,
            grid=(hidden // tile,),
            in_specs=[whole((tokens, width)), *tall, across(tokens), *wide],
            out_specs=[across(tokens), whole((hidden // tile, tile)), whole((tokens, width))],
            scratch_shapes=[pltpu.VMEM((width, tile), BF16), pltpu.VMEM((tile, width), BF16)],
        ),
        out_shape=[
            jax.ShapeDtypeStruct((tokens, hidden), BF16),
            jax.ShapeDtypeStruct((hidden // tile, tile), F32),
            jax.ShapeDtypeStruct((tokens, width), F32),
        ],
        compiler_params=pltpu.CompilerParams(vmem_limit_bytes=VMEM_BYTES),
        cost_estimate=pl.CostEstimate(flops=4 * tokens * width * hidden, bytes_accessed=30 << 20, transcendentals=0),
    )(place, grad, *pairs[1], slope, *pairs[0])


def middle_back(grad_norm, mixed, grad, vec, lay):
    tokens, width = mixed.shape
    moved = (lay["modes"], width)
    outs = [(moved, BF16), ((tokens, width), F32), ((3, width), F32)]
    return call(middle_back_kernel, outs, [(tokens, width), moved], grad_norm, mixed, grad, vec, lay["to_modes_grad"], flops=lay["cost"], **lay["sizes"])


def front_back(back, grad_mixed, x, vec, known, lay):
    tokens, width = grad_mixed.shape
    scratch = [(lay["modes"], width), (lay["waves"], width), (tokens, width)]
    outs = [(x.shape, BF16), ((tokens, width), BF16), ((G_ROWS * width // 128, 128), BF16)]
    return call(front_back_kernel, outs, scratch, back, grad_mixed, x, vec, lay["from_modes_grad"], known, flops=lay["cost"], **lay["sizes"])


def first_shed(place, grad_in, grad_in_got, grad_out, grad_out_got):
    width, hidden = grad_in.shape
    rows = hidden // ROUTES // 4
    tall = width // rows
    wide = pl.BlockSpec((rows, width), lambda j, c: (jnp.where(c[0] == 1, j % tall, 0), jnp.where(c[0] == 1, j // tall, 0)))
    high = pl.BlockSpec((rows, width), lambda j, c: (jnp.where(c[0] == 0, j, 0), 0))

    def target(route, keep):
        def index(j, c):
            step = jnp.clip(j - 4 * route, 0, 3)
            upper = (c[2 + route] == 1) == keep
            return (jnp.where(upper, jnp.maximum(step - 2, 0), jnp.minimum(step, 1)), 0)

        return pl.BlockSpec((rows, width), index)

    outs = pl.pallas_call(
        first_shed_kernel,
        grid_spec=pltpu.PrefetchScalarGridSpec(
            num_scalar_prefetch=1,
            grid=(4 * ROUTES,),
            in_specs=[wide, wide, high, high],
            out_specs=[target(route, keep) for route in range(ROUTES) for keep in (False, True)],
        ),
        out_shape=[jax.ShapeDtypeStruct((2 * rows, width), BF16)] * (2 * ROUTES),
        compiler_params=pltpu.CompilerParams(vmem_limit_bytes=VMEM_BYTES),
        cost_estimate=pl.CostEstimate(flops=0, bytes_accessed=width * hidden, transcendentals=0),
    )(place, grad_in, grad_in_got, grad_out, grad_out_got)
    return outs[::2], outs[1::2]


def shed(bits, kept, got):
    rows, width = kept[0].shape
    outs = call(shed_kernel, [((rows // 2, width), BF16)] * (2 * len(kept)), [], bits, *kept, *got, scalars=1)
    return outs[: len(kept)], outs[len(kept) :]


def double(bits, own, got):
    _, rows, width = own[0].shape
    return call(double_kernel, [((2, 2 * rows, width), BF16)] * len(own), [], bits, *own, *got, scalars=1)


def finish(place, pieces, shape, other_side, kept=()):
    width, hidden = shape
    half = pieces[0].shape[1]
    rows = hidden // ROUTES // 4
    tall = width // rows
    per_half = half // rows
    steps = ROUTES * per_half

    def block(j, c):
        route = j // per_half
        side = sum(jnp.where(route == r, c[2 + r], 0) for r in range(ROUTES))
        side = 1 - side if other_side else side
        return (2 * route + side) * per_half + j % per_half

    def wide(p, j, c):
        at = block(jnp.where(p == 1, j, 0), c)
        return at % tall, at // tall

    piece = pl.BlockSpec((1, half, width), lambda p, j, c: (p, 0, 0))
    inputs = [piece] * ROUTES + [pl.BlockSpec(memory_space=pl.ANY)] * len(kept)
    return pl.pallas_call(
        functools.partial(finish_kernel, routes=ROUTES),
        grid_spec=pltpu.PrefetchScalarGridSpec(
            num_scalar_prefetch=1,
            grid=(2, steps),
            in_specs=inputs,
            out_specs=[
                pl.BlockSpec((rows, width), wide),
                pl.BlockSpec((rows, width), lambda p, j, c: (block(jnp.where(p == 0, j, steps - 1), c), 0)),
            ],
        ),
        out_shape=[jax.ShapeDtypeStruct((width, hidden), F32), jax.ShapeDtypeStruct((hidden, width), F32)],
        input_output_aliases={1 + ROUTES + i: i for i in range(len(kept))},
        compiler_params=pltpu.CompilerParams(vmem_limit_bytes=VMEM_BYTES),
        cost_estimate=pl.CostEstimate(flops=0, bytes_accessed=6 * width * hidden, transcendentals=0),
    )(place, *pieces, *kept)


def deliver(core, half, layer_zero, layer_one):
    first, second = (list(parts[:2]) for parts in (layer_zero, layer_one))
    for level, (parts, whole) in enumerate(((first, layer_zero), (second, layer_one))):
        parts[level] = jnp.where(half == level, whole[2], parts[level])
    return jnp.stack([jnp.where(core == 0, a, b) for a, b in zip(first, second)])[None]


def after(item, *earlier):
    return lax.optimization_barrier((item, *earlier))[0]


def together(*items):
    return lax.optimization_barrier(items)


def exchange(item):
    count = lax.axis_size("lane") * 2
    pieces = item.reshape(count, item.shape[0] // count, item.shape[1])
    return lax.all_to_all(pieces, ROWS_AXES, 0, 0, tiled=True).reshape(item.shape)


ROUTES = 3


def routes_of():
    bits = [1 << i for i in range(lax.axis_size("lane").bit_length() - 1)]
    turns = [route * len(bits) // ROUTES for route in range(ROUTES)]
    return [bits[turn:] + bits[:turn] for turn in turns]


def swap(item, bit):
    return lax.ppermute(item, "lane", [(i, i ^ bit) for i in range(lax.axis_size("lane"))])


def swap_all(items, at):
    return [swap(item, route[at]) for item, route in zip(items, routes_of())]


def stack(kept, got):
    rows, width = kept[0].shape
    return call(stack_kernel, [((ROUTES * rows, width), BF16)], [], *kept, *got)[0]


def across_halves(item):
    return lax.ppermute(item, "half", [(0, 1), (1, 0)])


def pack(place, one, one_got, two, two_got):
    rows, width = one.shape
    mine, give = call(add_kernel, [(one.shape, BF16)] * 2, [], place, one, one_got, two, two_got, scalars=1)
    got = lax.ppermute(give, "section", [(0, 1), (1, 0)])
    return mine, call(pack_kernel, [((2, rows // ROUTES, width), BF16)] * ROUTES, [], place, mine, got, scalars=1)


def small_sums(parts, earlier):
    slabs = lax.axis_size("lane") * lax.axis_size("half")
    count = sum(a.shape[0] for a in parts)
    each = -(-count // (slabs * 8)) * 8
    parts = [*parts, jnp.zeros((slabs * each - count, 128), BF16)]
    pieces = jnp.concatenate(parts, 0).reshape(slabs, each, 128)
    got = after(lax.all_to_all(pieces, SLAB, 0, 0, tiled=True), *earlier)
    spread = call(small_sum_kernel, [(got.shape, BF16)], [], got)[0]
    total = lax.all_to_all(spread, SLAB, 0, 0, tiled=True).reshape(slabs * each, 128)
    return total, lax.ppermute(total, "section", [(0, 1), (1, 0)])


def fetch(pair, core, half):
    first = lax.ppermute(pair[1], ("section", "half"), [(0, 1)])
    second = lax.ppermute(pair[0], ("section", "half"), [(3, 2)])
    own = jnp.where(half == 0, pair[0], pair[1])
    return jnp.where(core == half, own, jnp.where(core == 0, first, second))


def send_out(item, level):
    pairs = lambda micro: [(2 * side + micro, 2 * level + side) for side in range(2)]
    return [lax.ppermute(item, ("section", "half"), [p for p in pairs(micro) if p[0] != p[1]]) for micro in range(2)] + [item]


ACROSS = (((0,), (0,)), ((), ()))


def exchanged(items):
    return [(item, lax.ppermute(item, "section", [(0, 1), (1, 0)])) for item in items]


def shards(tokens, cotangent, *params):
    core = lax.axis_index("section")
    half = lax.axis_index("half")
    lane = lax.axis_index("lane")
    lanes = lax.axis_size("lane")
    _, rows, longitudes, width = tokens.shape
    total_rows = rows * lanes * 2
    fields = total_rows // LAT
    live = fields * LAT
    per = -(-(longitudes // 2 + 1) // lanes)
    forward_table, inverse_table = longitude_tables(longitudes, per * lanes)
    lay = {
        "to_modes": jnp.asarray(split_table(forward_table.T)),
        "from_modes": jnp.asarray(split_table(inverse_table)),
        "to_modes_grad": jnp.asarray(split_table(inverse_table.T)),
        "from_modes_grad": jnp.asarray(split_table(forward_table)),
        "latitude": jnp.asarray(split_table(latitude_table(total_rows, fields))),
        "modes": 2 * lanes * rows * per,
        "waves": 2 * lanes * per,
        "cost": 1 << 30,
        "sizes": {"rows": rows, "lanes": lanes, "per": per},
    }
    first_row = (core * lanes + lane) * rows
    live_rows = jnp.clip(live - first_row, 0, rows).astype(jnp.int32)
    blocks = BLOCKS // 2
    size = width // BLOCKS
    routes = routes_of()
    levels = len(routes[0])
    bits = [jnp.stack([((lane & route[at]) > 0).astype(jnp.int32) for route in routes]) for at in range(levels)]
    place = jnp.concatenate([jnp.stack([core.astype(jnp.int32), live_rows]), bits[0]])
    params = [item[0] for item in params]
    gain_one, shift_one, spectral_one, bias_one, spectral_two, bias_two, gain_two, shift_two, dense_in, in_bias, dense_out, out_bias = params
    x = fetch(tokens, core, half)
    vectors = [gain_one, shift_one, gain_two, shift_two, out_bias, in_bias, bias_one, bias_two]
    vectors = jnp.concatenate([a.reshape(-1, width) for a in vectors], 0)
    vectors, other = exchanged([vectors])[0]
    vectors = jnp.stack([jnp.where(core == 0, vectors, other), jnp.where(core == 0, other, vectors)]).astype(F32)
    mine = lax.dynamic_slice_in_dim(vectors[:, BIAS_ONE:], core * (width // 2), width // 2, 2).reshape(2, 2, width)
    vectors = jnp.concatenate([vectors[:, :BIAS_ONE], mine], 1)
    vec_one, vec_two = vectors[0], vectors[1]
    spectra = exchanged([spectral_one, spectral_two])
    one_a, two_a, one_b, two_b = matrices(place, [a for a, _ in spectra], [b for _, b in spectra])
    shape = x.shape

    got = exchange(front(x, vec_one, lay))
    dense_in, dense_out = after((dense_in, dense_out), got)
    pairs = exchanged([dense_in, dense_out])
    sent, low_one, active_one, slope_one, factor_one = spectral(got, one_a, two_a, vec_one, lay)
    got = exchange(sent)
    grad = fetch(after(cotangent, got), core, half)
    mixed_one, norm_one = middle(got, x, vec_one, lay)
    out_one, activated_one, bend_one = dense(place, norm_one, mixed_one, pairs, vec_one, shape, 0)
    grad = jnp.where(jnp.arange(rows, dtype=jnp.int32)[:, None, None] < live_rows, grad, jnp.zeros_like(grad))
    got = exchange(front(after(out_one, grad), vec_two, lay))
    grad = grad.reshape(-1, width)
    sent, low_two, active_two, slope_two, factor_two = spectral(got, one_b, two_b, vec_two, lay)
    got = exchange(sent)
    delivered_one = send_out(after(out_one, got), 0)
    mixed_two, norm_two = middle(got, out_one, vec_two, lay)
    out_two, activated_two, bend_two = dense(place, norm_two, mixed_two, pairs, vec_two, shape, 1)
    grad_hidden, in_bias_two, grad_norm = dense_back(place, after(grad, *delivered_one), pairs, bend_two, 1)
    sent, grad_mixed, small_two = middle_back(grad_norm, mixed_two, grad, vec_two, lay)
    got = exchange(sent)
    delivered_two = send_out(out_two, 1)
    norm_two, activated_two = after((norm_two, activated_two), sent)
    sums_two = (
        lax.dot_general(norm_two, grad_hidden, ACROSS, preferred_element_type=F32).astype(BF16),
        lax.dot_general(activated_two, grad, ACROSS, preferred_element_type=F32).astype(BF16),
    )
    from_two = (lax.ppermute(sums_two[0], "section", [(0, 1)]), lax.ppermute(sums_two[1], "section", [(1, 0)]))
    sent, grad_second, grad_first = spectral_back(after(got, *delivered_two, *sums_two), one_b, two_b, slope_two, factor_two, lay)
    got = exchange(sent)
    blocks_two, known = spectral_grads(low_two, grad_first, active_two, grad_second, small_two, in_bias_two)
    sums_two, from_two = after((sums_two, from_two), sent)
    sends_two, keeps_two = first_shed(place, sums_two[0], from_two[0], sums_two[1], from_two[1])
    gots_two = swap_all(sends_two, 0)
    activations = deliver(core, half, delivered_one, delivered_two)
    grad_x_two, grad, small_two = front_back(after(got, activations, *sends_two), grad_mixed, out_one, vec_two, known, lay)
    grads_two = send_out(grad_x_two, 1)
    grad_hidden, in_bias_one, grad_norm = dense_back(place, grad, pairs, bend_one, 0)
    sends_two, keeps_two = shed(bits[1], keeps_two, after(gots_two, grad_norm))
    gots_two = swap_all(sends_two, 1)
    sent, grad_mixed, small_one = middle_back(after(grad_norm, *sends_two), mixed_one, grad, vec_one, lay)
    got = exchange(sent)
    norm_one, activated_one = after((norm_one, activated_one), sent, *gots_two)
    norm_one = after(norm_one, *grads_two)
    grad_out = lax.dot_general(activated_one, grad, ACROSS, preferred_element_type=F32).astype(BF16)
    grad_in = lax.dot_general(norm_one, grad_hidden, ACROSS, preferred_element_type=F32).astype(BF16)
    for at in range(2, levels):
        sends_two, keeps_two = shed(bits[at], keeps_two, gots_two)
        gots_two = swap_all(sends_two, at)
    got = after(got, grad_in, grad_out, *sends_two)
    grad_in, grad_out = after((grad_in, grad_out), *sends_two)
    grad_out_got = lax.ppermute(grad_out, "section", [(1, 0)])
    grad_in_got = lax.ppermute(grad_in, "section", [(0, 1)])
    sent, grad_second, grad_first = spectral_back(got, one_a, two_a, slope_one, factor_one, lay)
    sent, gots_two = together(sent, gots_two)
    stacked_two = stack(keeps_two, gots_two)
    halved_two = across_halves(stacked_two)
    grad_in, grad_in_got, grad_out, grad_out_got = after((grad_in, grad_in_got, grad_out, grad_out_got), sent, stacked_two)
    sends, keeps = first_shed(place, grad_in, grad_in_got, grad_out, grad_out_got)
    gots = swap_all(sends, 0)
    got = exchange(sent)
    blocks_one, known = spectral_grads(low_one, grad_first, active_one, grad_second, small_one, in_bias_one)
    grad_x_one, _, small_one = front_back(after(got, *sends), grad_mixed, x, vec_one, known, lay)
    gots = after(gots, grad_x_one, halved_two)
    for at in range(1, levels):
        sends, keeps = shed(bits[at], keeps, gots)
        gots = swap_all(sends, at)
    stacked = stack(keeps, gots)
    mine, own = pack(place, stacked, across_halves(stacked), stacked_two, after(halved_two, stacked))
    grads_one = send_out(after(grad_x_one, mine), 0)
    for at in reversed(range(levels)):
        gots = swap_all(own, at)
        if at > 0:
            own = double(bits[at], own, after(gots, *grads_one) if at == 1 else gots)
    total, other = small_sums([blocks_one, blocks_two, small_one, small_two], [stacked])
    row = ((1, width), F32)
    outs = [((2, BLOCKS, size, size), F32)] * 2 + [((2, width), F32)] * 2 + [row] * 4 + [((4, width), F32), row]
    one, two, bias_one, bias_two, gain_one, shift_one, gain_two, shift_two, in_bias, out_bias = call(
        small_finish_kernel, outs, [(G_ROWS, width)] * 2, place, total, other, scalars=1, blocks=blocks
    )
    dense_grads = finish(place, own, dense_in.shape, False)
    input_grads = deliver(core, half, grads_one, grads_two)
    bias_one, bias_two, in_bias = bias_one.reshape(1, 2, BLOCKS, size), bias_two.reshape(1, 2, BLOCKS, size), in_bias.reshape(1, -1)
    gots = after(gots, input_grads, bias_one, bias_two, in_bias, gain_one)
    grad_in, grad_out = finish(place, gots, dense_in.shape, True, dense_grads)
    return (
        activations, input_grads, gain_one, shift_one, one[None], bias_one, two[None], bias_two,
        gain_two, shift_two, grad_in[None], in_bias, grad_out[None], out_bias,
    )


def solution(mesh):
    devices = mesh.devices
    slabs = devices.shape[1]
    wide = Mesh(devices.reshape(2, 2, slabs // 2), ALL)
    rows = P(None, ("half", "lane"))
    own = P("section")
    return jax.shard_map(
        shards,
        mesh=wide,
        in_specs=(rows, rows) + (own,) * 12,
        out_specs=(P("section", None, ("half", "lane")),) * 2 + (own,) * 12,
        check_vma=False,
    )
```

```python
import functools
import math

import jax
import jax.numpy as jnp
import numpy as np
from jax import lax
from jax.experimental import pallas as pl
from jax.experimental.pallas import tpu as pltpu
from jax.sharding import Mesh, PartitionSpec as P

BLOCKS = 8
LAT = 90
EPSILON = 1e-05
SHRINK = 0.01
SOFTNESS = 0.1
ROWS_AXES = ("section", "lane")
ALL = ("section", "half", "lane")
SLAB = ("half", "lane")
F32 = jnp.float32
BF16 = jnp.bfloat16
VMEM_BYTES = 56 * 1024 * 1024
GAIN_ONE, SHIFT_ONE, GAIN_TWO, SHIFT_TWO, OUT_BIAS, IN_BIAS, BIAS_ONE, BIAS_TWO = 0, 1, 2, 3, 4, 5, 9, 10
G_GAIN_TWO, G_SHIFT_TWO, G_OUT_BIAS, G_IN_BIAS, G_BIAS_ONE, G_BIAS_TWO, G_GAIN_ONE, G_SHIFT_ONE, G_ROWS = 0, 1, 2, 3, 7, 8, 9, 10, 16


def split_table(table):
    high = np.asarray(table, np.float32).astype(jnp.bfloat16)
    low = (np.asarray(table, np.float64) - high.astype(np.float64)).astype(jnp.bfloat16)
    return np.concatenate([high, low], 0)


def longitude_tables(longitudes, padded):
    column = np.arange(longitudes)[:, None]
    frequency = np.arange(padded)[None, :]
    angle = (column * frequency % longitudes) * (2.0 * math.pi / longitudes)
    usable = (frequency <= longitudes // 2) / math.sqrt(longitudes)
    forward = np.concatenate([np.cos(angle) * usable, -np.sin(angle) * usable], 1)
    doubled = np.where((frequency == 0) | (frequency == longitudes // 2), 1.0, 2.0)
    inverse = forward * np.concatenate([doubled, doubled], 1)
    return (forward, inverse)


def latitude_table(rows, fields):
    index = np.arange(LAT)
    angle = (index[:, None] * index[None, :] % LAT) * (2.0 * math.pi / LAT)
    parts = []
    for wave in (np.cos(angle), np.sin(angle)):
        whole = np.zeros((rows, rows))
        for field in range(fields):
            span = slice(field * LAT, (field + 1) * LAT)
            whole[span, span] = wave / math.sqrt(LAT)
        parts.append(whole)
    return np.concatenate(parts, 0)


def dot(left, right):
    return jnp.dot(left, right, preferred_element_type=F32)


def dot_transposed(left, right):
    return lax.dot_general(left, right, (((1,), (1,)), ((), ())), preferred_element_type=F32)


def both_parts(table_ref, value):
    count = table_ref.shape[0] // 2
    if count % 16:
        return dot(table_ref[:count, :], value) + dot(table_ref[count:, :], value)
    full = dot(table_ref[...], value)
    return full[:count, :] + full[count:, :]


def table_times_low(table_ref, low):
    return both_parts(table_ref, low)


def table_times(table_ref, value):
    count = table_ref.shape[0] // 2
    high = value.astype(BF16)
    rest = (value - high.astype(F32)).astype(BF16)
    return both_parts(table_ref, high) + dot(table_ref[:count, :], rest)


def gelu_pair(value):
    size = jnp.abs(value) * math.sqrt(0.5)
    inverse = 1.0 / (1.0 + 0.3275911 * size)
    wave = jnp.exp(-0.5 * value * value)
    series = inverse * (0.254829592 + inverse * (-0.284496736 + inverse * (1.421413741 + inverse * (-1.453152027 + inverse * 1.061405429))))
    tail = 0.5 * series * wave
    share = jnp.where(value > 0, 1.0 - tail, tail)
    return value * share, share + value * wave * (1.0 / math.sqrt(2.0 * math.pi))


def row_of(vec_ref, at):
    return vec_ref[at : at + 1, :]


def centered(value):
    center = value - jnp.mean(value, axis=-1, keepdims=True)
    inverse = lax.rsqrt(jnp.mean(center * center, axis=-1, keepdims=True) + EPSILON)
    return center * inverse, inverse


def norm_back(grad, gain, unit, inverse):
    scaled = grad * gain
    return (scaled - jnp.mean(scaled, axis=-1, keepdims=True) - unit * jnp.mean(scaled * unit, axis=-1, keepdims=True)) * inverse


def scatter_modes(sent, spectrum, row, rows, lanes, per):
    width = spectrum.shape[1]
    half = width // 2
    modes = lanes * per
    for part in range(2):
        for lane in range(lanes):
            base = ((part * lanes + lane) * rows + row) * per
            for wave in range(2):
                piece = spectrum[wave * modes + lane * per : wave * modes + (lane + 1) * per, part * half : (part + 1) * half]
                sent[base : base + per, wave * half : (wave + 1) * half] = piece


def gather_modes(spectrum, back, row, rows, lanes, per):
    width = spectrum.shape[1]
    half = width // 2
    modes = lanes * per
    for part in range(2):
        for lane in range(lanes):
            base = ((part * lanes + lane) * rows + row) * per
            for wave in range(2):
                piece = back[base : base + per, wave * half : (wave + 1) * half]
                spectrum[wave * modes + lane * per : wave * modes + (lane + 1) * per, part * half : (part + 1) * half] = piece


def front_kernel(x_ref, vec_ref, table_ref, sent_ref, sent32, *, rows, lanes, per):
    for row in range(rows):
        unit, _ = centered(x_ref[row].astype(F32))
        spectrum = table_times(table_ref, unit * row_of(vec_ref, GAIN_ONE) + row_of(vec_ref, SHIFT_ONE))
        scatter_modes(sent32, spectrum, row, rows, lanes, per)
    sent_ref[...] = sent32[...].astype(BF16)


def middle_kernel(back_ref, x_ref, vec_ref, table_ref, mixed_ref, norm_ref, back32, spectrum, norm32, *, rows, lanes, per):
    back32[...] = back_ref[...].astype(F32)
    longs = x_ref.shape[1]
    for row in range(rows):
        span = slice(row * longs, (row + 1) * longs)
        gather_modes(spectrum, back32, row, rows, lanes, per)
        value = x_ref[row].astype(F32)
        unit, _ = centered(value)
        mixed = table_times_low(table_ref, spectrum[...].astype(BF16)) + (unit * row_of(vec_ref, GAIN_ONE) + row_of(vec_ref, SHIFT_ONE)) + value
        mixed_ref[span, :] = mixed
        unit, _ = centered(mixed)
        norm32[span, :] = unit * row_of(vec_ref, GAIN_TWO) + row_of(vec_ref, SHIFT_TWO)
    norm_ref[...] = norm32[...].astype(BF16)


def latitude_forward(table_ref, value, count):
    half = value.shape[1] // 2
    both = table_times_low(table_ref, value)
    cosine, sine = both[:count, :], both[count:, :]
    return cosine[:, :half] + sine[:, half:], cosine[:, half:] - sine[:, :half]


def latitude_inverse(table_ref, value, count):
    half = value.shape[1] // 2
    both = table_times(table_ref, value)
    cosine, sine = both[:count, :], both[count:, :]
    return cosine[:, :half] - sine[:, half:], cosine[:, half:] + sine[:, :half]


def strided_fill(apart, got_ref):
    total, width = got_ref.shape
    for tile in range(width // 128):
        apart[tile * total : (tile + 1) * total, :] = got_ref[:, tile * 128 : (tile + 1) * 128].astype(F32)


def strided_take(apart, mode, per, total, width):
    spans = [pl.ds(tile * total + mode, total // per, stride=per) for tile in range(width // 128)]
    return jnp.concatenate([apart[span, :] for span in spans], 1).astype(BF16)


def strided_put(apart, mode, per, total, first, value):
    for tile in range(value.shape[1] // 128):
        span = pl.ds((first + tile) * total + mode, total // per, stride=per)
        apart[span, :] = value[:, tile * 128 : (tile + 1) * 128]


def strided_send(sent_ref, apart):
    total, width = sent_ref.shape
    for tile in range(width // 128):
        sent_ref[:, tile * 128 : (tile + 1) * 128] = apart[tile * total : (tile + 1) * total, :].astype(BF16)


def chunk_of(total):
    return total // 3 if total % 48 == 0 else total


def spectral_kernel(got_ref, table_ref, one_ref, two_ref, vec_ref, sent_ref, low_ref, active_ref, slope_ref, factor_ref, got32, shrunk, *, per):
    total, width = got_ref.shape
    count, half = total // per, width // 2
    strided_fill(got32, got_ref)
    for mode in range(per):
        real, imag = latitude_forward(table_ref, strided_take(got32, mode, per, total, width), count)
        span = slice(mode * count, (mode + 1) * count)
        low_ref[span, :half] = real.astype(BF16)
        low_ref[span, half:] = imag.astype(BF16)
    chunk = chunk_of(total)

    @pl.loop(0, total // chunk)
    def _(step):
        span = pl.ds(pl.multiple_of(step * chunk, chunk), chunk)
        first = dot(low_ref[span, :], one_ref[...]) + row_of(vec_ref, BIAS_ONE)
        active, slope = gelu_pair(first)
        active = active.astype(BF16)
        active_ref[span, :] = active
        slope_ref[span, :] = slope.astype(BF16)
        second = dot(active, two_ref[...]) + row_of(vec_ref, BIAS_TWO)
        bend = jnp.tanh(second * (1.0 / SOFTNESS))
        shrunk[span, :] = second - SHRINK * bend
        factor_ref[span, :] = (1.0 - SHRINK / SOFTNESS * (1.0 - bend * bend)).astype(BF16)

    for mode in range(per):
        real, imag = latitude_inverse(table_ref, shrunk[mode * count : (mode + 1) * count, :], count)
        strided_put(got32, mode, per, total, 0, real)
        strided_put(got32, mode, per, total, half // 128, imag)
    strided_send(sent_ref, got32)


def spectral_back_kernel(got_ref, table_ref, one_ref, two_ref, slope_ref, factor_ref, sent_ref, second_ref, first_ref, got32, grad, *, per):
    total, width = got_ref.shape
    count, half = total // per, width // 2
    strided_fill(got32, got_ref)
    for mode in range(per):
        real, imag = latitude_forward(table_ref, strided_take(got32, mode, per, total, width), count)
        span = slice(mode * count, (mode + 1) * count)
        second_ref[span, :half] = (real * factor_ref[span, :half].astype(F32)).astype(BF16)
        second_ref[span, half:] = (imag * factor_ref[span, half:].astype(F32)).astype(BF16)
    chunk = chunk_of(total)

    @pl.loop(0, total // chunk)
    def _(step):
        span = pl.ds(pl.multiple_of(step * chunk, chunk), chunk)
        grad_active = dot_transposed(second_ref[span, :], two_ref[...])
        first = (grad_active * slope_ref[span, :].astype(F32)).astype(BF16)
        first_ref[span, :] = first
        grad[span, :] = dot_transposed(first, one_ref[...])

    for mode in range(per):
        real, imag = latitude_inverse(table_ref, grad[mode * count : (mode + 1) * count, :], count)
        strided_put(got32, mode, per, total, 0, real)
        strided_put(got32, mode, per, total, half // 128, imag)
    strided_send(sent_ref, got32)


def choose(place_ref, level, own_ref, other_ref, chosen):
    @pl.when(place_ref[0] == level)
    def _():
        chosen[...] = own_ref[...]

    @pl.when(place_ref[0] != level)
    def _():
        chosen[...] = other_ref[...]


def dense_kernel(place_ref, norm_ref, in_ref, in_other_ref, out_ref, out_other_ref, vec_ref, mixed_ref, result_ref, active_ref, slope_ref, total, in_kept, out_kept, *, level):
    step = pl.program_id(0)
    choose(place_ref, level, in_ref, in_other_ref, in_kept)
    choose(place_ref, level, out_ref, out_other_ref, out_kept)
    tokens = norm_ref.shape[0]
    middle = -(-tokens // 32) * 16
    for span in (slice(0, middle), slice(middle, tokens)):
        hidden = dot(norm_ref[span, :], in_kept[...]) + vec_ref[pl.ds(IN_BIAS + step, 1), :]
        active, slope = gelu_pair(hidden)
        active = active.astype(BF16)
        active_ref[span, :] = active
        slope_ref[span, :] = slope.astype(BF16)
        before = jnp.where(step == 0, mixed_ref[span, :] + row_of(vec_ref, OUT_BIAS), total[span, :])
        total[span, :] = before + dot(active, out_kept[...])

    @pl.when(step == pl.num_programs(0) - 1)
    def _():
        rows, longs, _ = result_ref.shape
        for row in range(rows):
            value = total[row * longs : (row + 1) * longs, :]
            result_ref[row] = jnp.where(row < place_ref[1], value, 0.0).astype(BF16)


def dense_back_kernel(place_ref, grad_ref, out_ref, out_other_ref, slope_ref, in_ref, in_other_ref, hidden_ref, bias_ref, norm_ref, in_kept, out_kept, *, level):
    step = pl.program_id(0)
    choose(place_ref, level, in_ref, in_other_ref, in_kept)
    choose(place_ref, level, out_ref, out_other_ref, out_kept)
    grad_active = dot_transposed(grad_ref[...], out_kept[...])
    hidden = (grad_active * slope_ref[...].astype(F32)).astype(BF16)
    hidden_ref[...] = hidden
    bias_ref[pl.ds(step, 1), :] = jnp.sum(hidden.astype(F32), axis=0, keepdims=True)
    part = dot_transposed(hidden, in_kept[...])

    @pl.when(step == 0)
    def _():
        norm_ref[...] = part

    @pl.when(step > 0)
    def _():
        norm_ref[...] += part


def middle_back_kernel(norm_ref, mixed_ref, grad_ref, vec_ref, table_ref, sent_ref, grad_mixed_ref, small_ref, grad32, sent32, *, rows, lanes, per):
    grad32[...] = grad_ref[...].astype(F32)
    longs = mixed_ref.shape[0] // rows
    gain_grad = shift_grad = bias_grad = 0.0
    for row in range(rows):
        span = slice(row * longs, (row + 1) * longs)
        unit, inverse = centered(mixed_ref[span, :])
        grad_norm = norm_ref[span, :]
        grad_out = grad32[span, :]
        grad_mixed = norm_back(grad_norm, row_of(vec_ref, GAIN_TWO), unit, inverse) + grad_out
        gain_grad += jnp.sum(grad_norm * unit, axis=0, keepdims=True)
        shift_grad += jnp.sum(grad_norm, axis=0, keepdims=True)
        bias_grad += jnp.sum(grad_out, axis=0, keepdims=True)
        grad_mixed_ref[span, :] = grad_mixed
        scatter_modes(sent32, table_times(table_ref, grad_mixed), row, rows, lanes, per)
    small_ref[0:1, :] = gain_grad
    small_ref[1:2, :] = shift_grad
    small_ref[2:3, :] = bias_grad
    sent_ref[...] = sent32[...].astype(BF16)


def front_back_kernel(back_ref, grad_mixed_ref, x_ref, vec_ref, table_ref, known_ref, grad_ref, flat_ref, small_ref, back32, spectrum, flat32, *, rows, lanes, per):
    back32[...] = back_ref[...].astype(F32)
    longs = x_ref.shape[1]
    gain_grad = shift_grad = 0.0
    for row in range(rows):
        span = slice(row * longs, (row + 1) * longs)
        gather_modes(spectrum, back32, row, rows, lanes, per)
        grad_mixed = grad_mixed_ref[span, :]
        grad_normed = table_times_low(table_ref, spectrum[...].astype(BF16)) + grad_mixed
        unit, inverse = centered(x_ref[row].astype(F32))
        gain_grad += jnp.sum(grad_normed * unit, axis=0, keepdims=True)
        shift_grad += jnp.sum(grad_normed, axis=0, keepdims=True)
        grad = norm_back(grad_normed, row_of(vec_ref, GAIN_ONE), unit, inverse) + grad_mixed
        flat32[span, :] = grad
        grad_ref[row] = grad.astype(BF16)
    known = known_ref[...]
    index = lax.broadcasted_iota(jnp.int32, known.shape, 0)
    known = jnp.where(index == G_GAIN_ONE, gain_grad, jnp.where(index == G_SHIFT_ONE, shift_grad, known))
    for tile in range(known.shape[1] // 128):
        small_ref[tile * G_ROWS : (tile + 1) * G_ROWS, :] = known[:, tile * 128 : (tile + 1) * 128].astype(BF16)
    flat_ref[...] = flat32[...].astype(BF16)


def spectral_grad_kernel(low_ref, first_ref, active_ref, second_ref, small_ref, in_bias_ref, blocks_ref, known_ref, outer, *, blocks):
    half = outer.shape[0] // 2
    size = half // blocks
    blocks_ref[...] = jnp.zeros_like(blocks_ref)
    for which, (left, right) in enumerate(((low_ref, first_ref), (active_ref, second_ref))):
        outer[...] = lax.dot_general(left[...], right[...], (((0,), (0,)), ((), ())), preferred_element_type=F32)
        for block in range(blocks):
            up, down = slice(block * size, (block + 1) * size), slice(half + block * size, half + (block + 1) * size)
            at = (which * 2 * blocks + block) * size
            blocks_ref[at : at + size, :size] = (outer[up, up] + outer[down, down]).astype(BF16)
            at += blocks * size
            blocks_ref[at : at + size, :size] = (outer[up, down] - outer[down, up]).astype(BF16)
    known_ref[...] = jnp.zeros_like(known_ref)
    known_ref[G_GAIN_TWO : G_OUT_BIAS + 1, :] = small_ref[...]
    known_ref[G_IN_BIAS : G_IN_BIAS + 4, :] = in_bias_ref[...]
    known_ref[G_BIAS_ONE : G_BIAS_ONE + 1, :] = jnp.sum(first_ref[...].astype(F32), axis=0, keepdims=True)
    known_ref[G_BIAS_TWO : G_BIAS_TWO + 1, :] = jnp.sum(second_ref[...].astype(F32), axis=0, keepdims=True)


def matrices_kernel(place_ref, own_one_ref, own_two_ref, other_one_ref, other_two_ref, one_a_ref, two_a_ref, one_b_ref, two_b_ref, whole, *, blocks):
    core = place_ref[0]
    size = own_one_ref.shape[-1]
    half = blocks * size

    def build(source, target):
        whole[...] = jnp.zeros_like(whole)
        for block in range(blocks):
            real = source[0, core * blocks + block].astype(F32)
            imag = source[1, core * blocks + block].astype(F32)
            up, down = slice(block * size, (block + 1) * size), slice(half + block * size, half + (block + 1) * size)
            whole[up, up] = real
            whole[up, down] = imag
            whole[down, up] = -imag
            whole[down, down] = real
        target[...] = whole[...].astype(BF16)

    for level, targets in enumerate(((one_a_ref, two_a_ref), (one_b_ref, two_b_ref))):

        @pl.when(core == level)
        def _(targets=targets):
            build(own_one_ref, targets[0])
            build(own_two_ref, targets[1])

        @pl.when(core != level)
        def _(targets=targets):
            build(other_one_ref, targets[0])
            build(other_two_ref, targets[1])


def first_shed_kernel(place_ref, in_ref, in_got_ref, out_ref, out_got_ref, *targets):
    step = pl.program_id(0)
    for core, (mine, got) in enumerate(((out_ref, out_got_ref), (in_ref, in_got_ref))):

        @pl.when(place_ref[0] == core)
        def _(mine=mine, got=got):
            total = (mine[...].astype(F32) + got[...].astype(F32)).astype(BF16)
            for route in range(len(targets) // 2):
                keeps = (step // 2) % 2 == place_ref[2 + route]

                @pl.when((step // 4 == route) & keeps)
                def _(route=route, total=total):
                    targets[2 * route + 1][...] = total

                @pl.when((step // 4 == route) & jnp.logical_not(keeps))
                def _(route=route, total=total):
                    targets[2 * route][...] = total


def shed_kernel(bits_ref, *refs):
    count = len(refs) // 4
    kept, got, sends, keeps = (refs[i * count : (i + 1) * count] for i in range(4))
    for at in range(count):
        half = sends[at].shape[0]
        for target, bit in ((keeps[at], bits_ref[at]), (sends[at], 1 - bits_ref[at])):
            span = pl.ds(pl.multiple_of(bit * half, half), half)
            target[...] = (kept[at][span, :].astype(F32) + got[at][span, :].astype(F32)).astype(BF16)


def stack_kernel(*refs):
    *sources, target = refs
    count = len(sources) // 2
    rows = sources[0].shape[0]
    for at in range(count):
        target[at * rows : (at + 1) * rows, :] = (sources[at][...].astype(F32) + sources[count + at][...].astype(F32)).astype(BF16)


def add_kernel(place_ref, one_ref, one_got_ref, two_ref, two_got_ref, mine_ref, give_ref):
    for core, (first, second) in enumerate(((mine_ref, give_ref), (give_ref, mine_ref))):

        @pl.when(place_ref[0] == core)
        def _(first=first, second=second):
            first[...] = (one_ref[...].astype(F32) + one_got_ref[...].astype(F32)).astype(BF16)
            second[...] = (two_ref[...].astype(F32) + two_got_ref[...].astype(F32)).astype(BF16)


def pack_kernel(place_ref, mine_ref, got_ref, *targets):
    for core, (first, second) in enumerate(((mine_ref, got_ref), (got_ref, mine_ref))):

        @pl.when(place_ref[0] == core)
        def _(first=first, second=second):
            for at, target in enumerate(targets):
                rows = target.shape[1]
                target[0] = first[at * rows : (at + 1) * rows, :]
                target[1] = second[at * rows : (at + 1) * rows, :]


def double_kernel(bits_ref, *refs):
    count = len(refs) // 3
    own, got, targets = (refs[i * count : (i + 1) * count] for i in range(3))
    for at in range(count):
        rows = own[at].shape[1]
        for source, bit in ((own[at], bits_ref[at]), (got[at], 1 - bits_ref[at])):
            targets[at][:, pl.ds(pl.multiple_of(bit * rows, rows), rows), :] = source[...]


def finish_kernel(place_ref, *refs, routes):
    sources, (in_grad_ref, out_grad_ref) = refs[:routes], refs[-2:]
    part, step = pl.program_id(0), pl.program_id(1)
    rows = out_grad_ref.shape[0]
    per_half = sources[0].shape[1] // rows
    span = pl.ds(pl.multiple_of((step % per_half) * rows, rows), rows)
    for route in range(routes):
        for which, target in enumerate((out_grad_ref, in_grad_ref)):

            @pl.when((step // per_half == route) & (part == which))
            def _(target=target, source=sources[route]):
                target[...] = source[0, span, :].astype(F32)


def small_sum_kernel(got_ref, spread_ref):
    total = jnp.sum(got_ref[...].astype(F32), axis=0).astype(BF16)
    for at in range(spread_ref.shape[0]):
        spread_ref[at] = total


def small_finish_kernel(place_ref, own_ref, other_ref, one_ref, two_ref, bias_one_ref, bias_two_ref, gain_one_ref, shift_one_ref, gain_two_ref, shift_two_ref, in_bias_ref, out_bias_ref, vec, vec_other, *, blocks):
    core = place_ref[0]
    size = one_ref.shape[-1]
    matrix_rows = 4 * blocks * size
    tiles = vec.shape[1] // 128
    for which, target in enumerate((one_ref, two_ref)):
        for wave in range(2):
            for block in range(blocks):
                at = core * matrix_rows + ((which * 2 + wave) * blocks + block) * size
                span = pl.ds(pl.multiple_of(at, 32), size)
                target[wave, core * blocks + block] = own_ref[span, :].astype(F32)[:, :size]
                target[wave, (1 - core) * blocks + block] = other_ref[span, :].astype(F32)[:, :size]
    for source, target in ((own_ref, vec), (other_ref, vec_other)):
        for tile in range(tiles):
            at = 2 * matrix_rows + (core * tiles + tile) * G_ROWS
            target[:, tile * 128 : (tile + 1) * 128] = source[pl.ds(pl.multiple_of(at, G_ROWS), G_ROWS), :].astype(F32)
    half = vec.shape[1] // 2
    for row, target in ((G_BIAS_ONE, bias_one_ref), (G_BIAS_TWO, bias_two_ref)):
        for wave in range(2):
            for source, place in ((vec, core), (vec_other, 1 - core)):
                target[wave : wave + 1, pl.ds(pl.multiple_of(place * half, 128), half)] = source[row : row + 1, wave * half : (wave + 1) * half]
    total = vec[...] + vec_other[...]
    for row, target in ((G_GAIN_ONE, gain_one_ref), (G_SHIFT_ONE, shift_one_ref), (G_GAIN_TWO, gain_two_ref), (G_SHIFT_TWO, shift_two_ref), (G_OUT_BIAS, out_bias_ref)):
        target[...] = total[row : row + 1, :]
    in_bias_ref[...] = total[G_IN_BIAS : G_IN_BIAS + 4, :]


def call(body, outs, scratch, *args, flops=0, scalars=0, **named):
    bytes_moved = sum(a.size * a.dtype.itemsize for a in args) + sum(math.prod(s) * np.dtype(d).itemsize for s, d in outs)
    return pl.pallas_call(
        functools.partial(body, **named),
        out_shape=[jax.ShapeDtypeStruct(s, d) for s, d in outs],
        in_specs=[pl.BlockSpec(memory_space=pltpu.SMEM if i < scalars else pltpu.VMEM) for i in range(len(args))],
        out_specs=[pl.BlockSpec(memory_space=pltpu.VMEM)] * len(outs),
        scratch_shapes=[pltpu.VMEM(s, F32) for s in scratch],
        compiler_params=pltpu.CompilerParams(vmem_limit_bytes=VMEM_BYTES),
        cost_estimate=pl.CostEstimate(flops=flops, bytes_accessed=bytes_moved if flops else bytes_moved // 8, transcendentals=0),
    )(*args)


def front(x, vec, lay):
    moved = (lay["modes"], x.shape[2])
    return call(front_kernel, [(moved, BF16)], [moved], x, vec, lay["to_modes"], flops=lay["cost"], **lay["sizes"])[0]


def middle(back, x, vec, lay):
    tokens, width = x.shape[0] * x.shape[1], x.shape[2]
    scratch = [(lay["modes"], width), (lay["waves"], width), (tokens, width)]
    outs = [((tokens, width), F32), ((tokens, width), BF16)]
    return call(middle_kernel, outs, scratch, back, x, vec, lay["from_modes"], flops=lay["cost"], **lay["sizes"])


def apart(shape):
    return (shape[0] * shape[1] // 128, 128)


def spectral(got, one, two, vec, lay):
    shape = got.shape
    return call(spectral_kernel, [(shape, BF16)] * 5, [apart(shape), shape], got, lay["latitude"], one, two, vec, flops=4 * lay["cost"], per=lay["sizes"]["per"])


def spectral_back(got, one, two, slope, factor, lay):
    shape = got.shape
    return call(spectral_back_kernel, [(shape, BF16)] * 3, [apart(shape), shape], got, lay["latitude"], one, two, slope, factor, flops=4 * lay["cost"], per=lay["sizes"]["per"])


def spectral_grads(low, first, active, second, small, in_bias):
    width = low.shape[1]
    blocks = BLOCKS // 2
    outs = [((4 * width // 2, 128), BF16), ((G_ROWS, width), F32)]
    return call(spectral_grad_kernel, outs, [(width, width)], low, first, active, second, small, in_bias, flops=4 * low.shape[0] * width * width, blocks=blocks)


def matrices(place, own, other):
    _, blocks, size, _ = own[0].shape
    shape = (blocks * size, blocks * size)
    return call(matrices_kernel, [(shape, BF16)] * 4, [shape], place, *own, *other, scalars=1, blocks=blocks // 2)


def dense_specs(tokens, width, tile, level):
    whole = lambda shape: pl.BlockSpec(shape, lambda j, c: (0,) * len(shape))
    across = lambda count: pl.BlockSpec((count, tile), lambda j, c: (0, j))
    pick = lambda own: (lambda j, c: jnp.where((c[0] == level) == own, j, 0))
    wide = [pl.BlockSpec((width, tile), lambda j, c, own=own: (0, pick(own)(j, c))) for own in (True, False)]
    tall = [pl.BlockSpec((tile, width), lambda j, c, own=own: (pick(own)(j, c), 0)) for own in (True, False)]
    return whole, across, wide, tall


def dense(place, norm, mixed, pairs, vec, shape, level):
    tokens, width = norm.shape
    hidden = pairs[0][0].shape[1]
    tile = width
    whole, across, wide, tall = dense_specs(tokens, width, tile, level)
    return pl.pallas_call(
        functools.partial(dense_kernel, level=level),
        grid_spec=pltpu.PrefetchScalarGridSpec(
            num_scalar_prefetch=1,
            grid=(hidden // tile,),
            in_specs=[whole((tokens, width)), *wide, *tall, whole(vec.shape), whole((tokens, width))],
            out_specs=[whole(shape), across(tokens), across(tokens)],
            scratch_shapes=[pltpu.VMEM((tokens, width), F32), pltpu.VMEM((width, tile), BF16), pltpu.VMEM((tile, width), BF16)],
        ),
        out_shape=[
            jax.ShapeDtypeStruct(shape, BF16),
            jax.ShapeDtypeStruct((tokens, hidden), BF16),
            jax.ShapeDtypeStruct((tokens, hidden), BF16),
        ],
        compiler_params=pltpu.CompilerParams(vmem_limit_bytes=VMEM_BYTES),
        cost_estimate=pl.CostEstimate(flops=4 * tokens * width * hidden, bytes_accessed=30 << 20, transcendentals=tokens * hidden),
    )(place, norm, *pairs[0], *pairs[1], vec, mixed)


def dense_back(place, grad, pairs, slope, level):
    tokens, width = grad.shape
    hidden = pairs[0][0].shape[1]
    tile = width
    whole, across, wide, tall = dense_specs(tokens, width, tile, level)
    return pl.pallas_call(
        functools.partial(dense_back_kernel, level=level),
        grid_spec=pltpu.PrefetchScalarGridSpec(
            num_scalar_prefetch=1,
            grid=(hidden // tile,),
            in_specs=[whole((tokens, width)), *tall, across(tokens), *wide],
            out_specs=[across(tokens), whole((hidden // tile, tile)), whole((tokens, width))],
            scratch_shapes=[pltpu.VMEM((width, tile), BF16), pltpu.VMEM((tile, width), BF16)],
        ),
        out_shape=[
            jax.ShapeDtypeStruct((tokens, hidden), BF16),
            jax.ShapeDtypeStruct((hidden // tile, tile), F32),
            jax.ShapeDtypeStruct((tokens, width), F32),
        ],
        compiler_params=pltpu.CompilerParams(vmem_limit_bytes=VMEM_BYTES),
        cost_estimate=pl.CostEstimate(flops=4 * tokens * width * hidden, bytes_accessed=30 << 20, transcendentals=0),
    )(place, grad, *pairs[1], slope, *pairs[0])


def middle_back(grad_norm, mixed, grad, vec, lay):
    tokens, width = mixed.shape
    moved = (lay["modes"], width)
    outs = [(moved, BF16), ((tokens, width), F32), ((3, width), F32)]
    return call(middle_back_kernel, outs, [(tokens, width), moved], grad_norm, mixed, grad, vec, lay["to_modes_grad"], flops=lay["cost"], **lay["sizes"])


def front_back(back, grad_mixed, x, vec, known, lay):
    tokens, width = grad_mixed.shape
    scratch = [(lay["modes"], width), (lay["waves"], width), (tokens, width)]
    outs = [(x.shape, BF16), ((tokens, width), BF16), ((G_ROWS * width // 128, 128), BF16)]
    return call(front_back_kernel, outs, scratch, back, grad_mixed, x, vec, lay["from_modes_grad"], known, flops=lay["cost"], **lay["sizes"])


def first_shed(place, grad_in, grad_in_got, grad_out, grad_out_got):
    width, hidden = grad_in.shape
    rows = hidden // ROUTES // 4
    tall = width // rows
    wide = pl.BlockSpec((rows, width), lambda j, c: (jnp.where(c[0] == 1, j % tall, 0), jnp.where(c[0] == 1, j // tall, 0)))
    high = pl.BlockSpec((rows, width), lambda j, c: (jnp.where(c[0] == 0, j, 0), 0))

    def target(route, keep):
        def index(j, c):
            step = jnp.clip(j - 4 * route, 0, 3)
            upper = (c[2 + route] == 1) == keep
            return (jnp.where(upper, jnp.maximum(step - 2, 0), jnp.minimum(step, 1)), 0)

        return pl.BlockSpec((rows, width), index)

    outs = pl.pallas_call(
        first_shed_kernel,
        grid_spec=pltpu.PrefetchScalarGridSpec(
            num_scalar_prefetch=1,
            grid=(4 * ROUTES,),
            in_specs=[wide, wide, high, high],
            out_specs=[target(route, keep) for route in range(ROUTES) for keep in (False, True)],
        ),
        out_shape=[jax.ShapeDtypeStruct((2 * rows, width), BF16)] * (2 * ROUTES),
        compiler_params=pltpu.CompilerParams(vmem_limit_bytes=VMEM_BYTES),
        cost_estimate=pl.CostEstimate(flops=0, bytes_accessed=width * hidden, transcendentals=0),
    )(place, grad_in, grad_in_got, grad_out, grad_out_got)
    return outs[::2], outs[1::2]


def shed(bits, kept, got):
    rows, width = kept[0].shape
    outs = call(shed_kernel, [((rows // 2, width), BF16)] * (2 * len(kept)), [], bits, *kept, *got, scalars=1)
    return outs[: len(kept)], outs[len(kept) :]


def double(bits, own, got):
    _, rows, width = own[0].shape
    return call(double_kernel, [((2, 2 * rows, width), BF16)] * len(own), [], bits, *own, *got, scalars=1)


def finish(place, pieces, shape, other_side, kept=()):
    width, hidden = shape
    half = pieces[0].shape[1]
    rows = hidden // ROUTES // 4
    tall = width // rows
    per_half = half // rows
    steps = ROUTES * per_half

    def block(j, c):
        route = j // per_half
        side = sum(jnp.where(route == r, c[2 + r], 0) for r in range(ROUTES))
        side = 1 - side if other_side else side
        return (2 * route + side) * per_half + j % per_half

    def wide(p, j, c):
        at = block(jnp.where(p == 1, j, 0), c)
        return at % tall, at // tall

    piece = pl.BlockSpec((1, half, width), lambda p, j, c: (p, 0, 0))
    inputs = [piece] * ROUTES + [pl.BlockSpec(memory_space=pl.ANY)] * len(kept)
    return pl.pallas_call(
        functools.partial(finish_kernel, routes=ROUTES),
        grid_spec=pltpu.PrefetchScalarGridSpec(
            num_scalar_prefetch=1,
            grid=(2, steps),
            in_specs=inputs,
            out_specs=[
                pl.BlockSpec((rows, width), wide),
                pl.BlockSpec((rows, width), lambda p, j, c: (block(jnp.where(p == 0, j, steps - 1), c), 0)),
            ],
        ),
        out_shape=[jax.ShapeDtypeStruct((width, hidden), F32), jax.ShapeDtypeStruct((hidden, width), F32)],
        input_output_aliases={1 + ROUTES + i: i for i in range(len(kept))},
        compiler_params=pltpu.CompilerParams(vmem_limit_bytes=VMEM_BYTES),
        cost_estimate=pl.CostEstimate(flops=0, bytes_accessed=6 * width * hidden, transcendentals=0),
    )(place, *pieces, *kept)


def deliver(core, half, layer_zero, layer_one):
    first, second = (list(parts[:2]) for parts in (layer_zero, layer_one))
    for level, (parts, whole) in enumerate(((first, layer_zero), (second, layer_one))):
        parts[level] = jnp.where(half == level, whole[2], parts[level])
    return jnp.stack([jnp.where(core == 0, a, b) for a, b in zip(first, second)])[None]


def after(item, *earlier):
    return lax.optimization_barrier((item, *earlier))[0]


def together(*items):
    return lax.optimization_barrier(items)


def exchange(item):
    count = lax.axis_size("lane") * 2
    pieces = item.reshape(count, item.shape[0] // count, item.shape[1])
    return lax.all_to_all(pieces, ROWS_AXES, 0, 0, tiled=True).reshape(item.shape)


ROUTES = 3


def routes_of():
    bits = [1 << i for i in range(lax.axis_size("lane").bit_length() - 1)]
    turns = [route * len(bits) // ROUTES for route in range(ROUTES)]
    return [bits[turn:] + bits[:turn] for turn in turns]


def swap(item, bit):
    return lax.ppermute(item, "lane", [(i, i ^ bit) for i in range(lax.axis_size("lane"))])


def swap_all(items, at):
    return [swap(item, route[at]) for item, route in zip(items, routes_of())]


def stack(kept, got):
    rows, width = kept[0].shape
    return call(stack_kernel, [((ROUTES * rows, width), BF16)], [], *kept, *got)[0]


def across_halves(item):
    return lax.ppermute(item, "half", [(0, 1), (1, 0)])


def pack(place, one, one_got, two, two_got):
    rows, width = one.shape
    mine, give = call(add_kernel, [(one.shape, BF16)] * 2, [], place, one, one_got, two, two_got, scalars=1)
    got = lax.ppermute(give, "section", [(0, 1), (1, 0)])
    return mine, call(pack_kernel, [((2, rows // ROUTES, width), BF16)] * ROUTES, [], place, mine, got, scalars=1)


def small_sums(parts, earlier):
    slabs = lax.axis_size("lane") * lax.axis_size("half")
    count = sum(a.shape[0] for a in parts)
    each = -(-count // (slabs * 8)) * 8
    parts = [*parts, jnp.zeros((slabs * each - count, 128), BF16)]
    pieces = jnp.concatenate(parts, 0).reshape(slabs, each, 128)
    got = after(lax.all_to_all(pieces, SLAB, 0, 0, tiled=True), *earlier)
    spread = call(small_sum_kernel, [(got.shape, BF16)], [], got)[0]
    total = lax.all_to_all(spread, SLAB, 0, 0, tiled=True).reshape(slabs * each, 128)
    return total, lax.ppermute(total, "section", [(0, 1), (1, 0)])


def fetch(pair, core, half):
    first = lax.ppermute(pair[1], ("section", "half"), [(0, 1)])
    second = lax.ppermute(pair[0], ("section", "half"), [(3, 2)])
    own = jnp.where(half == 0, pair[0], pair[1])
    return jnp.where(core == half, own, jnp.where(core == 0, first, second))


def send_out(item, level):
    pairs = lambda micro: [(2 * side + micro, 2 * level + side) for side in range(2)]
    return [lax.ppermute(item, ("section", "half"), [p for p in pairs(micro) if p[0] != p[1]]) for micro in range(2)] + [item]


ACROSS = (((0,), (0,)), ((), ()))


def exchanged(items):
    return [(item, lax.ppermute(item, "section", [(0, 1), (1, 0)])) for item in items]


def shards(tokens, cotangent, *params):
    core = lax.axis_index("section")
    half = lax.axis_index("half")
    lane = lax.axis_index("lane")
    lanes = lax.axis_size("lane")
    _, rows, longitudes, width = tokens.shape
    total_rows = rows * lanes * 2
    fields = total_rows // LAT
    live = fields * LAT
    per = -(-(longitudes // 2 + 1) // lanes)
    forward_table, inverse_table = longitude_tables(longitudes, per * lanes)
    lay = {
        "to_modes": jnp.asarray(split_table(forward_table.T)),
        "from_modes": jnp.asarray(split_table(inverse_table)),
        "to_modes_grad": jnp.asarray(split_table(inverse_table.T)),
        "from_modes_grad": jnp.asarray(split_table(forward_table)),
        "latitude": jnp.asarray(split_table(latitude_table(total_rows, fields))),
        "modes": 2 * lanes * rows * per,
        "waves": 2 * lanes * per,
        "cost": 1 << 30,
        "sizes": {"rows": rows, "lanes": lanes, "per": per},
    }
    first_row = (core * lanes + lane) * rows
    live_rows = jnp.clip(live - first_row, 0, rows).astype(jnp.int32)
    blocks = BLOCKS // 2
    size = width // BLOCKS
    routes = routes_of()
    levels = len(routes[0])
    bits = [jnp.stack([((lane & route[at]) > 0).astype(jnp.int32) for route in routes]) for at in range(levels)]
    place = jnp.concatenate([jnp.stack([core.astype(jnp.int32), live_rows]), bits[0]])
    params = [item[0] for item in params]
    gain_one, shift_one, spectral_one, bias_one, spectral_two, bias_two, gain_two, shift_two, dense_in, in_bias, dense_out, out_bias = params
    x = fetch(tokens, core, half)
    vectors = [gain_one, shift_one, gain_two, shift_two, out_bias, in_bias, bias_one, bias_two]
    vectors = jnp.concatenate([a.reshape(-1, width) for a in vectors], 0)
    vectors, other = exchanged([vectors])[0]
    vectors = jnp.stack([jnp.where(core == 0, vectors, other), jnp.where(core == 0, other, vectors)]).astype(F32)
    mine = lax.dynamic_slice_in_dim(vectors[:, BIAS_ONE:], core * (width // 2), width // 2, 2).reshape(2, 2, width)
    vectors = jnp.concatenate([vectors[:, :BIAS_ONE], mine], 1)
    vec_one, vec_two = vectors[0], vectors[1]
    spectra = exchanged([spectral_one, spectral_two])
    one_a, two_a, one_b, two_b = matrices(place, [a for a, _ in spectra], [b for _, b in spectra])
    shape = x.shape

    got = exchange(front(x, vec_one, lay))
    dense_in, dense_out = after((dense_in, dense_out), got)
    pairs = exchanged([dense_in, dense_out])
    sent, low_one, active_one, slope_one, factor_one = spectral(got, one_a, two_a, vec_one, lay)
    got = exchange(sent)
    grad = fetch(after(cotangent, got), core, half)
    mixed_one, norm_one = middle(got, x, vec_one, lay)
    out_one, activated_one, bend_one = dense(place, norm_one, mixed_one, pairs, vec_one, shape, 0)
    grad = jnp.where(jnp.arange(rows, dtype=jnp.int32)[:, None, None] < live_rows, grad, jnp.zeros_like(grad))
    got = exchange(front(after(out_one, grad), vec_two, lay))
    grad = grad.reshape(-1, width)
    sent, low_two, active_two, slope_two, factor_two = spectral(got, one_b, two_b, vec_two, lay)
    got = exchange(sent)
    delivered_one = send_out(after(out_one, got), 0)
    mixed_two, norm_two = middle(got, out_one, vec_two, lay)
    out_two, activated_two, bend_two = dense(place, norm_two, mixed_two, pairs, vec_two, shape, 1)
    grad_hidden, in_bias_two, grad_norm = dense_back(place, after(grad, *delivered_one), pairs, bend_two, 1)
    sent, grad_mixed, small_two = middle_back(grad_norm, mixed_two, grad, vec_two, lay)
    got = exchange(sent)
    delivered_two = send_out(out_two, 1)
    norm_two, activated_two = after((norm_two, activated_two), sent)
    sums_two = (
        lax.dot_general(norm_two, grad_hidden, ACROSS, preferred_element_type=F32).astype(BF16),
        lax.dot_general(activated_two, grad, ACROSS, preferred_element_type=F32).astype(BF16),
    )
    from_two = (lax.ppermute(sums_two[0], "section", [(0, 1)]), lax.ppermute(sums_two[1], "section", [(1, 0)]))
    sent, grad_second, grad_first = spectral_back(after(got, *delivered_two, *sums_two), one_b, two_b, slope_two, factor_two, lay)
    got = exchange(sent)
    blocks_two, known = spectral_grads(low_two, grad_first, active_two, grad_second, small_two, in_bias_two)
    sums_two, from_two = after((sums_two, from_two), sent)
    sends_two, keeps_two = first_shed(place, sums_two[0], from_two[0], sums_two[1], from_two[1])
    gots_two = swap_all(sends_two, 0)
    activations = deliver(core, half, delivered_one, delivered_two)
    grad_x_two, grad, small_two = front_back(after(got, activations, *sends_two), grad_mixed, out_one, vec_two, known, lay)
    grads_two = send_out(grad_x_two, 1)
    grad_hidden, in_bias_one, grad_norm = dense_back(place, grad, pairs, bend_one, 0)
    sends_two, keeps_two = shed(bits[1], keeps_two, after(gots_two, grad_norm))
    gots_two = swap_all(sends_two, 1)
    sent, grad_mixed, small_one = middle_back(after(grad_norm, *sends_two), mixed_one, grad, vec_one, lay)
    got = exchange(sent)
    norm_one, activated_one = after((norm_one, activated_one), sent, *gots_two)
    norm_one = after(norm_one, *grads_two)
    grad_out = lax.dot_general(activated_one, grad, ACROSS, preferred_element_type=F32).astype(BF16)
    grad_in = lax.dot_general(norm_one, grad_hidden, ACROSS, preferred_element_type=F32).astype(BF16)
    for at in range(2, levels):
        sends_two, keeps_two = shed(bits[at], keeps_two, gots_two)
        gots_two = swap_all(sends_two, at)
    got = after(got, grad_in, grad_out, *sends_two)
    grad_in, grad_out = after((grad_in, grad_out), *sends_two)
    grad_out_got = lax.ppermute(grad_out, "section", [(1, 0)])
    grad_in_got = lax.ppermute(grad_in, "section", [(0, 1)])
    sent, grad_second, grad_first = spectral_back(got, one_a, two_a, slope_one, factor_one, lay)
    sent, gots_two = together(sent, gots_two)
    stacked_two = stack(keeps_two, gots_two)
    halved_two = across_halves(stacked_two)
    grad_in, grad_in_got, grad_out, grad_out_got = after((grad_in, grad_in_got, grad_out, grad_out_got), sent, stacked_two)
    sends, keeps = first_shed(place, grad_in, grad_in_got, grad_out, grad_out_got)
    gots = swap_all(sends, 0)
    got = exchange(sent)
    blocks_one, known = spectral_grads(low_one, grad_first, active_one, grad_second, small_one, in_bias_one)
    grad_x_one, _, small_one = front_back(after(got, *sends), grad_mixed, x, vec_one, known, lay)
    gots = after(gots, grad_x_one, halved_two)
    for at in range(1, levels):
        sends, keeps = shed(bits[at], keeps, gots)
        gots = swap_all(sends, at)
    stacked = stack(keeps, gots)
    mine, own = pack(place, stacked, across_halves(stacked), stacked_two, after(halved_two, stacked))
    grads_one = send_out(after(grad_x_one, mine), 0)
    for at in reversed(range(levels)):
        gots = swap_all(own, at)
        if at > 0:
            own = double(bits[at], own, after(gots, *grads_one) if at == 1 else gots)
    total, other = small_sums([blocks_one, blocks_two, small_one, small_two], [stacked])
    row = ((1, width), F32)
    outs = [((2, BLOCKS, size, size), F32)] * 2 + [((2, width), F32)] * 2 + [row] * 4 + [((4, width), F32), row]
    one, two, bias_one, bias_two, gain_one, shift_one, gain_two, shift_two, in_bias, out_bias = call(
        small_finish_kernel, outs, [(G_ROWS, width)] * 2, place, total, other, scalars=1, blocks=blocks
    )
    dense_grads = finish(place, own, dense_in.shape, False)
    input_grads = deliver(core, half, grads_one, grads_two)
    bias_one, bias_two, in_bias = bias_one.reshape(1, 2, BLOCKS, size), bias_two.reshape(1, 2, BLOCKS, size), in_bias.reshape(1, -1)
    gots = after(gots, input_grads, bias_one, bias_two, in_bias, gain_one)
    grad_in, grad_out = finish(place, gots, dense_in.shape, True, dense_grads)
    return (
        activations, input_grads, gain_one, shift_one, one[None], bias_one, two[None], bias_two,
        gain_two, shift_two, grad_in[None], in_bias, grad_out[None], out_bias,
    )


def solution(mesh):
    devices = mesh.devices
    slabs = devices.shape[1]
    wide = Mesh(devices.reshape(2, 2, slabs // 2), ALL)
    rows = P(None, ("half", "lane"))
    own = P("section")
    return jax.shard_map(
        shards,
        mesh=wide,
        in_specs=(rows, rows) + (own,) * 12,
        out_specs=(P("section", None, ("half", "lane")),) * 2 + (own,) * 12,
        check_vma=False,
    )
```

```python
import functools
import math

import jax
import jax.numpy as jnp
import numpy as np
from jax import lax
from jax.experimental import pallas as pl
from jax.experimental.pallas import tpu as pltpu
from jax.sharding import Mesh, PartitionSpec as P

BLOCKS = 8
LAT = 90
EPSILON = 1e-05
SHRINK = 0.01
SOFTNESS = 0.1
ROWS_AXES = ("section", "lane")
ALL = ("section", "half", "lane")
SLAB = ("half", "lane")
F32 = jnp.float32
BF16 = jnp.bfloat16
VMEM_BYTES = 56 * 1024 * 1024
GAIN_ONE, SHIFT_ONE, GAIN_TWO, SHIFT_TWO, OUT_BIAS, IN_BIAS, BIAS_ONE, BIAS_TWO = 0, 1, 2, 3, 4, 5, 9, 10
G_GAIN_TWO, G_SHIFT_TWO, G_OUT_BIAS, G_IN_BIAS, G_BIAS_ONE, G_BIAS_TWO, G_GAIN_ONE, G_SHIFT_ONE, G_ROWS = 0, 1, 2, 3, 7, 8, 9, 10, 16


def split_table(table):
    high = np.asarray(table, np.float32).astype(jnp.bfloat16)
    low = (np.asarray(table, np.float64) - high.astype(np.float64)).astype(jnp.bfloat16)
    return np.concatenate([high, low], 0)


def longitude_tables(longitudes, padded):
    column = np.arange(longitudes)[:, None]
    frequency = np.arange(padded)[None, :]
    angle = (column * frequency % longitudes) * (2.0 * math.pi / longitudes)
    usable = (frequency <= longitudes // 2) / math.sqrt(longitudes)
    forward = np.concatenate([np.cos(angle) * usable, -np.sin(angle) * usable], 1)
    doubled = np.where((frequency == 0) | (frequency == longitudes // 2), 1.0, 2.0)
    inverse = forward * np.concatenate([doubled, doubled], 1)
    return (forward, inverse)


def latitude_table(rows, fields):
    index = np.arange(LAT)
    angle = (index[:, None] * index[None, :] % LAT) * (2.0 * math.pi / LAT)
    parts = []
    for wave in (np.cos(angle), np.sin(angle)):
        whole = np.zeros((rows, rows))
        for field in range(fields):
            span = slice(field * LAT, (field + 1) * LAT)
            whole[span, span] = wave / math.sqrt(LAT)
        parts.append(whole)
    return np.concatenate(parts, 0)


def dot(left, right):
    return jnp.dot(left, right, preferred_element_type=F32)


def dot_transposed(left, right):
    return lax.dot_general(left, right, (((1,), (1,)), ((), ())), preferred_element_type=F32)


def both_parts(table_ref, value):
    count = table_ref.shape[0] // 2
    if count % 16:
        return dot(table_ref[:count, :], value) + dot(table_ref[count:, :], value)
    full = dot(table_ref[...], value)
    return full[:count, :] + full[count:, :]


def table_times_low(table_ref, low):
    return both_parts(table_ref, low)


def table_times(table_ref, value):
    count = table_ref.shape[0] // 2
    high = value.astype(BF16)
    rest = (value - high.astype(F32)).astype(BF16)
    return both_parts(table_ref, high) + dot(table_ref[:count, :], rest)


def gelu_pair(value):
    size = jnp.abs(value) * math.sqrt(0.5)
    inverse = 1.0 / (1.0 + 0.3275911 * size)
    wave = jnp.exp(-0.5 * value * value)
    series = inverse * (0.254829592 + inverse * (-0.284496736 + inverse * (1.421413741 + inverse * (-1.453152027 + inverse * 1.061405429))))
    tail = 0.5 * series * wave
    share = jnp.where(value > 0, 1.0 - tail, tail)
    return value * share, share + value * wave * (1.0 / math.sqrt(2.0 * math.pi))


def row_of(vec_ref, at):
    return vec_ref[at : at + 1, :]


def centered(value):
    center = value - jnp.mean(value, axis=-1, keepdims=True)
    inverse = lax.rsqrt(jnp.mean(center * center, axis=-1, keepdims=True) + EPSILON)
    return center * inverse, inverse


def norm_back(grad, gain, unit, inverse):
    scaled = grad * gain
    return (scaled - jnp.mean(scaled, axis=-1, keepdims=True) - unit * jnp.mean(scaled * unit, axis=-1, keepdims=True)) * inverse


def scatter_modes(sent, spectrum, row, rows, lanes, per):
    width = spectrum.shape[1]
    half = width // 2
    modes = lanes * per
    for part in range(2):
        for lane in range(lanes):
            base = ((part * lanes + lane) * rows + row) * per
            for wave in range(2):
                piece = spectrum[wave * modes + lane * per : wave * modes + (lane + 1) * per, part * half : (part + 1) * half]
                sent[base : base + per, wave * half : (wave + 1) * half] = piece


def gather_modes(spectrum, back, row, rows, lanes, per):
    width = spectrum.shape[1]
    half = width // 2
    modes = lanes * per
    for part in range(2):
        for lane in range(lanes):
            base = ((part * lanes + lane) * rows + row) * per
            for wave in range(2):
                piece = back[base : base + per, wave * half : (wave + 1) * half]
                spectrum[wave * modes + lane * per : wave * modes + (lane + 1) * per, part * half : (part + 1) * half] = piece


def front_kernel(x_ref, vec_ref, table_ref, sent_ref, sent32, *, rows, lanes, per):
    for row in range(rows):
        unit, _ = centered(x_ref[row].astype(F32))
        spectrum = table_times(table_ref, unit * row_of(vec_ref, GAIN_ONE) + row_of(vec_ref, SHIFT_ONE))
        scatter_modes(sent32, spectrum, row, rows, lanes, per)
    sent_ref[...] = sent32[...].astype(BF16)


def middle_kernel(back_ref, x_ref, vec_ref, table_ref, mixed_ref, norm_ref, back32, spectrum, norm32, *, rows, lanes, per):
    back32[...] = back_ref[...].astype(F32)
    longs = x_ref.shape[1]
    for row in range(rows):
        span = slice(row * longs, (row + 1) * longs)
        gather_modes(spectrum, back32, row, rows, lanes, per)
        value = x_ref[row].astype(F32)
        unit, _ = centered(value)
        mixed = table_times_low(table_ref, spectrum[...].astype(BF16)) + (unit * row_of(vec_ref, GAIN_ONE) + row_of(vec_ref, SHIFT_ONE)) + value
        mixed_ref[span, :] = mixed
        unit, _ = centered(mixed)
        norm32[span, :] = unit * row_of(vec_ref, GAIN_TWO) + row_of(vec_ref, SHIFT_TWO)
    norm_ref[...] = norm32[...].astype(BF16)


def latitude_forward(table_ref, value, count):
    half = value.shape[1] // 2
    both = table_times_low(table_ref, value)
    cosine, sine = both[:count, :], both[count:, :]
    return cosine[:, :half] + sine[:, half:], cosine[:, half:] - sine[:, :half]


def latitude_inverse(table_ref, value, count):
    half = value.shape[1] // 2
    both = table_times(table_ref, value)
    cosine, sine = both[:count, :], both[count:, :]
    return cosine[:, :half] - sine[:, half:], cosine[:, half:] + sine[:, :half]


def strided_fill(apart, got_ref):
    total, width = got_ref.shape
    for tile in range(width // 128):
        apart[tile * total : (tile + 1) * total, :] = got_ref[:, tile * 128 : (tile + 1) * 128].astype(F32)


def strided_take(apart, mode, per, total, width):
    spans = [pl.ds(tile * total + mode, total // per, stride=per) for tile in range(width // 128)]
    return jnp.concatenate([apart[span, :] for span in spans], 1).astype(BF16)


def strided_put(apart, mode, per, total, first, value):
    for tile in range(value.shape[1] // 128):
        span = pl.ds((first + tile) * total + mode, total // per, stride=per)
        apart[span, :] = value[:, tile * 128 : (tile + 1) * 128]


def strided_send(sent_ref, apart):
    total, width = sent_ref.shape
    for tile in range(width // 128):
        sent_ref[:, tile * 128 : (tile + 1) * 128] = apart[tile * total : (tile + 1) * total, :].astype(BF16)


def chunk_of(total):
    return total // 3 if total % 48 == 0 else total


def spectral_kernel(got_ref, table_ref, one_ref, two_ref, vec_ref, sent_ref, low_ref, active_ref, slope_ref, factor_ref, got32, shrunk, *, per):
    total, width = got_ref.shape
    count, half = total // per, width // 2
    strided_fill(got32, got_ref)
    for mode in range(per):
        real, imag = latitude_forward(table_ref, strided_take(got32, mode, per, total, width), count)
        span = slice(mode * count, (mode + 1) * count)
        low_ref[span, :half] = real.astype(BF16)
        low_ref[span, half:] = imag.astype(BF16)
    chunk = chunk_of(total)

    @pl.loop(0, total // chunk)
    def _(step):
        span = pl.ds(pl.multiple_of(step * chunk, chunk), chunk)
        first = dot(low_ref[span, :], one_ref[...]) + row_of(vec_ref, BIAS_ONE)
        active, slope = gelu_pair(first)
        active = active.astype(BF16)
        active_ref[span, :] = active
        slope_ref[span, :] = slope.astype(BF16)
        second = dot(active, two_ref[...]) + row_of(vec_ref, BIAS_TWO)
        bend = jnp.tanh(second * (1.0 / SOFTNESS))
        shrunk[span, :] = second - SHRINK * bend
        factor_ref[span, :] = (1.0 - SHRINK / SOFTNESS * (1.0 - bend * bend)).astype(BF16)

    for mode in range(per):
        real, imag = latitude_inverse(table_ref, shrunk[mode * count : (mode + 1) * count, :], count)
        strided_put(got32, mode, per, total, 0, real)
        strided_put(got32, mode, per, total, half // 128, imag)
    strided_send(sent_ref, got32)


def spectral_back_kernel(got_ref, table_ref, one_ref, two_ref, slope_ref, factor_ref, sent_ref, second_ref, first_ref, got32, grad, *, per):
    total, width = got_ref.shape
    count, half = total // per, width // 2
    strided_fill(got32, got_ref)
    for mode in range(per):
        real, imag = latitude_forward(table_ref, strided_take(got32, mode, per, total, width), count)
        span = slice(mode * count, (mode + 1) * count)
        second_ref[span, :half] = (real * factor_ref[span, :half].astype(F32)).astype(BF16)
        second_ref[span, half:] = (imag * factor_ref[span, half:].astype(F32)).astype(BF16)
    chunk = chunk_of(total)

    @pl.loop(0, total // chunk)
    def _(step):
        span = pl.ds(pl.multiple_of(step * chunk, chunk), chunk)
        grad_active = dot_transposed(second_ref[span, :], two_ref[...])
        first = (grad_active * slope_ref[span, :].astype(F32)).astype(BF16)
        first_ref[span, :] = first
        grad[span, :] = dot_transposed(first, one_ref[...])

    for mode in range(per):
        real, imag = latitude_inverse(table_ref, grad[mode * count : (mode + 1) * count, :], count)
        strided_put(got32, mode, per, total, 0, real)
        strided_put(got32, mode, per, total, half // 128, imag)
    strided_send(sent_ref, got32)


def choose(place_ref, level, own_ref, other_ref, chosen):
    @pl.when(place_ref[0] == level)
    def _():
        chosen[...] = own_ref[...]

    @pl.when(place_ref[0] != level)
    def _():
        chosen[...] = other_ref[...]


def dense_kernel(place_ref, norm_ref, in_ref, in_other_ref, out_ref, out_other_ref, vec_ref, mixed_ref, result_ref, active_ref, slope_ref, total, in_kept, out_kept, *, level):
    step = pl.program_id(0)
    choose(place_ref, level, in_ref, in_other_ref, in_kept)
    choose(place_ref, level, out_ref, out_other_ref, out_kept)
    tokens = norm_ref.shape[0]
    middle = -(-tokens // 32) * 16
    for span in (slice(0, middle), slice(middle, tokens)):
        hidden = dot(norm_ref[span, :], in_kept[...]) + vec_ref[pl.ds(IN_BIAS + step, 1), :]
        active, slope = gelu_pair(hidden)
        active = active.astype(BF16)
        active_ref[span, :] = active
        slope_ref[span, :] = slope.astype(BF16)
        before = jnp.where(step == 0, mixed_ref[span, :] + row_of(vec_ref, OUT_BIAS), total[span, :])
        total[span, :] = before + dot(active, out_kept[...])

    @pl.when(step == pl.num_programs(0) - 1)
    def _():
        rows, longs, _ = result_ref.shape
        for row in range(rows):
            value = total[row * longs : (row + 1) * longs, :]
            result_ref[row] = jnp.where(row < place_ref[1], value, 0.0).astype(BF16)


def dense_back_kernel(place_ref, grad_ref, out_ref, out_other_ref, slope_ref, in_ref, in_other_ref, hidden_ref, bias_ref, norm_ref, in_kept, out_kept, *, level):
    step = pl.program_id(0)
    choose(place_ref, level, in_ref, in_other_ref, in_kept)
    choose(place_ref, level, out_ref, out_other_ref, out_kept)
    tokens = grad_ref.shape[0]
    middle = -(-tokens // 32) * 16
    bias = 0.0
    for span in (slice(0, middle), slice(middle, tokens)):
        grad_active = dot_transposed(grad_ref[span, :], out_kept[...])
        hidden = (grad_active * slope_ref[span, :].astype(F32)).astype(BF16)
        hidden_ref[span, :] = hidden
        bias += jnp.sum(hidden.astype(F32), axis=0, keepdims=True)
        before = jnp.where(step == 0, 0.0, norm_ref[span, :])
        norm_ref[span, :] = before + dot_transposed(hidden, in_kept[...])
    bias_ref[pl.ds(step, 1), :] = bias


def middle_back_kernel(norm_ref, mixed_ref, grad_ref, vec_ref, table_ref, sent_ref, grad_mixed_ref, small_ref, grad32, sent32, *, rows, lanes, per):
    grad32[...] = grad_ref[...].astype(F32)
    longs = mixed_ref.shape[0] // rows
    gain_grad = shift_grad = bias_grad = 0.0
    for row in range(rows):
        span = slice(row * longs, (row + 1) * longs)
        unit, inverse = centered(mixed_ref[span, :])
        grad_norm = norm_ref[span, :]
        grad_out = grad32[span, :]
        grad_mixed = norm_back(grad_norm, row_of(vec_ref, GAIN_TWO), unit, inverse) + grad_out
        gain_grad += jnp.sum(grad_norm * unit, axis=0, keepdims=True)
        shift_grad += jnp.sum(grad_norm, axis=0, keepdims=True)
        bias_grad += jnp.sum(grad_out, axis=0, keepdims=True)
        grad_mixed_ref[span, :] = grad_mixed
        scatter_modes(sent32, table_times(table_ref, grad_mixed), row, rows, lanes, per)
    small_ref[0:1, :] = gain_grad
    small_ref[1:2, :] = shift_grad
    small_ref[2:3, :] = bias_grad
    sent_ref[...] = sent32[...].astype(BF16)


def front_back_kernel(back_ref, grad_mixed_ref, x_ref, vec_ref, table_ref, known_ref, grad_ref, flat_ref, small_ref, back32, spectrum, flat32, *, rows, lanes, per):
    back32[...] = back_ref[...].astype(F32)
    longs = x_ref.shape[1]
    gain_grad = shift_grad = 0.0
    for row in range(rows):
        span = slice(row * longs, (row + 1) * longs)
        gather_modes(spectrum, back32, row, rows, lanes, per)
        grad_mixed = grad_mixed_ref[span, :]
        grad_normed = table_times_low(table_ref, spectrum[...].astype(BF16)) + grad_mixed
        unit, inverse = centered(x_ref[row].astype(F32))
        gain_grad += jnp.sum(grad_normed * unit, axis=0, keepdims=True)
        shift_grad += jnp.sum(grad_normed, axis=0, keepdims=True)
        grad = norm_back(grad_normed, row_of(vec_ref, GAIN_ONE), unit, inverse) + grad_mixed
        flat32[span, :] = grad
        grad_ref[row] = grad.astype(BF16)
    known = known_ref[...]
    index = lax.broadcasted_iota(jnp.int32, known.shape, 0)
    known = jnp.where(index == G_GAIN_ONE, gain_grad, jnp.where(index == G_SHIFT_ONE, shift_grad, known))
    for tile in range(known.shape[1] // 128):
        small_ref[tile * G_ROWS : (tile + 1) * G_ROWS, :] = known[:, tile * 128 : (tile + 1) * 128].astype(BF16)
    flat_ref[...] = flat32[...].astype(BF16)


def spectral_grad_kernel(low_ref, first_ref, active_ref, second_ref, small_ref, in_bias_ref, blocks_ref, known_ref, outer, *, blocks):
    half = outer.shape[0] // 2
    size = half // blocks
    blocks_ref[...] = jnp.zeros_like(blocks_ref)
    for which, (left, right) in enumerate(((low_ref, first_ref), (active_ref, second_ref))):
        outer[...] = lax.dot_general(left[...], right[...], (((0,), (0,)), ((), ())), preferred_element_type=F32)
        for block in range(blocks):
            up, down = slice(block * size, (block + 1) * size), slice(half + block * size, half + (block + 1) * size)
            at = (which * 2 * blocks + block) * size
            blocks_ref[at : at + size, :size] = (outer[up, up] + outer[down, down]).astype(BF16)
            at += blocks * size
            blocks_ref[at : at + size, :size] = (outer[up, down] - outer[down, up]).astype(BF16)
    known_ref[...] = jnp.zeros_like(known_ref)
    known_ref[G_GAIN_TWO : G_OUT_BIAS + 1, :] = small_ref[...]
    known_ref[G_IN_BIAS : G_IN_BIAS + 4, :] = in_bias_ref[...]
    known_ref[G_BIAS_ONE : G_BIAS_ONE + 1, :] = jnp.sum(first_ref[...].astype(F32), axis=0, keepdims=True)
    known_ref[G_BIAS_TWO : G_BIAS_TWO + 1, :] = jnp.sum(second_ref[...].astype(F32), axis=0, keepdims=True)


def matrices_kernel(place_ref, own_one_ref, own_two_ref, other_one_ref, other_two_ref, one_a_ref, two_a_ref, one_b_ref, two_b_ref, whole, *, blocks):
    core = place_ref[0]
    size = own_one_ref.shape[-1]
    half = blocks * size

    def build(source, target):
        whole[...] = jnp.zeros_like(whole)
        for block in range(blocks):
            real = source[0, core * blocks + block].astype(F32)
            imag = source[1, core * blocks + block].astype(F32)
            up, down = slice(block * size, (block + 1) * size), slice(half + block * size, half + (block + 1) * size)
            whole[up, up] = real
            whole[up, down] = imag
            whole[down, up] = -imag
            whole[down, down] = real
        target[...] = whole[...].astype(BF16)

    for level, targets in enumerate(((one_a_ref, two_a_ref), (one_b_ref, two_b_ref))):

        @pl.when(core == level)
        def _(targets=targets):
            build(own_one_ref, targets[0])
            build(own_two_ref, targets[1])

        @pl.when(core != level)
        def _(targets=targets):
            build(other_one_ref, targets[0])
            build(other_two_ref, targets[1])


def first_shed_kernel(place_ref, in_ref, in_got_ref, out_ref, out_got_ref, *targets):
    step = pl.program_id(0)
    for core, (mine, got) in enumerate(((out_ref, out_got_ref), (in_ref, in_got_ref))):

        @pl.when(place_ref[0] == core)
        def _(mine=mine, got=got):
            total = (mine[...].astype(F32) + got[...].astype(F32)).astype(BF16)
            for route in range(len(targets) // 2):
                keeps = (step // 2) % 2 == place_ref[2 + route]

                @pl.when((step // 4 == route) & keeps)
                def _(route=route, total=total):
                    targets[2 * route + 1][...] = total

                @pl.when((step // 4 == route) & jnp.logical_not(keeps))
                def _(route=route, total=total):
                    targets[2 * route][...] = total


def shed_kernel(bits_ref, *refs):
    count = len(refs) // 4
    kept, got, sends, keeps = (refs[i * count : (i + 1) * count] for i in range(4))
    for at in range(count):
        half = sends[at].shape[0]
        for target, bit in ((keeps[at], bits_ref[at]), (sends[at], 1 - bits_ref[at])):
            span = pl.ds(pl.multiple_of(bit * half, half), half)
            target[...] = (kept[at][span, :].astype(F32) + got[at][span, :].astype(F32)).astype(BF16)


def stack_kernel(*refs):
    *sources, target = refs
    count = len(sources) // 2
    rows = sources[0].shape[0]
    for at in range(count):
        target[at * rows : (at + 1) * rows, :] = (sources[at][...].astype(F32) + sources[count + at][...].astype(F32)).astype(BF16)


def add_kernel(place_ref, one_ref, one_got_ref, two_ref, two_got_ref, mine_ref, give_ref):
    for core, (first, second) in enumerate(((mine_ref, give_ref), (give_ref, mine_ref))):

        @pl.when(place_ref[0] == core)
        def _(first=first, second=second):
            first[...] = (one_ref[...].astype(F32) + one_got_ref[...].astype(F32)).astype(BF16)
            second[...] = (two_ref[...].astype(F32) + two_got_ref[...].astype(F32)).astype(BF16)


def pack_kernel(place_ref, mine_ref, got_ref, *targets):
    for core, (first, second) in enumerate(((mine_ref, got_ref), (got_ref, mine_ref))):

        @pl.when(place_ref[0] == core)
        def _(first=first, second=second):
            for at, target in enumerate(targets):
                rows = target.shape[1]
                target[0] = first[at * rows : (at + 1) * rows, :]
                target[1] = second[at * rows : (at + 1) * rows, :]


def double_kernel(bits_ref, *refs):
    count = len(refs) // 3
    own, got, targets = (refs[i * count : (i + 1) * count] for i in range(3))
    for at in range(count):
        rows = own[at].shape[1]
        for source, bit in ((own[at], bits_ref[at]), (got[at], 1 - bits_ref[at])):
            targets[at][:, pl.ds(pl.multiple_of(bit * rows, rows), rows), :] = source[...]


def finish_kernel(place_ref, *refs, routes):
    sources, (in_grad_ref, out_grad_ref) = refs[:routes], refs[-2:]
    part, step = pl.program_id(0), pl.program_id(1)
    rows = out_grad_ref.shape[0]
    per_half = sources[0].shape[1] // rows
    span = pl.ds(pl.multiple_of((step % per_half) * rows, rows), rows)
    for route in range(routes):
        for which, target in enumerate((out_grad_ref, in_grad_ref)):

            @pl.when((step // per_half == route) & (part == which))
            def _(target=target, source=sources[route]):
                target[...] = source[0, span, :].astype(F32)


def small_sum_kernel(got_ref, spread_ref):
    total = jnp.sum(got_ref[...].astype(F32), axis=0).astype(BF16)
    for at in range(spread_ref.shape[0]):
        spread_ref[at] = total


def small_finish_kernel(place_ref, own_ref, other_ref, one_ref, two_ref, bias_one_ref, bias_two_ref, gain_one_ref, shift_one_ref, gain_two_ref, shift_two_ref, in_bias_ref, out_bias_ref, vec, vec_other, *, blocks):
    core = place_ref[0]
    size = one_ref.shape[-1]
    matrix_rows = 4 * blocks * size
    tiles = vec.shape[1] // 128
    for which, target in enumerate((one_ref, two_ref)):
        for wave in range(2):
            for block in range(blocks):
                at = core * matrix_rows + ((which * 2 + wave) * blocks + block) * size
                span = pl.ds(pl.multiple_of(at, 32), size)
                target[wave, core * blocks + block] = own_ref[span, :].astype(F32)[:, :size]
                target[wave, (1 - core) * blocks + block] = other_ref[span, :].astype(F32)[:, :size]
    for source, target in ((own_ref, vec), (other_ref, vec_other)):
        for tile in range(tiles):
            at = 2 * matrix_rows + (core * tiles + tile) * G_ROWS
            target[:, tile * 128 : (tile + 1) * 128] = source[pl.ds(pl.multiple_of(at, G_ROWS), G_ROWS), :].astype(F32)
    half = vec.shape[1] // 2
    for row, target in ((G_BIAS_ONE, bias_one_ref), (G_BIAS_TWO, bias_two_ref)):
        for wave in range(2):
            for source, place in ((vec, core), (vec_other, 1 - core)):
                target[wave : wave + 1, pl.ds(pl.multiple_of(place * half, 128), half)] = source[row : row + 1, wave * half : (wave + 1) * half]
    total = vec[...] + vec_other[...]
    for row, target in ((G_GAIN_ONE, gain_one_ref), (G_SHIFT_ONE, shift_one_ref), (G_GAIN_TWO, gain_two_ref), (G_SHIFT_TWO, shift_two_ref), (G_OUT_BIAS, out_bias_ref)):
        target[...] = total[row : row + 1, :]
    in_bias_ref[...] = total[G_IN_BIAS : G_IN_BIAS + 4, :]


def call(body, outs, scratch, *args, flops=0, scalars=0, **named):
    bytes_moved = sum(a.size * a.dtype.itemsize for a in args) + sum(math.prod(s) * np.dtype(d).itemsize for s, d in outs)
    return pl.pallas_call(
        functools.partial(body, **named),
        out_shape=[jax.ShapeDtypeStruct(s, d) for s, d in outs],
        in_specs=[pl.BlockSpec(memory_space=pltpu.SMEM if i < scalars else pltpu.VMEM) for i in range(len(args))],
        out_specs=[pl.BlockSpec(memory_space=pltpu.VMEM)] * len(outs),
        scratch_shapes=[pltpu.VMEM(s, F32) for s in scratch],
        compiler_params=pltpu.CompilerParams(vmem_limit_bytes=VMEM_BYTES),
        cost_estimate=pl.CostEstimate(flops=flops, bytes_accessed=bytes_moved if flops else bytes_moved // 8, transcendentals=0),
    )(*args)


def front(x, vec, lay):
    moved = (lay["modes"], x.shape[2])
    return call(front_kernel, [(moved, BF16)], [moved], x, vec, lay["to_modes"], flops=lay["cost"], **lay["sizes"])[0]


def middle(back, x, vec, lay):
    tokens, width = x.shape[0] * x.shape[1], x.shape[2]
    scratch = [(lay["modes"], width), (lay["waves"], width), (tokens, width)]
    outs = [((tokens, width), F32), ((tokens, width), BF16)]
    return call(middle_kernel, outs, scratch, back, x, vec, lay["from_modes"], flops=lay["cost"], **lay["sizes"])


def apart(shape):
    return (shape[0] * shape[1] // 128, 128)


def spectral(got, one, two, vec, lay):
    shape = got.shape
    return call(spectral_kernel, [(shape, BF16)] * 5, [apart(shape), shape], got, lay["latitude"], one, two, vec, flops=4 * lay["cost"], per=lay["sizes"]["per"])


def spectral_back(got, one, two, slope, factor, lay):
    shape = got.shape
    return call(spectral_back_kernel, [(shape, BF16)] * 3, [apart(shape), shape], got, lay["latitude"], one, two, slope, factor, flops=4 * lay["cost"], per=lay["sizes"]["per"])


def spectral_grads(low, first, active, second, small, in_bias):
    width = low.shape[1]
    blocks = BLOCKS // 2
    outs = [((4 * width // 2, 128), BF16), ((G_ROWS, width), F32)]
    return call(spectral_grad_kernel, outs, [(width, width)], low, first, active, second, small, in_bias, flops=4 * low.shape[0] * width * width, blocks=blocks)


def matrices(place, own, other):
    _, blocks, size, _ = own[0].shape
    shape = (blocks * size, blocks * size)
    return call(matrices_kernel, [(shape, BF16)] * 4, [shape], place, *own, *other, scalars=1, blocks=blocks // 2)


def dense_specs(tokens, width, tile, level):
    whole = lambda shape: pl.BlockSpec(shape, lambda j, c: (0,) * len(shape))
    across = lambda count: pl.BlockSpec((count, tile), lambda j, c: (0, j))
    pick = lambda own: (lambda j, c: jnp.where((c[0] == level) == own, j, 0))
    wide = [pl.BlockSpec((width, tile), lambda j, c, own=own: (0, pick(own)(j, c))) for own in (True, False)]
    tall = [pl.BlockSpec((tile, width), lambda j, c, own=own: (pick(own)(j, c), 0)) for own in (True, False)]
    return whole, across, wide, tall


def dense(place, norm, mixed, pairs, vec, shape, level):
    tokens, width = norm.shape
    hidden = pairs[0][0].shape[1]
    tile = width
    whole, across, wide, tall = dense_specs(tokens, width, tile, level)
    return pl.pallas_call(
        functools.partial(dense_kernel, level=level),
        grid_spec=pltpu.PrefetchScalarGridSpec(
            num_scalar_prefetch=1,
            grid=(hidden // tile,),
            in_specs=[whole((tokens, width)), *wide, *tall, whole(vec.shape), whole((tokens, width))],
            out_specs=[whole(shape), across(tokens), across(tokens)],
            scratch_shapes=[pltpu.VMEM((tokens, width), F32), pltpu.VMEM((width, tile), BF16), pltpu.VMEM((tile, width), BF16)],
        ),
        out_shape=[
            jax.ShapeDtypeStruct(shape, BF16),
            jax.ShapeDtypeStruct((tokens, hidden), BF16),
            jax.ShapeDtypeStruct((tokens, hidden), BF16),
        ],
        compiler_params=pltpu.CompilerParams(vmem_limit_bytes=VMEM_BYTES),
        cost_estimate=pl.CostEstimate(flops=4 * tokens * width * hidden, bytes_accessed=30 << 20, transcendentals=tokens * hidden),
    )(place, norm, *pairs[0], *pairs[1], vec, mixed)


def dense_back(place, grad, pairs, slope, level):
    tokens, width = grad.shape
    hidden = pairs[0][0].shape[1]
    tile = width
    whole, across, wide, tall = dense_specs(tokens, width, tile, level)
    return pl.pallas_call(
        functools.partial(dense_back_kernel, level=level),
        grid_spec=pltpu.PrefetchScalarGridSpec(
            num_scalar_prefetch=1,
            grid=(hidden // tile,),
            in_specs=[whole((tokens, width)), *tall, across(tokens), *wide],
            out_specs=[across(tokens), whole((hidden // tile, tile)), whole((tokens, width))],
            scratch_shapes=[pltpu.VMEM((width, tile), BF16), pltpu.VMEM((tile, width), BF16)],
        ),
        out_shape=[
            jax.ShapeDtypeStruct((tokens, hidden), BF16),
            jax.ShapeDtypeStruct((hidden // tile, tile), F32),
            jax.ShapeDtypeStruct((tokens, width), F32),
        ],
        compiler_params=pltpu.CompilerParams(vmem_limit_bytes=VMEM_BYTES),
        cost_estimate=pl.CostEstimate(flops=4 * tokens * width * hidden, bytes_accessed=30 << 20, transcendentals=0),
    )(place, grad, *pairs[1], slope, *pairs[0])


def middle_back(grad_norm, mixed, grad, vec, lay):
    tokens, width = mixed.shape
    moved = (lay["modes"], width)
    outs = [(moved, BF16), ((tokens, width), F32), ((3, width), F32)]
    return call(middle_back_kernel, outs, [(tokens, width), moved], grad_norm, mixed, grad, vec, lay["to_modes_grad"], flops=lay["cost"], **lay["sizes"])


def front_back(back, grad_mixed, x, vec, known, lay):
    tokens, width = grad_mixed.shape
    scratch = [(lay["modes"], width), (lay["waves"], width), (tokens, width)]
    outs = [(x.shape, BF16), ((tokens, width), BF16), ((G_ROWS * width // 128, 128), BF16)]
    return call(front_back_kernel, outs, scratch, back, grad_mixed, x, vec, lay["from_modes_grad"], known, flops=lay["cost"], **lay["sizes"])


def first_shed(place, grad_in, grad_in_got, grad_out, grad_out_got):
    width, hidden = grad_in.shape
    rows = hidden // ROUTES // 4
    tall = width // rows
    wide = pl.BlockSpec((rows, width), lambda j, c: (jnp.where(c[0] == 1, j % tall, 0), jnp.where(c[0] == 1, j // tall, 0)))
    high = pl.BlockSpec((rows, width), lambda j, c: (jnp.where(c[0] == 0, j, 0), 0))

    def target(route, keep):
        def index(j, c):
            step = jnp.clip(j - 4 * route, 0, 3)
            upper = (c[2 + route] == 1) == keep
            return (jnp.where(upper, jnp.maximum(step - 2, 0), jnp.minimum(step, 1)), 0)

        return pl.BlockSpec((rows, width), index)

    outs = pl.pallas_call(
        first_shed_kernel,
        grid_spec=pltpu.PrefetchScalarGridSpec(
            num_scalar_prefetch=1,
            grid=(4 * ROUTES,),
            in_specs=[wide, wide, high, high],
            out_specs=[target(route, keep) for route in range(ROUTES) for keep in (False, True)],
        ),
        out_shape=[jax.ShapeDtypeStruct((2 * rows, width), BF16)] * (2 * ROUTES),
        compiler_params=pltpu.CompilerParams(vmem_limit_bytes=VMEM_BYTES),
        cost_estimate=pl.CostEstimate(flops=0, bytes_accessed=width * hidden, transcendentals=0),
    )(place, grad_in, grad_in_got, grad_out, grad_out_got)
    return outs[::2], outs[1::2]


def shed(bits, kept, got):
    rows, width = kept[0].shape
    outs = call(shed_kernel, [((rows // 2, width), BF16)] * (2 * len(kept)), [], bits, *kept, *got, scalars=1)
    return outs[: len(kept)], outs[len(kept) :]


def double(bits, own, got):
    _, rows, width = own[0].shape
    return call(double_kernel, [((2, 2 * rows, width), BF16)] * len(own), [], bits, *own, *got, scalars=1)


def finish(place, pieces, shape, other_side, kept=()):
    width, hidden = shape
    half = pieces[0].shape[1]
    rows = hidden // ROUTES // 4
    tall = width // rows
    per_half = half // rows
    steps = ROUTES * per_half

    def block(j, c):
        route = j // per_half
        side = sum(jnp.where(route == r, c[2 + r], 0) for r in range(ROUTES))
        side = 1 - side if other_side else side
        return (2 * route + side) * per_half + j % per_half

    def wide(p, j, c):
        at = block(jnp.where(p == 1, j, 0), c)
        return at % tall, at // tall

    piece = pl.BlockSpec((1, half, width), lambda p, j, c: (p, 0, 0))
    inputs = [piece] * ROUTES + [pl.BlockSpec(memory_space=pl.ANY)] * len(kept)
    return pl.pallas_call(
        functools.partial(finish_kernel, routes=ROUTES),
        grid_spec=pltpu.PrefetchScalarGridSpec(
            num_scalar_prefetch=1,
            grid=(2, steps),
            in_specs=inputs,
            out_specs=[
                pl.BlockSpec((rows, width), wide),
                pl.BlockSpec((rows, width), lambda p, j, c: (block(jnp.where(p == 0, j, steps - 1), c), 0)),
            ],
        ),
        out_shape=[jax.ShapeDtypeStruct((width, hidden), F32), jax.ShapeDtypeStruct((hidden, width), F32)],
        input_output_aliases={1 + ROUTES + i: i for i in range(len(kept))},
        compiler_params=pltpu.CompilerParams(vmem_limit_bytes=VMEM_BYTES),
        cost_estimate=pl.CostEstimate(flops=0, bytes_accessed=6 * width * hidden, transcendentals=0),
    )(place, *pieces, *kept)


def deliver(core, half, layer_zero, layer_one):
    first, second = (list(parts[:2]) for parts in (layer_zero, layer_one))
    for level, (parts, whole) in enumerate(((first, layer_zero), (second, layer_one))):
        parts[level] = jnp.where(half == level, whole[2], parts[level])
    return jnp.stack([jnp.where(core == 0, a, b) for a, b in zip(first, second)])[None]


def after(item, *earlier):
    return lax.optimization_barrier((item, *earlier))[0]


def together(*items):
    return lax.optimization_barrier(items)


def exchange(item):
    count = lax.axis_size("lane") * 2
    pieces = item.reshape(count, item.shape[0] // count, item.shape[1])
    return lax.all_to_all(pieces, ROWS_AXES, 0, 0, tiled=True).reshape(item.shape)


ROUTES = 3


def routes_of():
    bits = [1 << i for i in range(lax.axis_size("lane").bit_length() - 1)]
    turns = [route * len(bits) // ROUTES for route in range(ROUTES)]
    return [bits[turn:] + bits[:turn] for turn in turns]


def swap(item, bit):
    return lax.ppermute(item, "lane", [(i, i ^ bit) for i in range(lax.axis_size("lane"))])


def swap_all(items, at):
    return [swap(item, route[at]) for item, route in zip(items, routes_of())]


def stack(kept, got):
    rows, width = kept[0].shape
    return call(stack_kernel, [((ROUTES * rows, width), BF16)], [], *kept, *got)[0]


def across_halves(item):
    return lax.ppermute(item, "half", [(0, 1), (1, 0)])


def pack(place, one, one_got, two, two_got):
    rows, width = one.shape
    mine, give = call(add_kernel, [(one.shape, BF16)] * 2, [], place, one, one_got, two, two_got, scalars=1)
    got = lax.ppermute(give, "section", [(0, 1), (1, 0)])
    return mine, call(pack_kernel, [((2, rows // ROUTES, width), BF16)] * ROUTES, [], place, mine, got, scalars=1)


def small_sums(parts, earlier):
    slabs = lax.axis_size("lane") * lax.axis_size("half")
    count = sum(a.shape[0] for a in parts)
    each = -(-count // (slabs * 8)) * 8
    parts = [*parts, jnp.zeros((slabs * each - count, 128), BF16)]
    pieces = jnp.concatenate(parts, 0).reshape(slabs, each, 128)
    got = after(lax.all_to_all(pieces, SLAB, 0, 0, tiled=True), *earlier)
    spread = call(small_sum_kernel, [(got.shape, BF16)], [], got)[0]
    total = lax.all_to_all(spread, SLAB, 0, 0, tiled=True).reshape(slabs * each, 128)
    return total, lax.ppermute(total, "section", [(0, 1), (1, 0)])


def fetch(pair, core, half):
    first = lax.ppermute(pair[1], ("section", "half"), [(0, 1)])
    second = lax.ppermute(pair[0], ("section", "half"), [(3, 2)])
    own = jnp.where(half == 0, pair[0], pair[1])
    return jnp.where(core == half, own, jnp.where(core == 0, first, second))


def send_out(item, level):
    pairs = lambda micro: [(2 * side + micro, 2 * level + side) for side in range(2)]
    return [lax.ppermute(item, ("section", "half"), [p for p in pairs(micro) if p[0] != p[1]]) for micro in range(2)] + [item]


ACROSS = (((0,), (0,)), ((), ()))


def exchanged(items):
    return [(item, lax.ppermute(item, "section", [(0, 1), (1, 0)])) for item in items]


def shards(tokens, cotangent, *params):
    core = lax.axis_index("section")
    half = lax.axis_index("half")
    lane = lax.axis_index("lane")
    lanes = lax.axis_size("lane")
    _, rows, longitudes, width = tokens.shape
    total_rows = rows * lanes * 2
    fields = total_rows // LAT
    live = fields * LAT
    per = -(-(longitudes // 2 + 1) // lanes)
    forward_table, inverse_table = longitude_tables(longitudes, per * lanes)
    lay = {
        "to_modes": jnp.asarray(split_table(forward_table.T)),
        "from_modes": jnp.asarray(split_table(inverse_table)),
        "to_modes_grad": jnp.asarray(split_table(inverse_table.T)),
        "from_modes_grad": jnp.asarray(split_table(forward_table)),
        "latitude": jnp.asarray(split_table(latitude_table(total_rows, fields))),
        "modes": 2 * lanes * rows * per,
        "waves": 2 * lanes * per,
        "cost": 1 << 30,
        "sizes": {"rows": rows, "lanes": lanes, "per": per},
    }
    first_row = (core * lanes + lane) * rows
    live_rows = jnp.clip(live - first_row, 0, rows).astype(jnp.int32)
    blocks = BLOCKS // 2
    size = width // BLOCKS
    routes = routes_of()
    levels = len(routes[0])
    bits = [jnp.stack([((lane & route[at]) > 0).astype(jnp.int32) for route in routes]) for at in range(levels)]
    place = jnp.concatenate([jnp.stack([core.astype(jnp.int32), live_rows]), bits[0]])
    params = [item[0] for item in params]
    gain_one, shift_one, spectral_one, bias_one, spectral_two, bias_two, gain_two, shift_two, dense_in, in_bias, dense_out, out_bias = params
    x = fetch(tokens, core, half)
    vectors = [gain_one, shift_one, gain_two, shift_two, out_bias, in_bias, bias_one, bias_two]
    vectors = jnp.concatenate([a.reshape(-1, width) for a in vectors], 0)
    vectors, other = exchanged([vectors])[0]
    vectors = jnp.stack([jnp.where(core == 0, vectors, other), jnp.where(core == 0, other, vectors)]).astype(F32)
    mine = lax.dynamic_slice_in_dim(vectors[:, BIAS_ONE:], core * (width // 2), width // 2, 2).reshape(2, 2, width)
    vectors = jnp.concatenate([vectors[:, :BIAS_ONE], mine], 1)
    vec_one, vec_two = vectors[0], vectors[1]
    spectra = exchanged([spectral_one, spectral_two])
    one_a, two_a, one_b, two_b = matrices(place, [a for a, _ in spectra], [b for _, b in spectra])
    shape = x.shape

    got = exchange(front(x, vec_one, lay))
    dense_in, dense_out = after((dense_in, dense_out), got)
    pairs = exchanged([dense_in, dense_out])
    sent, low_one, active_one, slope_one, factor_one = spectral(got, one_a, two_a, vec_one, lay)
    got = exchange(sent)
    grad = fetch(after(cotangent, got), core, half)
    mixed_one, norm_one = middle(got, x, vec_one, lay)
    out_one, activated_one, bend_one = dense(place, norm_one, mixed_one, pairs, vec_one, shape, 0)
    grad = jnp.where(jnp.arange(rows, dtype=jnp.int32)[:, None, None] < live_rows, grad, jnp.zeros_like(grad))
    got = exchange(front(after(out_one, grad), vec_two, lay))
    grad = grad.reshape(-1, width)
    sent, low_two, active_two, slope_two, factor_two = spectral(got, one_b, two_b, vec_two, lay)
    got = exchange(sent)
    delivered_one = send_out(after(out_one, got), 0)
    mixed_two, norm_two = middle(got, out_one, vec_two, lay)
    out_two, activated_two, bend_two = dense(place, norm_two, mixed_two, pairs, vec_two, shape, 1)
    grad_hidden, in_bias_two, grad_norm = dense_back(place, after(grad, *delivered_one), pairs, bend_two, 1)
    sent, grad_mixed, small_two = middle_back(grad_norm, mixed_two, grad, vec_two, lay)
    got = exchange(sent)
    delivered_two = send_out(out_two, 1)
    norm_two, activated_two = after((norm_two, activated_two), sent)
    sums_two = (
        lax.dot_general(norm_two, grad_hidden, ACROSS, preferred_element_type=F32).astype(BF16),
        lax.dot_general(activated_two, grad, ACROSS, preferred_element_type=F32).astype(BF16),
    )
    from_two = (lax.ppermute(sums_two[0], "section", [(0, 1)]), lax.ppermute(sums_two[1], "section", [(1, 0)]))
    sent, grad_second, grad_first = spectral_back(after(got, *delivered_two, *sums_two), one_b, two_b, slope_two, factor_two, lay)
    got = exchange(sent)
    blocks_two, known = spectral_grads(low_two, grad_first, active_two, grad_second, small_two, in_bias_two)
    sums_two, from_two = after((sums_two, from_two), sent)
    sends_two, keeps_two = first_shed(place, sums_two[0], from_two[0], sums_two[1], from_two[1])
    gots_two = swap_all(sends_two, 0)
    activations = deliver(core, half, delivered_one, delivered_two)
    grad_x_two, grad, small_two = front_back(after(got, activations, *sends_two), grad_mixed, out_one, vec_two, known, lay)
    grads_two = send_out(grad_x_two, 1)
    grad_hidden, in_bias_one, grad_norm = dense_back(place, grad, pairs, bend_one, 0)
    sends_two, keeps_two = shed(bits[1], keeps_two, after(gots_two, grad_norm))
    gots_two = swap_all(sends_two, 1)
    sent, grad_mixed, small_one = middle_back(after(grad_norm, *sends_two), mixed_one, grad, vec_one, lay)
    got = exchange(sent)
    norm_one, activated_one = after((norm_one, activated_one), sent, *gots_two)
    norm_one = after(norm_one, *grads_two)
    grad_out = lax.dot_general(activated_one, grad, ACROSS, preferred_element_type=F32).astype(BF16)
    grad_in = lax.dot_general(norm_one, grad_hidden, ACROSS, preferred_element_type=F32).astype(BF16)
    for at in range(2, levels):
        sends_two, keeps_two = shed(bits[at], keeps_two, gots_two)
        gots_two = swap_all(sends_two, at)
    got = after(got, grad_in, grad_out, *sends_two)
    grad_in, grad_out = after((grad_in, grad_out), *sends_two)
    grad_out_got = lax.ppermute(grad_out, "section", [(1, 0)])
    grad_in_got = lax.ppermute(grad_in, "section", [(0, 1)])
    sent, grad_second, grad_first = spectral_back(got, one_a, two_a, slope_one, factor_one, lay)
    sent, gots_two = together(sent, gots_two)
    stacked_two = stack(keeps_two, gots_two)
    halved_two = across_halves(stacked_two)
    grad_in, grad_in_got, grad_out, grad_out_got = after((grad_in, grad_in_got, grad_out, grad_out_got), sent, stacked_two)
    sends, keeps = first_shed(place, grad_in, grad_in_got, grad_out, grad_out_got)
    gots = swap_all(sends, 0)
    got = exchange(sent)
    blocks_one, known = spectral_grads(low_one, grad_first, active_one, grad_second, small_one, in_bias_one)
    grad_x_one, _, small_one = front_back(after(got, *sends), grad_mixed, x, vec_one, known, lay)
    gots = after(gots, grad_x_one, halved_two)
    for at in range(1, levels):
        sends, keeps = shed(bits[at], keeps, gots)
        gots = swap_all(sends, at)
    stacked = stack(keeps, gots)
    mine, own = pack(place, stacked, across_halves(stacked), stacked_two, after(halved_two, stacked))
    grads_one = send_out(after(grad_x_one, mine), 0)
    for at in reversed(range(levels)):
        gots = swap_all(own, at)
        if at > 0:
            own = double(bits[at], own, after(gots, *grads_one) if at == 1 else gots)
    total, other = small_sums([blocks_one, blocks_two, small_one, small_two], [stacked])
    row = ((1, width), F32)
    outs = [((2, BLOCKS, size, size), F32)] * 2 + [((2, width), F32)] * 2 + [row] * 4 + [((4, width), F32), row]
    one, two, bias_one, bias_two, gain_one, shift_one, gain_two, shift_two, in_bias, out_bias = call(
        small_finish_kernel, outs, [(G_ROWS, width)] * 2, place, total, other, scalars=1, blocks=blocks
    )
    dense_grads = finish(place, own, dense_in.shape, False)
    input_grads = deliver(core, half, grads_one, grads_two)
    bias_one, bias_two, in_bias = bias_one.reshape(1, 2, BLOCKS, size), bias_two.reshape(1, 2, BLOCKS, size), in_bias.reshape(1, -1)
    gots = after(gots, input_grads, bias_one, bias_two, in_bias, gain_one)
    grad_in, grad_out = finish(place, gots, dense_in.shape, True, dense_grads)
    return (
        activations, input_grads, gain_one, shift_one, one[None], bias_one, two[None], bias_two,
        gain_two, shift_two, grad_in[None], in_bias, grad_out[None], out_bias,
    )


def solution(mesh):
    devices = mesh.devices
    slabs = devices.shape[1]
    wide = Mesh(devices.reshape(2, 2, slabs // 2), ALL)
    rows = P(None, ("half", "lane"))
    own = P("section")
    return jax.shard_map(
        shards,
        mesh=wide,
        in_specs=(rows, rows) + (own,) * 12,
        out_specs=(P("section", None, ("half", "lane")),) * 2 + (own,) * 12,
        check_vma=False,
    )
```
